32 devices in a mesh: groups: 2 (over x), dp: 8 (over z, y), tensor: 2 (over core).
Axes of the slice: x: 2, y: 2, z: 4, core: 2. Of those that a mesh axis runs over, the one named last changes fastest.
Arguments:
- layer_input: bfloat16 [16384, 4096], P(('groups', 'dp'), 'tensor'), parts along dimension 0, may hold values from -6 to 6
- out_grad: bfloat16 [16384, 4096], P(('groups', 'dp')), parts along dimension 0, may hold values from -6 to 6
- proj_in: bfloat16 [4096, 64], P('tensor'), may hold values from -0.09375 to 0.09375
- proj_out: bfloat16 [4096, 64], replicated, may hold values from -0.09375 to 0.09375
- query_features: float32 [64, 4096], P(('groups', 'dp')), parts along dimension 0, may hold values from -6 to 6
Outputs:
- scores: float32 [128, 32], P(('groups', 'dp', 'tensor')), parts along dimension 0
The draws below stay inside these ranges and needn't reach their ends.
There are 2 independent parts, one for each index of `groups`. The reference program is written for one: setup_inputs(seed, part) draws one part's arguments, and reference() takes and returns one part's arrays. A program takes and returns all parts, laid end to end along the dimension named above; an argument that names none is the same for every part. Nothing has to cross between parts.
All inputs are finite; a program needn't handle non-finite values.
Results may differ from the reference program's by a relative error of at most 0.0003.
Values sent between devices are 32-bit elements; how exact they have to be, the bound alone decides.
No kernel may reach another device: no remote copies, remote signals or barrier semaphores. Data moves between devices by JAX's collectives and lax.ppermute only.
A program may use at most 64 MiB of HBM per device.

```python
import math
import jax
import jax.numpy as jnp
from jax import lax

D = 4096
R = 64
LEN = 128
TOKENS = 8192
QUERIES = 32


def steps_of(key, dims, shards, least, largest):
    factor_of = 1.0
    for dim, parts in shards:
        heights = jax.random.uniform(jax.random.fold_in(jax.random.fold_in(key, 6), dim), (parts,), jnp.float32, least / len(shards), largest / len(shards))
        factor_of = factor_of * jnp.repeat(jnp.exp(heights), dims[dim] // parts).reshape((-1,) + (1,) * (len(dims) - 1 - dim))
    return factor_of


def scatter_about(rng, dims, deviation, bound, pieces=(), kind=jnp.bfloat16):
    factor_of = steps_of(rng, dims, pieces, -0.22, 0.18) if pieces else 1.0
    values = jax.random.normal(rng, dims, jnp.float32) * deviation * factor_of
    return jnp.minimum(jnp.maximum(values, -bound), bound).astype(kind)


def setup_inputs(seed: int = 0, part: int = 0) -> dict:
    arg_keys = jax.random.split(jax.random.key(seed), 6)
    part_splits = jax.random.split(jax.random.fold_in(arg_keys[5], part), 6)
    layer_input = scatter_about(part_splits[0], (TOKENS, D), 1.0, 6.0, ((0, 8), (1, 2)))
    out_grad = scatter_about(part_splits[1], (TOKENS, D), 1.0, 6.0, ((0, 8),))
    proj_in = scatter_about(arg_keys[2], (D, R), D ** -0.5, 0.09375, ((0, 2),))
    proj_out = scatter_about(arg_keys[3], (D, R), D ** -0.5, 0.09375)
    query_features = scatter_about(part_splits[4], (QUERIES, R * R), 1.0, 6.0, ((0, 8),), jnp.float32)
    return dict(layer_input=layer_input, out_grad=out_grad, proj_in=proj_in, proj_out=proj_out, query_features=query_features)


def reference(layer_input, out_grad, proj_in, proj_out, query_features):
    left = jnp.dot(layer_input, proj_in, preferred_element_type=jnp.float32)
    right = jnp.dot(out_grad, proj_out, preferred_element_type=jnp.float32)
    count = left.shape[0] // LEN
    features = jnp.einsum('elr,els->ers', left.reshape(count, LEN, R), right.reshape(count, LEN, R), precision=lax.Precision.HIGHEST)
    features = features.reshape(count, R * R)
    scores = jnp.dot(features, query_features.T, precision=lax.Precision.HIGHEST, preferred_element_type=jnp.float32)
    return scores / (R * math.sqrt(LEN))
```

```python
import math

import jax
import jax.numpy as jnp
from jax import lax
from jax.sharding import PartitionSpec as P

R = 64
LEN = 128


def passed_along(block, axis, distance):
    devices = range(lax.axis_size(axis))
    route = [((i - distance) % len(devices), i) for i in devices]
    return lax.ppermute(block, axis, route)


def example_features(left, right):
    count = left.shape[0] // LEN
    features = jnp.einsum(
        "elr,els->ers",
        left.reshape(count, LEN, R),
        right.reshape(count, LEN, R),
        precision=lax.Precision.HIGHEST,
    )
    return features.reshape(count, R * R)


def local(layer_input, out_grad, proj_in, proj_out, query_features):
    half = layer_input.shape[0] // lax.axis_size("tensor")
    core = lax.axis_index("tensor")
    dp = lax.axis_size("dp")
    position = lax.axis_index("dp")

    blocks = [query_features] + [passed_along(query_features, "dp", d) for d in range(1, dp)]

    def projected(start):
        rows = lax.dynamic_slice_in_dim(layer_input, start, half, 0)
        return jnp.dot(rows, proj_in, preferred_element_type=jnp.float32)

    received = passed_along(projected((1 - core) * half), "tensor", 1)
    mine = lax.dynamic_slice_in_dim(out_grad, core * half, half, 0)
    right = jnp.dot(mine, proj_out, preferred_element_type=jnp.float32)
    left = projected(core * half) + received
    owned = example_features(left, right)

    queries = jnp.concatenate(blocks[::-1], 0)
    product = jnp.dot(
        owned, queries.T, precision=lax.Precision.HIGHEST, preferred_element_type=jnp.float32
    ) / (R * math.sqrt(LEN))
    return jnp.roll(product, (position + 1) * query_features.shape[0], axis=1)


def solution(mesh):
    in_specs = (
        P(("groups", "dp"), "tensor"),
        P(("groups", "dp"), None),
        P("tensor", None),
        P(),
        P(("groups", "dp"), None),
    )
    out_specs = P(("groups", "dp", "tensor"), None)
    return jax.shard_map(local, mesh=mesh, in_specs=in_specs, out_specs=out_specs, check_vma=False)
```

```python
import math

import jax
import jax.numpy as jnp
from jax import lax
from jax.sharding import PartitionSpec as P

R = 64
LEN = 128


def passed_along(block, axis, distance):
    devices = range(lax.axis_size(axis))
    route = [((i - distance) % len(devices), i) for i in devices]
    return lax.ppermute(block, axis, route)


def example_features(left, right):
    count = left.shape[0] // LEN
    features = jnp.einsum(
        "elr,els->ers",
        left.reshape(count, LEN, R),
        right.reshape(count, LEN, R),
        precision=lax.Precision.HIGHEST,
    )
    return features.reshape(count, R * R)


def local(layer_input, out_grad, proj_in, proj_out, query_features):
    half = layer_input.shape[0] // lax.axis_size("tensor")
    core = lax.axis_index("tensor")
    dp = lax.axis_size("dp")
    position = lax.axis_index("dp")

    width = query_features.shape[1] // lax.axis_size("tensor")
    piece = lax.dynamic_slice_in_dim(query_features, core * width, width, 1)
    part = lax.all_to_all(jnp.broadcast_to(piece, (dp,) + piece.shape), "dp", 0, 0)
    part = part.reshape(dp * piece.shape[0], width)

    def projected(start):
        rows = lax.dynamic_slice_in_dim(layer_input, start, half, 0)
        return jnp.dot(rows, proj_in, preferred_element_type=jnp.float32)

    received = passed_along(projected((1 - core) * half), "tensor", 1)
    mine = lax.dynamic_slice_in_dim(out_grad, core * half, half, 0)
    right = jnp.dot(mine, proj_out, preferred_element_type=jnp.float32)
    left = projected(core * half) + received
    owned = example_features(left, right)

    other = passed_along(part, "tensor", 1)

    def scored(start, queries):
        columns = lax.dynamic_slice_in_dim(owned, start * width, width, 1)
        return jnp.dot(
            columns, queries.T, precision=lax.Precision.HIGHEST, preferred_element_type=jnp.float32
        )

    return (scored(core, part) + scored(1 - core, other)) / (R * math.sqrt(LEN))


def solution(mesh):
    in_specs = (
        P(("groups", "dp"), "tensor"),
        P(("groups", "dp"), None),
        P("tensor", None),
        P(),
        P(("groups", "dp"), None),
    )
    out_specs = P(("groups", "dp", "tensor"), None)
    return jax.shard_map(local, mesh=mesh, in_specs=in_specs, out_specs=out_specs, check_vma=False)
```

```python
import math

import jax
import jax.numpy as jnp
from jax import lax
from jax.sharding import PartitionSpec as P

R = 64
LEN = 128


def example_features(left, right):
    count = left.shape[0] // LEN
    features = jnp.einsum(
        "elr,els->ers",
        left.reshape(count, LEN, R),
        right.reshape(count, LEN, R),
        precision=lax.Precision.HIGHEST,
    )
    return features.reshape(count, R * R)


def fetched(block, offsets):
    axes = ("dp", "tensor")
    dp, cores = (lax.axis_size(a) for a in axes)
    route = [((p ^ offsets[c]) * cores + c, p * cores + c) for p in range(dp) for c in range(cores)]
    return lax.ppermute(block, axes, route)


def swapped(block):
    return lax.ppermute(block, "tensor", [(0, 1), (1, 0)])


def local(layer_input, out_grad, proj_in, proj_out, query_features):
    half = layer_input.shape[0] // lax.axis_size("tensor")
    core = lax.axis_index("tensor")
    dp = lax.axis_size("dp")
    position = lax.axis_index("dp")
    block = query_features.shape[0]

    pairs = list(range(dp - 2, 1, -2))
    mine_blocks = [fetched(query_features, (m, m + 1)) for m in pairs]
    beside = fetched(query_features, (1, 1))

    def projected(start):
        rows = lax.dynamic_slice_in_dim(layer_input, start, half, 0)
        return jnp.dot(rows, proj_in, preferred_element_type=jnp.float32)

    received = swapped(projected((1 - core) * half))
    mine = lax.dynamic_slice_in_dim(out_grad, core * half, half, 0)
    right = jnp.dot(mine, proj_out, preferred_element_type=jnp.float32)
    left = projected(core * half) + received
    owned = example_features(left, right)

    first = jnp.concatenate(mine_blocks, 0)
    second = swapped(first)

    def scored(queries):
        return jnp.dot(
            owned, queries.T, precision=lax.Precision.HIGHEST, preferred_element_type=jnp.float32
        ) / (R * math.sqrt(LEN))

    near = scored(jnp.concatenate([query_features, beside], 0))
    product = jnp.concatenate([near, scored(first), scored(second)], 1)
    product = product.reshape(product.shape[0], dp, block)
    held = jnp.array([0, 1] + pairs + pairs)
    held = held + jnp.where(jnp.arange(dp) < 2, 0, jnp.where(jnp.arange(dp) < 1 + dp // 2, core, 1 - core))
    order = (held[:, None] == (jnp.arange(dp)[None, :] ^ position)).astype(jnp.float32)
    scores = jnp.einsum("ehb,hs->esb", product, order, precision=lax.Precision.HIGHEST)
    return scores.reshape(scores.shape[0], dp * block)


def solution(mesh):
    in_specs = (
        P(("groups", "dp"), "tensor"),
        P(("groups", "dp"), None),
        P("tensor", None),
        P(),
        P(("groups", "dp"), None),
    )
    out_specs = P(("groups", "dp", "tensor"), None)
    return jax.shard_map(local, mesh=mesh, in_specs=in_specs, out_specs=out_specs, check_vma=False)
```

```python
import functools
import math

import jax
import jax.numpy as jnp
from jax import lax
from jax.experimental import pallas as pl
from jax.experimental.pallas import tpu as pltpu
from jax.sharding import PartitionSpec as P

R = 64
LEN = 128
LANES = 128
MIB = 1024 * 1024


def fetched(block, offsets):
    axes = ("dp", "tensor")
    dp, cores = (lax.axis_size(a) for a in axes)
    route = [((p ^ offsets[c]) * cores + c, p * cores + c) for p in range(dp) for c in range(cores)]
    return lax.ppermute(block, axes, route)


def swapped(block):
    return lax.ppermute(block, "tensor", [(0, 1), (1, 0)])


def times_transposed(a, b, **kwargs):
    return lax.dot_general(
        a, b, (((1,), (1,)), ((), ())), preferred_element_type=jnp.float32, **kwargs
    )


def project_packed(start, rows, x_ref, p_ref, out_ref):
    part = rows // 2
    for k in range(2):
        x = x_ref[pl.ds(pl.multiple_of(start + k * part, part), part), :]
        out_ref[:, k * R : (k + 1) * R] = times_transposed(x, p_ref[...])


def sent_kernel(x_ref, p_ref, out_ref):
    rows = 2 * out_ref.shape[0]
    project_packed((1 - lax.axis_index("tensor")) * rows, rows, x_ref, p_ref, out_ref)


def kept_kernel(x_ref, p_ref, g_ref, q_ref, left_ref, right_ref):
    rows = 2 * left_ref.shape[0]
    start = lax.axis_index("tensor") * rows
    project_packed(start, rows, g_ref, q_ref, right_ref)
    project_packed(start, rows, x_ref, p_ref, left_ref)


def features_kernel(kept_ref, received_ref, right_ref, out_ref, square):
    packed = kept_ref.shape[0] // LEN
    for k in range(packed):
        rows = slice(k * LEN, (k + 1) * LEN)
        square[k] = lax.dot_general(
            kept_ref[rows, :] + received_ref[rows, :],
            right_ref[rows, :],
            (((0,), (0,)), ((), ())),
            precision=lax.Precision.HIGHEST,
            preferred_element_type=jnp.float32,
        )
        for h in range(2):
            e = h * packed + k
            even = square[k, pl.ds(h * R, R // 2, stride=2), :]
            odd = square[k, pl.ds(h * R + 1, R // 2, stride=2), :]
            lanes = slice(h * R, (h + 1) * R)
            out_ref[e * R // 2 : (e + 1) * R // 2, :] = jnp.concatenate(
                [even[:, lanes], odd[:, lanes]], 1
            )


def scores_kernel(dp, f_ref, own_ref, beside_ref, first_ref, second_ref, out_ref, sums):
    core, position = lax.axis_index("tensor"), lax.axis_index("dp")
    block = own_ref.shape[0]
    examples = out_ref.shape[0]
    tiles = own_ref.shape[1] // LANES
    pairs = list(range(dp - 2, 1, -2))
    held = [(own_ref, 0, [0]), (beside_ref, 0, [1])]
    for ref, side in ((first_ref, core), (second_ref, 1 - core)):
        for k in range(0, len(pairs), 2):
            held.append((ref, k * block, [m + side for m in pairs[k : k + 2]]))
    for group in range(0, len(held), 6):
        chosen = held[group : group + 6]
        totals = [[None] * examples for _ in chosen]
        for r in range(tiles):
            for i, (ref, row, offsets) in enumerate(chosen):
                q = ref[row : row + len(offsets) * block, r * LANES : (r + 1) * LANES]
                for e in range(examples):
                    term = q * f_ref[e * tiles + r : e * tiles + r + 1, :]
                    totals[i][e] = term if r == 0 else totals[i][e] + term
        for (ref, row, offsets), total in zip(chosen, totals):
            for j, offset in enumerate(offsets):
                for e in range(examples):
                    sums[position ^ offset, :, e * LANES : (e + 1) * LANES] = total[e][
                        j * block : (j + 1) * block, :
                    ]
    every = sums[...].reshape(dp * block, examples * LANES)
    row = lax.broadcasted_iota(jnp.int32, (examples, examples * LANES), 0)
    lane = lax.broadcasted_iota(jnp.int32, (examples, examples * LANES), 1)
    chosen = jnp.where(lane // LANES == row, 1.0, 0.0).astype(jnp.float32)
    out_ref[...] = times_transposed(chosen, every, precision=lax.Precision.HIGHEST) / (
        R * math.sqrt(LEN)
    )


def call(kernel, shapes, operands, flops, limit=16, scratch=()):
    outs = [jax.ShapeDtypeStruct(s, jnp.float32) for s in shapes]
    moved = sum(math.prod(o.shape) * o.dtype.itemsize for o in list(operands) + outs)
    spec = pl.BlockSpec(memory_space=pltpu.VMEM)
    return pl.pallas_call(
        kernel,
        out_shape=outs,
        in_specs=[spec] * len(operands),
        out_specs=[spec] * len(outs),
        scratch_shapes=list(scratch),
        cost_estimate=pl.CostEstimate(flops=flops, bytes_accessed=moved, transcendentals=0),
        compiler_params=pltpu.CompilerParams(vmem_limit_bytes=limit * MIB),
    )(*operands)


def local(layer_input, out_grad, proj_in, proj_out, query_features):
    dp = lax.axis_size("dp")
    half = layer_input.shape[0] // lax.axis_size("tensor")
    examples = half // LEN
    packed = (half // 2, 2 * R)
    pairs = list(range(dp - 2, 1, -2))

    first = [fetched(query_features, (m, m + 1)) for m in pairs]
    beside = fetched(query_features, (1, 1))

    p_in, p_out = proj_in.T, proj_out.T
    flops = 2 * half * R * layer_input.shape[1]
    (sent,) = call(sent_kernel, [packed], [layer_input, p_in], flops)
    received = swapped(sent)
    kept, right = call(kept_kernel, [packed] * 2, [layer_input, p_in, out_grad, p_out], 3 * flops, 24)
    (features,) = call(
        features_kernel,
        [(examples * R // 2, LANES)],
        [kept, received, right],
        12 * half * R * R,
        scratch=[pltpu.VMEM((half // 2 // LEN, LANES, LANES), jnp.float32)],
    )

    first = jnp.concatenate(first, 0)
    second = swapped(first)
    block = query_features.shape[0]
    (scores,) = call(
        functools.partial(scores_kernel, dp),
        [(examples, dp * block)],
        [features, query_features, beside, first, second],
        2 * examples * dp * block * R * R,
        scratch=[pltpu.VMEM((dp, block, examples * LANES), jnp.float32)],
    )
    return scores


def solution(mesh):
    in_specs = (
        P(("groups", "dp"), "tensor"),
        P(("groups", "dp"), None),
        P("tensor", None),
        P(),
        P(("groups", "dp"), None),
    )
    out_specs = P(("groups", "dp", "tensor"), None)
    return jax.shard_map(local, mesh=mesh, in_specs=in_specs, out_specs=out_specs, check_vma=False)
```

```python
import functools
import math

import jax
import jax.numpy as jnp
from jax import lax
from jax.experimental import pallas as pl
from jax.experimental.pallas import tpu as pltpu
from jax.sharding import PartitionSpec as P

R = 64
LEN = 128
LANES = 128
MIB = 1024 * 1024


def fetched(block, offsets):
    axes = ("dp", "tensor")
    dp, cores = (lax.axis_size(a) for a in axes)
    route = [((p ^ offsets[c]) * cores + c, p * cores + c) for p in range(dp) for c in range(cores)]
    return lax.ppermute(block, axes, route)


def swapped(block):
    return lax.ppermute(block, "tensor", [(0, 1), (1, 0)])


def times_transposed(a, b, **kwargs):
    return lax.dot_general(
        a, b, (((1,), (1,)), ((), ())), preferred_element_type=jnp.float32, **kwargs
    )


def start_rows(start, x_hbm, p_hbm, x, p, sem):
    chunks, depth = x.shape[:2]
    copies = [pltpu.make_async_copy(p_hbm, p, sem.at[chunks])]
    for k in range(chunks):
        rows = pl.ds(pl.multiple_of(start + k * depth, depth), depth)
        copies.append(pltpu.make_async_copy(x_hbm.at[rows, :], x.at[k], sem.at[k]))
    for copy in copies:
        copy.start()
    return copies


def project_packed(copies, x, p, out_ref):
    chunks, depth = x.shape[:2]
    copies[0].wait()
    for k in range(chunks):
        copies[k + 1].wait()
        h, row = divmod(k, chunks // 2)
        out_ref[row * depth : (row + 1) * depth, h * R : (h + 1) * R] = times_transposed(x[k], p[...])


def sent_kernel(x_hbm, p_hbm, out_ref, x, p, sem):
    start = (1 - lax.axis_index("tensor")) * 2 * out_ref.shape[0]
    project_packed(start_rows(start, x_hbm, p_hbm, x, p, sem), x, p, out_ref)


def kept_kernel(
    x_hbm, p_hbm, g_hbm, q_hbm, sent, block, left_ref, right_ref, out, x, p, sem, g, q, g_sem
):
    start = lax.axis_index("tensor") * 2 * left_ref.shape[0]
    g_copies = start_rows(start, g_hbm, q_hbm, g, q, g_sem)
    x_copies = start_rows(start, x_hbm, p_hbm, x, p, sem)
    project_packed(g_copies, g, q, right_ref)
    project_packed(x_copies, x, p, left_ref)


def features_kernel(kept_ref, received_ref, right_ref, out_ref, square):
    packed = kept_ref.shape[0] // LEN
    for k in range(packed):
        rows = slice(k * LEN, (k + 1) * LEN)
        square[k] = lax.dot_general(
            kept_ref[rows, :] + received_ref[rows, :],
            right_ref[rows, :],
            (((0,), (0,)), ((), ())),
            precision=lax.Precision.HIGHEST,
            preferred_element_type=jnp.float32,
        )
        for h in range(2):
            e = h * packed + k
            even = square[k, pl.ds(h * R, R // 2, stride=2), :]
            odd = square[k, pl.ds(h * R + 1, R // 2, stride=2), :]
            lanes = slice(h * R, (h + 1) * R)
            out_ref[e * R // 2 : (e + 1) * R // 2, :] = jnp.concatenate(
                [even[:, lanes], odd[:, lanes]], 1
            )


def scores_kernel(dp, f_ref, own_ref, beside_ref, first_ref, second_ref, out_ref, sums):
    core, position = lax.axis_index("tensor"), lax.axis_index("dp")
    block = own_ref.shape[0]
    examples = out_ref.shape[0]
    tiles = own_ref.shape[1] // LANES
    pairs = list(range(dp - 2, 1, -2))
    held = [(own_ref, 0, [0]), (beside_ref, 0, [1])]
    for ref, side in ((first_ref, core), (second_ref, 1 - core)):
        for k in range(0, len(pairs), 2):
            held.append((ref, k * block, [m + side for m in pairs[k : k + 2]]))
    for group in range(0, len(held), 6):
        chosen = held[group : group + 6]
        totals = [[None] * examples for _ in chosen]
        for r in range(tiles):
            for i, (ref, row, offsets) in enumerate(chosen):
                q = ref[row : row + len(offsets) * block, r * LANES : (r + 1) * LANES]
                for e in range(examples):
                    term = q * f_ref[e * tiles + r : e * tiles + r + 1, :]
                    totals[i][e] = term if r == 0 else totals[i][e] + term
        for (ref, row, offsets), total in zip(chosen, totals):
            for j, offset in enumerate(offsets):
                for e in range(examples):
                    sums[position ^ offset, :, e * LANES : (e + 1) * LANES] = total[e][
                        j * block : (j + 1) * block, :
                    ]
    every = sums[...].reshape(dp * block, examples * LANES)
    row = lax.broadcasted_iota(jnp.int32, (examples, examples * LANES), 0)
    lane = lax.broadcasted_iota(jnp.int32, (examples, examples * LANES), 1)
    chosen = jnp.where(lane // LANES == row, 1.0, 0.0).astype(jnp.float32)
    out_ref[...] = times_transposed(chosen, every, precision=lax.Precision.HIGHEST) / (
        R * math.sqrt(LEN)
    )


VMEM = pl.BlockSpec(memory_space=pltpu.VMEM)
ANY = pl.BlockSpec(memory_space=pl.ANY)


def call(kernel, shapes, operands, flops, scratch=(), in_specs=None, out_specs=None, limit=16, **kwargs):
    outs = [jax.ShapeDtypeStruct(s, jnp.float32) for s in shapes]
    moved = sum(math.prod(o.shape) * o.dtype.itemsize for o in list(operands) + outs)
    return pl.pallas_call(
        kernel,
        out_shape=outs,
        in_specs=in_specs or [VMEM] * len(operands),
        out_specs=out_specs or [VMEM] * len(outs),
        scratch_shapes=list(scratch),
        cost_estimate=pl.CostEstimate(flops=flops, bytes_accessed=moved, transcendentals=0),
        compiler_params=pltpu.CompilerParams(vmem_limit_bytes=limit * MIB),
        **kwargs,
    )(*operands)


def row_buffers(rows, x, p, chunks=4):
    return [
        pltpu.VMEM((chunks, rows // chunks, x.shape[1]), x.dtype),
        pltpu.VMEM(p.shape, p.dtype),
        pltpu.SemaphoreType.DMA((chunks + 1,)),
    ]


def local(layer_input, out_grad, proj_in, proj_out, query_features):
    dp = lax.axis_size("dp")
    half = layer_input.shape[0] // lax.axis_size("tensor")
    examples = half // LEN
    packed = (half // 2, 2 * R)
    pairs = list(range(dp - 2, 1, -2))

    first = [fetched(query_features, (m, m + 1)) for m in pairs]
    beside = fetched(query_features, (1, 1))

    p_in, p_out = proj_in.T, proj_out.T
    flops = 2 * half * R * layer_input.shape[1]
    x_buffers = row_buffers(half, layer_input, p_in)
    (sent,) = call(
        sent_kernel, [packed], [layer_input, p_in], flops, x_buffers, in_specs=[ANY] * 2
    )
    received = swapped(sent)
    kept, right, first[0] = call(
        kept_kernel,
        [packed, packed, first[0].shape],
        [layer_input, p_in, out_grad, p_out, sent, first[0]],
        3 * flops,
        x_buffers + row_buffers(half, out_grad, p_out),
        in_specs=[ANY] * 6,
        out_specs=[VMEM, VMEM, ANY],
        input_output_aliases={5: 2},
    )
    (features,) = call(
        features_kernel,
        [(examples * R // 2, LANES)],
        [kept, received, right],
        12 * half * R * R,
        scratch=[pltpu.VMEM((half // 2 // LEN, LANES, LANES), jnp.float32)],
    )

    first = jnp.concatenate(first, 0)
    second = swapped(first)
    block = query_features.shape[0]
    (scores,) = call(
        functools.partial(scores_kernel, dp),
        [(examples, dp * block)],
        [features, query_features, beside, first, second],
        2 * examples * dp * block * R * R,
        scratch=[pltpu.VMEM((dp, block, examples * LANES), jnp.float32)],
    )
    return scores


def solution(mesh):
    in_specs = (
        P(("groups", "dp"), "tensor"),
        P(("groups", "dp"), None),
        P("tensor", None),
        P(),
        P(("groups", "dp"), None),
    )
    out_specs = P(("groups", "dp", "tensor"), None)
    return jax.shard_map(local, mesh=mesh, in_specs=in_specs, out_specs=out_specs, check_vma=False)
```

```python
import math

import jax
import jax.numpy as jnp
from jax import lax
from jax.experimental import pallas as pl
from jax.experimental.pallas import tpu as pltpu
from jax.sharding import PartitionSpec as P

R = 64
LEN = 128
LANES = 128
MIB = 1024 * 1024


def fetched(block, offsets):
    axes = ("dp", "tensor")
    dp, cores = (lax.axis_size(a) for a in axes)
    route = [((p ^ offsets[c]) * cores + c, p * cores + c) for p in range(dp) for c in range(cores)]
    return lax.ppermute(block, axes, route)


def swapped(block):
    return lax.ppermute(block, "tensor", [(0, 1), (1, 0)])


def times_transposed(a, b, **kwargs):
    return lax.dot_general(
        a, b, (((1,), (1,)), ((), ())), preferred_element_type=jnp.float32, **kwargs
    )


def start_rows(start, x_hbm, p_hbm, x, p, sem):
    chunks, depth = x.shape[:2]
    copies = [pltpu.make_async_copy(p_hbm, p, sem.at[chunks])]
    for k in range(chunks):
        rows = pl.ds(pl.multiple_of(start + k * depth, depth), depth)
        copies.append(pltpu.make_async_copy(x_hbm.at[rows, :], x.at[k], sem.at[k]))
    for copy in copies:
        copy.start()
    return copies


def project_packed(copies, x, p, out_ref):
    chunks, depth = x.shape[:2]
    copies[0].wait()
    for k in range(chunks):
        copies[k + 1].wait()
        h, row = divmod(k, chunks // 2)
        out_ref[row * depth : (row + 1) * depth, h * R : (h + 1) * R] = times_transposed(x[k], p[...])


def sent_kernel(x_hbm, p_hbm, out_ref, x, p, sem):
    start = (1 - lax.axis_index("tensor")) * 2 * out_ref.shape[0]
    project_packed(start_rows(start, x_hbm, p_hbm, x, p, sem), x, p, out_ref)


def kept_kernel(x_hbm, p_hbm, g_hbm, q_hbm, _, __, left_ref, right_ref, x, p, sem, g, q, g_sem):
    start = lax.axis_index("tensor") * 2 * left_ref.shape[0]
    g_copies = start_rows(start, g_hbm, q_hbm, g, q, g_sem)
    x_copies = start_rows(start, x_hbm, p_hbm, x, p, sem)
    project_packed(g_copies, g, q, right_ref)
    project_packed(x_copies, x, p, left_ref)


def features_kernel(kept_ref, received_ref, right_ref, _, out_ref, __, square):
    packed = kept_ref.shape[0] // LEN
    for k in range(packed):
        rows = slice(k * LEN, (k + 1) * LEN)
        square[k] = lax.dot_general(
            kept_ref[rows, :] + received_ref[rows, :],
            right_ref[rows, :],
            (((0,), (0,)), ((), ())),
            precision=lax.Precision.HIGHEST,
            preferred_element_type=jnp.float32,
        )
        for h in range(2):
            e = h * packed + k
            even = square[k, pl.ds(h * R, R // 2, stride=2), :]
            odd = square[k, pl.ds(h * R + 1, R // 2, stride=2), :]
            lanes = slice(h * R, (h + 1) * R)
            out_ref[e * R // 2 : (e + 1) * R // 2, :] = jnp.concatenate(
                [even[:, lanes], odd[:, lanes]], 1
            )


def add_products(held, f_ref, sums):
    position = lax.axis_index("dp")
    block = sums.shape[1]
    examples = sums.shape[2] // LANES
    tiles = f_ref.shape[0] // examples
    sums[...] = jnp.zeros_like(sums)
    for group in range(0, len(held), 6):
        chosen = held[group : group + 6]
        totals = [[None] * examples for _ in chosen]
        for r in range(tiles):
            for i, (ref, row, offsets) in enumerate(chosen):
                q = ref[row : row + len(offsets) * block, r * LANES : (r + 1) * LANES]
                for e in range(examples):
                    term = q * f_ref[e * tiles + r : e * tiles + r + 1, :]
                    totals[i][e] = term if r == 0 else totals[i][e] + term
        for (ref, row, offsets), total in zip(chosen, totals):
            for j, offset in enumerate(offsets):
                for e in range(examples):
                    sums[position ^ offset, :, e * LANES : (e + 1) * LANES] = total[e][
                        j * block : (j + 1) * block, :
                    ]


def paired(ref, side, dp, block):
    pairs = list(range(dp - 2, 1, -2))
    return [
        (ref, k * block, [m + side for m in pairs[k : k + 2]]) for k in range(0, len(pairs), 2)
    ]


def near_kernel(f_ref, own_ref, beside_ref, first_ref, sums):
    dp, block, _ = sums.shape
    held = [(own_ref, 0, [0]), (beside_ref, 0, [1])]
    add_products(held + paired(first_ref, lax.axis_index("tensor"), dp, block), f_ref, sums)


def scores_kernel(f_ref, second_ref, near_ref, out_ref, sums):
    dp, block, width = sums.shape
    add_products(paired(second_ref, 1 - lax.axis_index("tensor"), dp, block), f_ref, sums)
    every = (sums[...] + near_ref[...]).reshape(dp * block, width)
    row = lax.broadcasted_iota(jnp.int32, (width // LANES, width), 0)
    lane = lax.broadcasted_iota(jnp.int32, (width // LANES, width), 1)
    own_lanes = jnp.where(lane // LANES == row, 1.0, 0.0).astype(jnp.float32)
    out_ref[...] = times_transposed(own_lanes, every, precision=lax.Precision.HIGHEST) / (
        R * math.sqrt(LEN)
    )


VMEM = pl.BlockSpec(memory_space=pltpu.VMEM)
ANY = pl.BlockSpec(memory_space=pl.ANY)


def call(kernel, shapes, operands, flops, scratch=(), in_specs=None, out_specs=None, limit=16, **kwargs):
    outs = [jax.ShapeDtypeStruct(s, jnp.float32) for s in shapes]
    moved = sum(math.prod(o.shape) * o.dtype.itemsize for o in list(operands) + outs)
    return pl.pallas_call(
        kernel,
        out_shape=outs,
        in_specs=in_specs or [VMEM] * len(operands),
        out_specs=out_specs or [VMEM] * len(outs),
        scratch_shapes=list(scratch),
        cost_estimate=pl.CostEstimate(flops=flops, bytes_accessed=moved, transcendentals=0),
        compiler_params=pltpu.CompilerParams(vmem_limit_bytes=limit * MIB),
        **kwargs,
    )(*operands)


def row_buffers(rows, x, p, chunks=4):
    return [
        pltpu.VMEM((chunks, rows // chunks, x.shape[1]), x.dtype),
        pltpu.VMEM(p.shape, p.dtype),
        pltpu.SemaphoreType.DMA((chunks + 1,)),
    ]


def local(layer_input, out_grad, proj_in, proj_out, query_features):
    dp = lax.axis_size("dp")
    half = layer_input.shape[0] // lax.axis_size("tensor")
    examples = half // LEN
    packed = (half // 2, 2 * R)
    pairs = list(range(dp - 2, 1, -2))

    first = [fetched(query_features, (m, m + 1)) for m in pairs]
    beside = fetched(query_features, (1, 1))

    p_in, p_out = proj_in.T, proj_out.T
    flops = 2 * half * R * layer_input.shape[1]
    x_buffers = row_buffers(half, layer_input, p_in)
    (sent,) = call(
        sent_kernel, [packed], [layer_input, p_in], flops, x_buffers, in_specs=[ANY] * 2, limit=53
    )
    received = swapped(sent)
    kept, right = call(
        kept_kernel,
        [packed, packed],
        [layer_input, p_in, out_grad, p_out, sent, beside],
        3 * flops,
        x_buffers + row_buffers(half, out_grad, p_out),
        in_specs=[ANY] * 6,
        limit=53,
    )
    features, first[0] = call(
        features_kernel,
        [(examples * R // 2, LANES), first[0].shape],
        [kept, received, right, first[0]],
        12 * half * R * R,
        scratch=[pltpu.VMEM((half // 2 // LEN, LANES, LANES), jnp.float32)],
        in_specs=[VMEM] * 3 + [ANY],
        out_specs=[VMEM, ANY],
        input_output_aliases={3: 1},
    )

    first = jnp.concatenate(first, 0)
    second = swapped(first)
    block = query_features.shape[0]
    sums = (dp, block, examples * LANES)
    flops = 2 * examples * dp * block * R * R
    (near,) = call(near_kernel, [sums], [features, query_features, beside, first], flops)
    (scores,) = call(
        scores_kernel,
        [(examples, dp * block)],
        [features, second, near],
        flops,
        scratch=[pltpu.VMEM(sums, jnp.float32)],
    )
    return scores


def solution(mesh):
    in_specs = (
        P(("groups", "dp"), "tensor"),
        P(("groups", "dp"), None),
        P("tensor", None),
        P(),
        P(("groups", "dp"), None),
    )
    out_specs = P(("groups", "dp", "tensor"), None)
    return jax.shard_map(local, mesh=mesh, in_specs=in_specs, out_specs=out_specs, check_vma=False)
```

```python
import math

import jax
import jax.numpy as jnp
from jax import lax
from jax.experimental import pallas as pl
from jax.experimental.pallas import tpu as pltpu
from jax.sharding import PartitionSpec as P

R = 64
LEN = 128
LANES = 128
MIB = 1024 * 1024


def fetched(block, offsets):
    axes = ("dp", "tensor")
    dp, cores = (lax.axis_size(a) for a in axes)
    route = [((p ^ offsets[c]) * cores + c, p * cores + c) for p in range(dp) for c in range(cores)]
    return lax.ppermute(block, axes, route)


def swapped(block):
    return lax.ppermute(block, "tensor", [(0, 1), (1, 0)])


def times_transposed(a, b, **kwargs):
    return lax.dot_general(
        a, b, (((1,), (1,)), ((), ())), preferred_element_type=jnp.float32, **kwargs
    )


def ready_kernel(x_ref, out_ref):
    out_ref[...] = x_ref[...]


def project_packed(start, x_ref, p_ref, out_ref):
    rows = out_ref.shape[0]
    for h in range(2):
        some = x_ref[pl.ds(pl.multiple_of(start + h * rows, rows), rows), :]
        out_ref[:, h * R : (h + 1) * R] = times_transposed(some, p_ref[...])


def sent_kernel(x_ref, p_ref, _, out_ref):
    start = (1 - lax.axis_index("tensor")) * 2 * out_ref.shape[0]
    project_packed(start, x_ref, p_ref, out_ref)


def kept_kernel(x_ref, p_ref, g_ref, q_ref, _, __, left_ref, right_ref):
    start = lax.axis_index("tensor") * 2 * left_ref.shape[0]
    project_packed(start, g_ref, q_ref, right_ref)
    project_packed(start, x_ref, p_ref, left_ref)


def features_kernel(kept_ref, received_ref, right_ref, _, out_ref, __, square):
    packed = kept_ref.shape[0] // LEN
    for k in range(packed):
        rows = slice(k * LEN, (k + 1) * LEN)
        square[k] = lax.dot_general(
            kept_ref[rows, :] + received_ref[rows, :],
            right_ref[rows, :],
            (((0,), (0,)), ((), ())),
            precision=lax.Precision.HIGHEST,
            preferred_element_type=jnp.float32,
        )
        for h in range(2):
            e = h * packed + k
            even = square[k, pl.ds(h * R, R // 2, stride=2), :]
            odd = square[k, pl.ds(h * R + 1, R // 2, stride=2), :]
            lanes = slice(h * R, (h + 1) * R)
            out_ref[e * R // 2 : (e + 1) * R // 2, :] = jnp.concatenate(
                [even[:, lanes], odd[:, lanes]], 1
            )


def add_products(held, f_ref, sums):
    position = lax.axis_index("dp")
    block = sums.shape[1]
    examples = sums.shape[2] // LANES
    tiles = f_ref.shape[0] // examples
    sums[...] = jnp.zeros_like(sums)
    for group in range(0, len(held), 6):
        chosen = held[group : group + 6]
        totals = [[None] * examples for _ in chosen]
        for r in range(tiles):
            for i, (ref, row, offsets) in enumerate(chosen):
                q = ref[row : row + len(offsets) * block, r * LANES : (r + 1) * LANES]
                for e in range(examples):
                    term = q * f_ref[e * tiles + r : e * tiles + r + 1, :]
                    totals[i][e] = term if r == 0 else totals[i][e] + term
        for (ref, row, offsets), total in zip(chosen, totals):
            for j, offset in enumerate(offsets):
                for e in range(examples):
                    sums[position ^ offset, :, e * LANES : (e + 1) * LANES] = total[e][
                        j * block : (j + 1) * block, :
                    ]


def paired(ref, side, dp, block):
    pairs = list(range(dp - 2, 1, -2))
    return [
        (ref, k * block, [m + side for m in pairs[k : k + 2]]) for k in range(0, len(pairs), 2)
    ]


def near_kernel(f_ref, own_ref, beside_ref, first_ref, sums):
    dp, block, _ = sums.shape
    held = [(own_ref, 0, [0]), (beside_ref, 0, [1])]
    add_products(held + paired(first_ref, lax.axis_index("tensor"), dp, block), f_ref, sums)


def scores_kernel(f_ref, second_ref, near_ref, out_ref, sums):
    dp, block, width = sums.shape
    add_products(paired(second_ref, 1 - lax.axis_index("tensor"), dp, block), f_ref, sums)
    every = (sums[...] + near_ref[...]).reshape(dp * block, width)
    row = lax.broadcasted_iota(jnp.int32, (width // LANES, width), 0)
    lane = lax.broadcasted_iota(jnp.int32, (width // LANES, width), 1)
    own_lanes = jnp.where(lane // LANES == row, 1.0, 0.0).astype(jnp.float32)
    out_ref[...] = times_transposed(own_lanes, every, precision=lax.Precision.HIGHEST) / (
        R * math.sqrt(LEN)
    )


VMEM = pl.BlockSpec(memory_space=pltpu.VMEM)
ANY = pl.BlockSpec(memory_space=pl.ANY)


def call(kernel, shapes, operands, flops, scratch=(), in_specs=None, out_specs=None, limit=16, **kwargs):
    outs = [jax.ShapeDtypeStruct(s, jnp.float32) for s in shapes]
    moved = sum(math.prod(o.shape) * o.dtype.itemsize for o in list(operands) + outs)
    return pl.pallas_call(
        kernel,
        out_shape=outs,
        in_specs=in_specs or [VMEM] * len(operands),
        out_specs=out_specs or [VMEM] * len(outs),
        scratch_shapes=list(scratch),
        cost_estimate=pl.CostEstimate(flops=flops, bytes_accessed=moved, transcendentals=0),
        compiler_params=pltpu.CompilerParams(vmem_limit_bytes=limit * MIB),
        **kwargs,
    )(*operands)


def local(layer_input, out_grad, proj_in, proj_out, query_features):
    dp = lax.axis_size("dp")
    half = layer_input.shape[0] // lax.axis_size("tensor")
    examples = half // LEN
    packed = (half // 2, 2 * R)
    pairs = list(range(dp - 2, 1, -2))

    (queries,) = call(ready_kernel, [query_features.shape], [query_features], 10**10)

    beside = fetched(queries, (1, 1))
    first = [fetched(queries, (m, m + 1)) for m in pairs]

    p_in, p_out = proj_in.T, proj_out.T
    flops = 2 * half * R * layer_input.shape[1]
    (sent,) = call(
        sent_kernel, [packed], [layer_input, p_in, queries], flops, in_specs=[VMEM] * 2 + [ANY]
    )
    received = swapped(sent)
    kept, right = call(
        kept_kernel,
        [packed, packed],
        [layer_input, p_in, out_grad, p_out, sent, beside],
        3 * flops,
        in_specs=[VMEM] * 4 + [ANY] * 2,
    )
    features, first[0] = call(
        features_kernel,
        [(examples * R // 2, LANES), first[0].shape],
        [kept, received, right, first[0]],
        12 * half * R * R,
        scratch=[pltpu.VMEM((half // 2 // LEN, LANES, LANES), jnp.float32)],
        in_specs=[VMEM] * 3 + [ANY],
        out_specs=[VMEM, ANY],
        input_output_aliases={3: 1},
    )

    first = jnp.concatenate(first, 0)
    second = swapped(first)
    block = query_features.shape[0]
    sums = (dp, block, examples * LANES)
    flops = 2 * examples * dp * block * R * R
    (near,) = call(near_kernel, [sums], [features, queries, beside, first], flops)
    (scores,) = call(
        scores_kernel,
        [(examples, dp * block)],
        [features, second, near],
        flops,
        scratch=[pltpu.VMEM(sums, jnp.float32)],
    )
    return scores


def solution(mesh):
    in_specs = (
        P(("groups", "dp"), "tensor"),
        P(("groups", "dp"), None),
        P("tensor", None),
        P(),
        P(("groups", "dp"), None),
    )
    out_specs = P(("groups", "dp", "tensor"), None)
    return jax.shard_map(local, mesh=mesh, in_specs=in_specs, out_specs=out_specs, check_vma=False)
```

```python
import math

import jax
import jax.numpy as jnp
from jax import lax
from jax.experimental import pallas as pl
from jax.experimental.pallas import tpu as pltpu
from jax.sharding import PartitionSpec as P

R = 64
LEN = 128
LANES = 128
MIB = 1024 * 1024


def fetched(block, offsets):
    axes = ("dp", "tensor")
    dp, cores = (lax.axis_size(a) for a in axes)
    route = [((p ^ offsets[c]) * cores + c, p * cores + c) for p in range(dp) for c in range(cores)]
    return lax.ppermute(block, axes, route)


def gathered_offsets(dp):
    far = list(range(dp // 2, dp, 2))
    near = [o for o in range(dp // 2) if not o & 2][::-1]
    return far + [o ^ 1 for o in far], near + [o ^ 2 for o in near]


def swapped(block):
    return lax.ppermute(block, "tensor", [(0, 1), (1, 0)])


def times_transposed(a, b, **kwargs):
    return lax.dot_general(
        a, b, (((1,), (1,)), ((), ())), preferred_element_type=jnp.float32, **kwargs
    )


def ready_kernel(x_ref, out_ref):
    out_ref[...] = x_ref[...]


def project_packed(start, x_ref, p_ref, out_ref):
    rows = out_ref.shape[0]
    for h in range(2):
        some = x_ref[pl.ds(pl.multiple_of(start + h * rows, rows), rows), :]
        out_ref[:, h * R : (h + 1) * R] = times_transposed(some, p_ref[...])


def sent_kernel(x_ref, p_ref, _, out_ref):
    start = (1 - lax.axis_index("tensor")) * 2 * out_ref.shape[0]
    project_packed(start, x_ref, p_ref, out_ref)


def kept_kernel(x_ref, p_ref, g_ref, q_ref, _, left_ref, right_ref):
    start = lax.axis_index("tensor") * 2 * left_ref.shape[0]
    project_packed(start, g_ref, q_ref, right_ref)
    project_packed(start, x_ref, p_ref, left_ref)


def features_kernel(kept_ref, received_ref, right_ref, _, out_ref, __, square):
    packed = kept_ref.shape[0] // LEN
    for k in range(packed):
        rows = slice(k * LEN, (k + 1) * LEN)
        square[k] = lax.dot_general(
            kept_ref[rows, :] + received_ref[rows, :],
            right_ref[rows, :],
            (((0,), (0,)), ((), ())),
            precision=lax.Precision.HIGHEST,
            preferred_element_type=jnp.float32,
        )
        for h in range(2):
            e = h * packed + k
            even = square[k, pl.ds(h * R, R // 2, stride=2), :]
            odd = square[k, pl.ds(h * R + 1, R // 2, stride=2), :]
            lanes = slice(h * R, (h + 1) * R)
            out_ref[e * R // 2 : (e + 1) * R // 2, :] = jnp.concatenate(
                [even[:, lanes], odd[:, lanes]], 1
            )


def in_order(ref, core, shape):
    dp, block, _ = shape
    offsets = [jnp.where(core == 0, a, b) for a, b in zip(*gathered_offsets(dp))]
    return [(ref, k * block, offsets[k : k + 2]) for k in range(0, len(offsets), 2)]


def add_products(held, f_ref, sums):
    position = lax.axis_index("dp")
    block = sums.shape[1]
    examples = sums.shape[2] // LANES
    tiles = f_ref.shape[0] // examples
    for group in range(0, len(held), 6):
        chosen = held[group : group + 6]
        totals = [[None] * examples for _ in chosen]
        for r in range(tiles):
            for i, (ref, row, offsets) in enumerate(chosen):
                q = ref[row : row + len(offsets) * block, r * LANES : (r + 1) * LANES]
                for e in range(examples):
                    term = q * f_ref[e * tiles + r : e * tiles + r + 1, :]
                    totals[i][e] = term if r == 0 else totals[i][e] + term
        for (ref, row, offsets), total in zip(chosen, totals):
            for j, offset in enumerate(offsets):
                for e in range(examples):
                    sums[position ^ offset, :, e * LANES : (e + 1) * LANES] = total[e][
                        j * block : (j + 1) * block, :
                    ]


def near_kernel(f_ref, own_ref, first_ref, sums):
    held = [(own_ref, 0, [0])] + in_order(first_ref, lax.axis_index("tensor"), sums.shape)
    sums[...] = jnp.zeros_like(sums)
    add_products(held, f_ref, sums)


def scores_kernel(f_ref, second_ref, near_ref, out_ref, sums):
    dp, block, width = sums.shape
    sums[...] = near_ref[...]
    add_products(in_order(second_ref, 1 - lax.axis_index("tensor"), sums.shape), f_ref, sums)
    every = sums[...].reshape(dp * block, width)
    row = lax.broadcasted_iota(jnp.int32, (width // LANES, width), 0)
    lane = lax.broadcasted_iota(jnp.int32, (width // LANES, width), 1)
    own_lanes = jnp.where(lane // LANES == row, 1.0, 0.0).astype(jnp.float32)
    out_ref[...] = times_transposed(own_lanes, every, precision=lax.Precision.HIGHEST) / (
        R * math.sqrt(LEN)
    )


VMEM = pl.BlockSpec(memory_space=pltpu.VMEM)
ANY = pl.BlockSpec(memory_space=pl.ANY)


def call(kernel, shapes, operands, flops, scratch=(), in_specs=None, out_specs=None, limit=16, **kwargs):
    outs = [jax.ShapeDtypeStruct(s, jnp.float32) for s in shapes]
    moved = sum(math.prod(o.shape) * o.dtype.itemsize for o in list(operands) + outs)
    return pl.pallas_call(
        kernel,
        out_shape=outs,
        in_specs=in_specs or [VMEM] * len(operands),
        out_specs=out_specs or [VMEM] * len(outs),
        scratch_shapes=list(scratch),
        cost_estimate=pl.CostEstimate(flops=flops, bytes_accessed=moved, transcendentals=0),
        compiler_params=pltpu.CompilerParams(vmem_limit_bytes=limit * MIB),
        **kwargs,
    )(*operands)


def local(layer_input, out_grad, proj_in, proj_out, query_features):
    dp = lax.axis_size("dp")
    half = layer_input.shape[0] // lax.axis_size("tensor")
    examples = half // LEN
    packed = (half // 2, 2 * R)

    (queries,) = call(ready_kernel, [query_features.shape], [query_features], 10**10)

    direct = [fetched(queries, o) for o in list(zip(*gathered_offsets(dp)))[: dp // 4]]
    relayed = fetched(jnp.concatenate(direct, 0), (1, 2))

    p_in, p_out = proj_in.T, proj_out.T
    flops = 2 * half * R * layer_input.shape[1]
    (sent,) = call(
        sent_kernel, [packed], [layer_input, p_in, queries], flops, in_specs=[VMEM] * 2 + [ANY]
    )
    received = swapped(sent)
    kept, right = call(
        kept_kernel,
        [packed, packed],
        [layer_input, p_in, out_grad, p_out, sent],
        3 * flops,
        in_specs=[VMEM] * 4 + [ANY],
    )
    features, relayed = call(
        features_kernel,
        [(examples * R // 2, LANES), relayed.shape],
        [kept, received, right, relayed],
        12 * half * R * R,
        scratch=[pltpu.VMEM((half // 2 // LEN, LANES, LANES), jnp.float32)],
        in_specs=[VMEM] * 3 + [ANY],
        out_specs=[VMEM, ANY],
        input_output_aliases={3: 1},
    )

    first = jnp.concatenate(direct + [relayed], 0)
    second = swapped(first)
    block = query_features.shape[0]
    sums = (dp, block, examples * LANES)
    flops = 2 * examples * dp * block * R * R
    (near,) = call(near_kernel, [sums], [features, queries, first], flops)
    (scores,) = call(
        scores_kernel,
        [(examples, dp * block)],
        [features, second, near],
        flops,
        scratch=[pltpu.VMEM(sums, jnp.float32)],
    )
    return scores


def solution(mesh):
    in_specs = (
        P(("groups", "dp"), "tensor"),
        P(("groups", "dp"), None),
        P("tensor", None),
        P(),
        P(("groups", "dp"), None),
    )
    out_specs = P(("groups", "dp", "tensor"), None)
    return jax.shard_map(local, mesh=mesh, in_specs=in_specs, out_specs=out_specs, check_vma=False)
```

```python
import math

import jax
import jax.numpy as jnp
from jax import lax
from jax.experimental import pallas as pl
from jax.experimental.pallas import tpu as pltpu
from jax.sharding import PartitionSpec as P

R = 64
LEN = 128
LANES = 128
MIB = 1024 * 1024


def fetched(block, offsets):
    axes = ("dp", "tensor")
    dp, cores = (lax.axis_size(a) for a in axes)
    route = [((p ^ offsets[c]) * cores + c, p * cores + c) for p in range(dp) for c in range(cores)]
    return lax.ppermute(block, axes, route)


def swapped(block):
    return lax.ppermute(block, "tensor", [(0, 1), (1, 0)])


def times_transposed(a, b, **kwargs):
    return lax.dot_general(
        a, b, (((1,), (1,)), ((), ())), preferred_element_type=jnp.float32, **kwargs
    )


def ready_kernel(out_ref):
    out_ref[...] = jnp.zeros_like(out_ref)


def project_packed(start, x_ref, p_ref, out_ref):
    rows = out_ref.shape[0]
    for h in range(2):
        some = x_ref[pl.ds(pl.multiple_of(start + h * rows, rows), rows), :]
        out_ref[:, h * R : (h + 1) * R] = times_transposed(some, p_ref[...])


def sent_kernel(x_ref, p_ref, _, out_ref):
    start = (1 - lax.axis_index("tensor")) * 2 * out_ref.shape[0]
    project_packed(start, x_ref, p_ref, out_ref)


def kept_kernel(x_ref, p_ref, g_ref, q_ref, _, left_ref, right_ref):
    start = lax.axis_index("tensor") * 2 * left_ref.shape[0]
    project_packed(start, g_ref, q_ref, right_ref)
    project_packed(start, x_ref, p_ref, left_ref)


def order_kernel(*_):
    pass


def features_kernel(kept_ref, received_ref, right_ref, out_ref, square):
    packed = kept_ref.shape[0] // LEN
    for k in range(packed):
        rows = slice(k * LEN, (k + 1) * LEN)
        square[k] = lax.dot_general(
            kept_ref[rows, :] + received_ref[rows, :],
            right_ref[rows, :],
            (((0,), (0,)), ((), ())),
            precision=lax.Precision.HIGHEST,
            preferred_element_type=jnp.float32,
        )
        for h in range(2):
            e = h * packed + k
            even = square[k, pl.ds(h * R, R // 2, stride=2), :]
            odd = square[k, pl.ds(h * R + 1, R // 2, stride=2), :]
            lanes = slice(h * R, (h + 1) * R)
            out_ref[e * R // 2 : (e + 1) * R // 2, :] = jnp.concatenate(
                [even[:, lanes], odd[:, lanes]], 1
            )


def add_products(held, f_ref, sums):
    position = lax.axis_index("dp")
    block = sums.shape[1]
    examples = sums.shape[2] // LANES
    tiles = f_ref.shape[0] // examples
    sums[...] = jnp.zeros_like(sums)
    for group in range(0, len(held), 6):
        chosen = held[group : group + 6]
        totals = [[None] * examples for _ in chosen]
        for r in range(tiles):
            for i, (ref, row, offsets) in enumerate(chosen):
                q = ref[row : row + len(offsets) * block, r * LANES : (r + 1) * LANES]
                for e in range(examples):
                    term = q * f_ref[e * tiles + r : e * tiles + r + 1, :]
                    totals[i][e] = term if r == 0 else totals[i][e] + term
        for (ref, row, offsets), total in zip(chosen, totals):
            for j, offset in enumerate(offsets):
                for e in range(examples):
                    sums[position ^ offset, :, e * LANES : (e + 1) * LANES] = total[e][
                        j * block : (j + 1) * block, :
                    ]


def paired(ref, side, dp, block):
    pairs = list(range(dp - 2, 1, -2))
    return [
        (ref, k * block, [m + side for m in pairs[k : k + 2]]) for k in range(0, len(pairs), 2)
    ]


def near_kernel(f_ref, own_ref, beside_ref, first_ref, sums):
    dp, block, _ = sums.shape
    held = [(own_ref, 0, [0]), (beside_ref, 0, [1])]
    add_products(held + paired(first_ref, lax.axis_index("tensor"), dp, block), f_ref, sums)


def scores_kernel(f_ref, second_ref, near_ref, out_ref, sums):
    dp, block, width = sums.shape
    add_products(paired(second_ref, 1 - lax.axis_index("tensor"), dp, block), f_ref, sums)
    every = (sums[...] + near_ref[...]).reshape(dp * block, width)
    row = lax.broadcasted_iota(jnp.int32, (width // LANES, width), 0)
    lane = lax.broadcasted_iota(jnp.int32, (width // LANES, width), 1)
    own_lanes = jnp.where(lane // LANES == row, 1.0, 0.0).astype(jnp.float32)
    out_ref[...] = times_transposed(own_lanes, every, precision=lax.Precision.HIGHEST) / (
        R * math.sqrt(LEN)
    )


VMEM = pl.BlockSpec(memory_space=pltpu.VMEM)
ANY = pl.BlockSpec(memory_space=pl.ANY)


def call(kernel, shapes, operands, flops, scratch=(), in_specs=None, out_specs=None, limit=16, **kwargs):
    outs = [jax.ShapeDtypeStruct(s, jnp.float32) for s in shapes]
    moved = sum(math.prod(o.shape) * o.dtype.itemsize for o in list(operands) + outs)
    return pl.pallas_call(
        kernel,
        out_shape=outs,
        in_specs=in_specs or [VMEM] * len(operands),
        out_specs=out_specs or [VMEM] * len(outs),
        scratch_shapes=list(scratch),
        cost_estimate=pl.CostEstimate(flops=flops, bytes_accessed=moved, transcendentals=0),
        compiler_params=pltpu.CompilerParams(vmem_limit_bytes=limit * MIB),
        **kwargs,
    )(*operands)


def local(layer_input, out_grad, proj_in, proj_out, query_features):
    dp = lax.axis_size("dp")
    half = layer_input.shape[0] // lax.axis_size("tensor")
    examples = half // LEN
    packed = (half // 2, 2 * R)
    pairs = list(range(dp - 2, 1, -2))

    (ready,) = call(ready_kernel, [(8, LANES)], [], 10**10)

    beside = fetched(query_features, (1, 1))
    first = [fetched(query_features, (m, m + 1)) for m in pairs]

    p_in, p_out = proj_in.T, proj_out.T
    flops = 2 * half * R * layer_input.shape[1]
    (sent,) = call(
        sent_kernel, [packed], [layer_input, p_in, ready], flops, in_specs=[VMEM] * 2 + [ANY]
    )
    received = swapped(sent)
    kept, right = call(
        kept_kernel,
        [packed, packed],
        [layer_input, p_in, out_grad, p_out, sent],
        3 * flops,
        in_specs=[VMEM] * 4 + [ANY],
    )
    operands = [beside] + first[1:] + [right, first[0]]
    right, first[0] = call(
        order_kernel,
        [packed, first[0].shape],
        operands,
        1,
        in_specs=[ANY] * len(operands),
        out_specs=[ANY] * 2,
        input_output_aliases={len(operands) - 2: 0, len(operands) - 1: 1},
    )
    (features,) = call(
        features_kernel,
        [(examples * R // 2, LANES)],
        [kept, received, right],
        12 * half * R * R,
        scratch=[pltpu.VMEM((half // 2 // LEN, LANES, LANES), jnp.float32)],
    )

    first = jnp.concatenate(first, 0)
    second = swapped(first)
    block = query_features.shape[0]
    sums = (dp, block, examples * LANES)
    flops = 2 * examples * dp * block * R * R
    (near,) = call(near_kernel, [sums], [features, query_features, beside, first], flops)
    (scores,) = call(
        scores_kernel,
        [(examples, dp * block)],
        [features, second, near],
        flops,
        scratch=[pltpu.VMEM(sums, jnp.float32)],
    )
    return scores


def solution(mesh):
    in_specs = (
        P(("groups", "dp"), "tensor"),
        P(("groups", "dp"), None),
        P("tensor", None),
        P(),
        P(("groups", "dp"), None),
    )
    out_specs = P(("groups", "dp", "tensor"), None)
    return jax.shard_map(local, mesh=mesh, in_specs=in_specs, out_specs=out_specs, check_vma=False)
```

```python
import math

import jax
import jax.numpy as jnp
from jax import lax
from jax.experimental import pallas as pl
from jax.experimental.pallas import tpu as pltpu
from jax.sharding import PartitionSpec as P

R = 64
LEN = 128
LANES = 128
MIB = 1024 * 1024


def fetched(block, offsets):
    axes = ("dp", "tensor")
    dp, cores = (lax.axis_size(a) for a in axes)
    route = [((p ^ offsets[c]) * cores + c, p * cores + c) for p in range(dp) for c in range(cores)]
    return lax.ppermute(block, axes, route)


def swapped(block):
    return lax.ppermute(block, "tensor", [(0, 1), (1, 0)])


def times_transposed(a, b, **kwargs):
    return lax.dot_general(
        a, b, (((1,), (1,)), ((), ())), preferred_element_type=jnp.float32, **kwargs
    )


def ready_kernel(out_ref):
    out_ref[...] = jnp.zeros_like(out_ref)


def project_packed(start, x_ref, p_ref, out_ref):
    rows = out_ref.shape[0]
    for h in range(2):
        some = x_ref[pl.ds(pl.multiple_of(start + h * rows, rows), rows), :]
        out_ref[:, h * R : (h + 1) * R] = times_transposed(some, p_ref[...])


def sent_kernel(x_ref, p_ref, _, out_ref):
    start = (1 - lax.axis_index("tensor")) * 2 * out_ref.shape[0]
    project_packed(start, x_ref, p_ref, out_ref)


def kept_kernel(x_ref, p_ref, g_ref, q_ref, _, left_ref, right_ref):
    start = lax.axis_index("tensor") * 2 * left_ref.shape[0]
    project_packed(start, g_ref, q_ref, right_ref)
    project_packed(start, x_ref, p_ref, left_ref)


def order_kernel(*_):
    pass


def features_kernel(kept_ref, received_ref, right_ref, out_ref, square):
    packed = kept_ref.shape[0] // LEN
    for k in range(packed):
        rows = slice(k * LEN, (k + 1) * LEN)
        square[k] = lax.dot_general(
            kept_ref[rows, :] + received_ref[rows, :],
            right_ref[rows, :],
            (((0,), (0,)), ((), ())),
            precision=lax.Precision.HIGHEST,
            preferred_element_type=jnp.float32,
        )
        for h in range(2):
            e = h * packed + k
            even = square[k, pl.ds(h * R, R // 2, stride=2), :]
            odd = square[k, pl.ds(h * R + 1, R // 2, stride=2), :]
            lanes = slice(h * R, (h + 1) * R)
            out_ref[e * R // 2 : (e + 1) * R // 2, :] = jnp.concatenate(
                [even[:, lanes], odd[:, lanes]], 1
            )


def add_products(held, f_ref, sums):
    position = lax.axis_index("dp")
    block = sums.shape[1]
    examples = sums.shape[2] // LANES
    tiles = f_ref.shape[0] // examples
    sums[...] = jnp.zeros_like(sums)
    for group in range(0, len(held), 6):
        chosen = held[group : group + 6]
        totals = [[None] * examples for _ in chosen]
        for r in range(tiles):
            for i, (ref, row, offsets) in enumerate(chosen):
                q = ref[row : row + len(offsets) * block, r * LANES : (r + 1) * LANES]
                for e in range(examples):
                    term = q * f_ref[e * tiles + r : e * tiles + r + 1, :]
                    totals[i][e] = term if r == 0 else totals[i][e] + term
        for (ref, row, offsets), total in zip(chosen, totals):
            for j, offset in enumerate(offsets):
                for e in range(examples):
                    sums[position ^ offset, :, e * LANES : (e + 1) * LANES] = total[e][
                        j * block : (j + 1) * block, :
                    ]


def paired(ref, side, dp, block):
    pairs = list(range(dp - 2, 1, -2))
    return [
        (ref, k * block, [m + side for m in pairs[k : k + 2]]) for k in range(0, len(pairs), 2)
    ]


def near_kernel(f_ref, own_ref, beside_ref, first_ref, sums):
    dp, block, _ = sums.shape
    held = [(own_ref, 0, [0]), (beside_ref, 0, [1])]
    add_products(held + paired(first_ref, lax.axis_index("tensor"), dp, block), f_ref, sums)


def scores_kernel(f_ref, second_ref, near_ref, out_ref, sums):
    dp, block, width = sums.shape
    add_products(paired(second_ref, 1 - lax.axis_index("tensor"), dp, block), f_ref, sums)
    every = (sums[...] + near_ref[...]).reshape(dp * block, width)
    row = lax.broadcasted_iota(jnp.int32, (width // LANES, width), 0)
    lane = lax.broadcasted_iota(jnp.int32, (width // LANES, width), 1)
    own_lanes = jnp.where(lane // LANES == row, 1.0, 0.0).astype(jnp.float32)
    out_ref[...] = times_transposed(own_lanes, every, precision=lax.Precision.HIGHEST) / (
        R * math.sqrt(LEN)
    )


VMEM = pl.BlockSpec(memory_space=pltpu.VMEM)
ANY = pl.BlockSpec(memory_space=pl.ANY)


def call(kernel, shapes, operands, flops, scratch=(), in_specs=None, out_specs=None, limit=16, **kwargs):
    outs = [jax.ShapeDtypeStruct(s, jnp.float32) for s in shapes]
    moved = sum(math.prod(o.shape) * o.dtype.itemsize for o in list(operands) + outs)
    return pl.pallas_call(
        kernel,
        out_shape=outs,
        in_specs=in_specs or [VMEM] * len(operands),
        out_specs=out_specs or [VMEM] * len(outs),
        scratch_shapes=list(scratch),
        cost_estimate=pl.CostEstimate(flops=flops, bytes_accessed=moved, transcendentals=0),
        compiler_params=pltpu.CompilerParams(vmem_limit_bytes=limit * MIB),
        **kwargs,
    )(*operands)


def after(operands, arrays, flops):
    n = len(operands)
    return call(
        order_kernel,
        [a.shape for a in arrays],
        operands + arrays,
        flops,
        in_specs=[ANY] * (n + len(arrays)),
        out_specs=[ANY] * len(arrays),
        input_output_aliases={n + k: k for k in range(len(arrays))},
    )


def local(layer_input, out_grad, proj_in, proj_out, query_features):
    dp = lax.axis_size("dp")
    half = layer_input.shape[0] // lax.axis_size("tensor")
    examples = half // LEN
    packed = (half // 2, 2 * R)
    pairs = list(range(dp - 2, 1, -2))

    (ready,) = call(ready_kernel, [(8, LANES)], [], 5 * 10**9)

    beside = fetched(query_features, (1, 1))
    first = [fetched(query_features, (m, m + 1)) for m in pairs]

    p_in, p_out = proj_in.T, proj_out.T
    flops = 2 * half * R * layer_input.shape[1]
    (sent,) = call(
        sent_kernel, [packed], [layer_input, p_in, ready], flops, in_specs=[VMEM] * 2 + [ANY]
    )
    received = swapped(sent)
    kept, right = call(
        kept_kernel,
        [packed, packed],
        [layer_input, p_in, out_grad, p_out, sent],
        3 * flops,
        in_specs=[VMEM] * 4 + [ANY],
    )
    right, first[-1] = after([beside] + first[:-1][::-1], [right, first[-1]], 1)
    (right,) = after([received], [right], 10**9)
    (features,) = call(
        features_kernel,
        [(examples * R // 2, LANES)],
        [kept, received, right],
        12 * half * R * R,
        scratch=[pltpu.VMEM((half // 2 // LEN, LANES, LANES), jnp.float32)],
    )

    first = jnp.concatenate(first, 0)
    second = swapped(first)
    block = query_features.shape[0]
    sums = (dp, block, examples * LANES)
    flops = 2 * examples * dp * block * R * R
    (near,) = call(near_kernel, [sums], [features, query_features, beside, first], flops)
    (scores,) = call(
        scores_kernel,
        [(examples, dp * block)],
        [features, second, near],
        flops,
        scratch=[pltpu.VMEM(sums, jnp.float32)],
    )
    return scores


def solution(mesh):
    in_specs = (
        P(("groups", "dp"), "tensor"),
        P(("groups", "dp"), None),
        P("tensor", None),
        P(),
        P(("groups", "dp"), None),
    )
    out_specs = P(("groups", "dp", "tensor"), None)
    return jax.shard_map(local, mesh=mesh, in_specs=in_specs, out_specs=out_specs, check_vma=False)
```

```python
import math

import jax
import jax.numpy as jnp
from jax import lax
from jax.experimental import pallas as pl
from jax.experimental.pallas import tpu as pltpu
from jax.sharding import PartitionSpec as P

R = 64
LEN = 128
LANES = 128
MIB = 1024 * 1024


def fetched(block, offsets):
    axes = ("dp", "tensor")
    dp, cores = (lax.axis_size(a) for a in axes)
    route = [((p ^ offsets[c]) * cores + c, p * cores + c) for p in range(dp) for c in range(cores)]
    return lax.ppermute(block, axes, route)


def even_offsets(dp):
    evens = list(range(dp - 2, 1, -2))
    return evens[-1:] + evens[:-1]


def swapped(block):
    return lax.ppermute(block, "tensor", [(0, 1), (1, 0)])


def times_transposed(a, b, **kwargs):
    return lax.dot_general(
        a, b, (((1,), (1,)), ((), ())), preferred_element_type=jnp.float32, **kwargs
    )


def ready_kernel(out_ref):
    out_ref[...] = jnp.zeros_like(out_ref)


def project_packed(start, x_ref, p_ref, out_ref):
    rows = out_ref.shape[0]
    for h in range(2):
        some = x_ref[pl.ds(pl.multiple_of(start + h * rows, rows), rows), :]
        out_ref[:, h * R : (h + 1) * R] = times_transposed(some, p_ref[...])


def sent_kernel(x_ref, p_ref, _, out_ref):
    start = (1 - lax.axis_index("tensor")) * 2 * out_ref.shape[0]
    project_packed(start, x_ref, p_ref, out_ref)


def kept_kernel(x_ref, p_ref, g_ref, q_ref, _, left_ref, right_ref):
    start = lax.axis_index("tensor") * 2 * left_ref.shape[0]
    project_packed(start, g_ref, q_ref, right_ref)
    project_packed(start, x_ref, p_ref, left_ref)


def order_kernel(*_):
    pass


def features_kernel(kept_ref, received_ref, right_ref, out_ref, square):
    packed = kept_ref.shape[0] // LEN
    for k in range(packed):
        rows = slice(k * LEN, (k + 1) * LEN)
        square[k] = lax.dot_general(
            kept_ref[rows, :] + received_ref[rows, :],
            right_ref[rows, :],
            (((0,), (0,)), ((), ())),
            precision=lax.Precision.HIGHEST,
            preferred_element_type=jnp.float32,
        )
        for h in range(2):
            e = h * packed + k
            even = square[k, pl.ds(h * R, R // 2, stride=2), :]
            odd = square[k, pl.ds(h * R + 1, R // 2, stride=2), :]
            lanes = slice(h * R, (h + 1) * R)
            out_ref[e * R // 2 : (e + 1) * R // 2, :] = jnp.concatenate(
                [even[:, lanes], odd[:, lanes]], 1
            )


def add_products(held, f_ref, sums):
    position = lax.axis_index("dp")
    block = sums.shape[1]
    examples = sums.shape[2] // LANES
    tiles = f_ref.shape[0] // examples
    sums[...] = jnp.zeros_like(sums)
    for group in range(0, len(held), 6):
        chosen = held[group : group + 6]
        totals = [[None] * examples for _ in chosen]
        for r in range(tiles):
            for i, (ref, row, offsets) in enumerate(chosen):
                q = ref[row : row + len(offsets) * block, r * LANES : (r + 1) * LANES]
                for e in range(examples):
                    term = q * f_ref[e * tiles + r : e * tiles + r + 1, :]
                    totals[i][e] = term if r == 0 else totals[i][e] + term
        for (ref, row, offsets), total in zip(chosen, totals):
            for j, offset in enumerate(offsets):
                for e in range(examples):
                    sums[position ^ offset, :, e * LANES : (e + 1) * LANES] = total[e][
                        j * block : (j + 1) * block, :
                    ]


def paired(refs, side, dp, block):
    pairs, held = even_offsets(dp), []
    for ref in refs:
        for k in range(0, ref.shape[0] // block, 2):
            count = min(2, ref.shape[0] // block - k)
            here, pairs = pairs[:count], pairs[count:]
            held.append((ref, k * block, [m + side for m in here]))
    return held


def near_kernel(f_ref, own_ref, beside_ref, *refs):
    sums = refs[-1]
    dp, block, _ = sums.shape
    held = [(own_ref, 0, [0]), (beside_ref, 0, [1])]
    add_products(held + paired(refs[:-1], lax.axis_index("tensor"), dp, block), f_ref, sums)


def scores_kernel(f_ref, near_ref, *refs):
    out_ref, sums = refs[-2:]
    dp, block, width = sums.shape
    add_products(paired(refs[:-2], 1 - lax.axis_index("tensor"), dp, block), f_ref, sums)
    every = (sums[...] + near_ref[...]).reshape(dp * block, width)
    row = lax.broadcasted_iota(jnp.int32, (width // LANES, width), 0)
    lane = lax.broadcasted_iota(jnp.int32, (width // LANES, width), 1)
    own_lanes = jnp.where(lane // LANES == row, 1.0, 0.0).astype(jnp.float32)
    out_ref[...] = times_transposed(own_lanes, every, precision=lax.Precision.HIGHEST) / (
        R * math.sqrt(LEN)
    )


VMEM = pl.BlockSpec(memory_space=pltpu.VMEM)
ANY = pl.BlockSpec(memory_space=pl.ANY)


def call(kernel, shapes, operands, flops, scratch=(), in_specs=None, out_specs=None, limit=16, **kwargs):
    outs = [jax.ShapeDtypeStruct(s, jnp.float32) for s in shapes]
    moved = sum(math.prod(o.shape) * o.dtype.itemsize for o in list(operands) + outs)
    return pl.pallas_call(
        kernel,
        out_shape=outs,
        in_specs=in_specs or [VMEM] * len(operands),
        out_specs=out_specs or [VMEM] * len(outs),
        scratch_shapes=list(scratch),
        cost_estimate=pl.CostEstimate(flops=flops, bytes_accessed=moved, transcendentals=0),
        compiler_params=pltpu.CompilerParams(vmem_limit_bytes=limit * MIB),
        **kwargs,
    )(*operands)


def after(operands, arrays, flops):
    n = len(operands)
    return call(
        order_kernel,
        [a.shape for a in arrays],
        operands + arrays,
        flops,
        in_specs=[ANY] * (n + len(arrays)),
        out_specs=[ANY] * len(arrays),
        input_output_aliases={n + k: k for k in range(len(arrays))},
    )


def local(layer_input, out_grad, proj_in, proj_out, query_features):
    dp = lax.axis_size("dp")
    half = layer_input.shape[0] // lax.axis_size("tensor")
    examples = half // LEN
    packed = (half // 2, 2 * R)
    pairs = even_offsets(dp)

    (ready,) = call(ready_kernel, [(8, LANES)], [], 5 * 10**9)

    beside = fetched(query_features, (1, 1))
    first = [fetched(query_features, (m, m + 1)) for m in pairs]

    p_in, p_out = proj_in.T, proj_out.T
    flops = 2 * half * R * layer_input.shape[1]
    (sent,) = call(
        sent_kernel, [packed], [layer_input, p_in, ready], flops, in_specs=[VMEM] * 2 + [ANY]
    )
    received = swapped(sent)
    kept, right = call(
        kept_kernel,
        [packed, packed],
        [layer_input, p_in, out_grad, p_out, sent],
        3 * flops,
        in_specs=[VMEM] * 4 + [ANY],
    )
    early, late = first[:-1], first[-1]
    right, early[0] = after(early[1:], [right, early[0]], 1)
    right, late = after([early[0]], [right, late], 1)
    (right,) = after([beside, received], [right], 10**9)
    first = [jnp.concatenate(early, 0), late]
    (features,) = call(
        features_kernel,
        [(examples * R // 2, LANES)],
        [kept, received, right],
        12 * half * R * R,
        scratch=[pltpu.VMEM((half // 2 // LEN, LANES, LANES), jnp.float32)],
    )

    second = [swapped(b) for b in first]
    block = query_features.shape[0]
    sums = (dp, block, examples * LANES)
    flops = 2 * examples * dp * block * R * R
    (near,) = call(near_kernel, [sums], [features, query_features, beside] + first, flops)
    (scores,) = call(
        scores_kernel,
        [(examples, dp * block)],
        [features, near] + second,
        flops,
        scratch=[pltpu.VMEM(sums, jnp.float32)],
    )
    return scores


def solution(mesh):
    in_specs = (
        P(("groups", "dp"), "tensor"),
        P(("groups", "dp"), None),
        P("tensor", None),
        P(),
        P(("groups", "dp"), None),
    )
    out_specs = P(("groups", "dp", "tensor"), None)
    return jax.shard_map(local, mesh=mesh, in_specs=in_specs, out_specs=out_specs, check_vma=False)
```

```python
import math

import jax
import jax.numpy as jnp
from jax import lax
from jax.experimental import pallas as pl
from jax.experimental.pallas import tpu as pltpu
from jax.sharding import PartitionSpec as P

R = 64
LEN = 128
LANES = 128
MIB = 1024 * 1024


def fetched(block, offsets):
    axes = ("dp", "tensor")
    dp, cores = (lax.axis_size(a) for a in axes)
    route = [((p ^ offsets[c]) * cores + c, p * cores + c) for p in range(dp) for c in range(cores)]
    return lax.ppermute(block, axes, route)


def even_offsets(dp):
    evens = list(range(dp - 2, 1, -2))
    return evens[:1] + evens[:0:-1]


def swapped(block):
    return lax.ppermute(block, "tensor", [(0, 1), (1, 0)])


def times_transposed(a, b, **kwargs):
    return lax.dot_general(
        a, b, (((1,), (1,)), ((), ())), preferred_element_type=jnp.float32, **kwargs
    )


def ready_kernel(out_ref):
    out_ref[...] = jnp.zeros_like(out_ref)


def project_packed(start, x_ref, p_ref, out_ref):
    rows = out_ref.shape[0]
    for h in range(2):
        some = x_ref[pl.ds(pl.multiple_of(start + h * rows, rows), rows), :]
        out_ref[:, h * R : (h + 1) * R] = times_transposed(some, p_ref[...])


def sent_kernel(x_ref, p_ref, _, out_ref):
    start = (1 - lax.axis_index("tensor")) * 2 * out_ref.shape[0]
    project_packed(start, x_ref, p_ref, out_ref)


def kept_kernel(x_ref, p_ref, g_ref, q_ref, _, left_ref, right_ref):
    start = lax.axis_index("tensor") * 2 * left_ref.shape[0]
    project_packed(start, g_ref, q_ref, right_ref)
    project_packed(start, x_ref, p_ref, left_ref)


def order_kernel(*_):
    pass


def features_kernel(kept_ref, received_ref, right_ref, out_ref, square):
    packed = kept_ref.shape[0] // LEN
    for k in range(packed):
        rows = slice(k * LEN, (k + 1) * LEN)
        square[k] = lax.dot_general(
            kept_ref[rows, :] + received_ref[rows, :],
            right_ref[rows, :],
            (((0,), (0,)), ((), ())),
            precision=lax.Precision.HIGHEST,
            preferred_element_type=jnp.float32,
        )
        for h in range(2):
            e = h * packed + k
            even = square[k, pl.ds(h * R, R // 2, stride=2), :]
            odd = square[k, pl.ds(h * R + 1, R // 2, stride=2), :]
            lanes = slice(h * R, (h + 1) * R)
            out_ref[e * R // 2 : (e + 1) * R // 2, :] = jnp.concatenate(
                [even[:, lanes], odd[:, lanes]], 1
            )


def add_products(held, f_ref, sums):
    position = lax.axis_index("dp")
    block = sums.shape[1]
    examples = sums.shape[2] // LANES
    tiles = f_ref.shape[0] // examples
    sums[...] = jnp.zeros_like(sums)
    for group in range(0, len(held), 6):
        chosen = held[group : group + 6]
        totals = [[None] * examples for _ in chosen]
        for r in range(tiles):
            for i, (ref, row, offsets) in enumerate(chosen):
                q = ref[row : row + len(offsets) * block, r * LANES : (r + 1) * LANES]
                for e in range(examples):
                    term = q * f_ref[e * tiles + r : e * tiles + r + 1, :]
                    totals[i][e] = term if r == 0 else totals[i][e] + term
        for (ref, row, offsets), total in zip(chosen, totals):
            for j, offset in enumerate(offsets):
                for e in range(examples):
                    sums[position ^ offset, :, e * LANES : (e + 1) * LANES] = total[e][
                        j * block : (j + 1) * block, :
                    ]


def paired(refs, side, dp, block):
    pairs, held = even_offsets(dp), []
    for ref in refs:
        for k in range(0, ref.shape[0] // block, 2):
            count = min(2, ref.shape[0] // block - k)
            here, pairs = pairs[:count], pairs[count:]
            held.append((ref, k * block, [m + side for m in here]))
    return held


def near_kernel(f_ref, own_ref, beside_ref, *refs):
    sums = refs[-1]
    dp, block, _ = sums.shape
    held = [(own_ref, 0, [0]), (beside_ref, 0, [1])]
    add_products(held + paired(refs[:-1], lax.axis_index("tensor"), dp, block), f_ref, sums)


def scores_kernel(f_ref, near_ref, *refs):
    out_ref, sums = refs[-2:]
    dp, block, width = sums.shape
    add_products(paired(refs[:-2], 1 - lax.axis_index("tensor"), dp, block), f_ref, sums)
    every = (sums[...] + near_ref[...]).reshape(dp * block, width)
    row = lax.broadcasted_iota(jnp.int32, (width // LANES, width), 0)
    lane = lax.broadcasted_iota(jnp.int32, (width // LANES, width), 1)
    own_lanes = jnp.where(lane // LANES == row, 1.0, 0.0).astype(jnp.float32)
    out_ref[...] = times_transposed(own_lanes, every, precision=lax.Precision.HIGHEST) / (
        R * math.sqrt(LEN)
    )


VMEM = pl.BlockSpec(memory_space=pltpu.VMEM)
ANY = pl.BlockSpec(memory_space=pl.ANY)


def call(kernel, shapes, operands, flops, scratch=(), in_specs=None, out_specs=None, limit=16, **kwargs):
    outs = [jax.ShapeDtypeStruct(s, jnp.float32) for s in shapes]
    moved = sum(math.prod(o.shape) * o.dtype.itemsize for o in list(operands) + outs)
    return pl.pallas_call(
        kernel,
        out_shape=outs,
        in_specs=in_specs or [VMEM] * len(operands),
        out_specs=out_specs or [VMEM] * len(outs),
        scratch_shapes=list(scratch),
        cost_estimate=pl.CostEstimate(flops=flops, bytes_accessed=moved, transcendentals=0),
        compiler_params=pltpu.CompilerParams(vmem_limit_bytes=limit * MIB),
        **kwargs,
    )(*operands)


def after(operands, arrays, flops):
    n = len(operands)
    return call(
        order_kernel,
        [a.shape for a in arrays],
        operands + arrays,
        flops,
        in_specs=[ANY] * (n + len(arrays)),
        out_specs=[ANY] * len(arrays),
        input_output_aliases={n + k: k for k in range(len(arrays))},
    )


def local(layer_input, out_grad, proj_in, proj_out, query_features):
    dp = lax.axis_size("dp")
    half = layer_input.shape[0] // lax.axis_size("tensor")
    examples = half // LEN
    packed = (half // 2, 2 * R)
    pairs = even_offsets(dp)

    (ready,) = call(ready_kernel, [(8, LANES)], [], 5 * 10**9)

    beside = fetched(query_features, (1, 1))
    first = [fetched(query_features, (m, m + 1)) for m in pairs]

    p_in, p_out = proj_in.T, proj_out.T
    flops = 2 * half * R * layer_input.shape[1]
    (sent,) = call(
        sent_kernel, [packed], [layer_input, p_in, ready], flops, in_specs=[VMEM] * 2 + [ANY]
    )
    received = swapped(sent)
    kept, right = call(
        kept_kernel,
        [packed, packed],
        [layer_input, p_in, out_grad, p_out, sent],
        3 * flops,
        in_specs=[VMEM] * 4 + [ANY],
    )
    early, late = first[:-1], first[-1]
    right, early[0] = after(early[1:], [right, early[0]], 1)
    right, late = after([early[0]], [right, late], 1)
    (right,) = after([beside, received], [right], 10**9)
    first = [jnp.concatenate(early, 0), late]
    (features,) = call(
        features_kernel,
        [(examples * R // 2, LANES)],
        [kept, received, right],
        12 * half * R * R,
        scratch=[pltpu.VMEM((half // 2 // LEN, LANES, LANES), jnp.float32)],
    )

    second = [swapped(b) for b in first]
    block = query_features.shape[0]
    sums = (dp, block, examples * LANES)
    flops = 2 * examples * dp * block * R * R
    (near,) = call(near_kernel, [sums], [features, query_features, beside] + first, flops)
    (scores,) = call(
        scores_kernel,
        [(examples, dp * block)],
        [features, near] + second,
        flops,
        scratch=[pltpu.VMEM(sums, jnp.float32)],
    )
    return scores


def solution(mesh):
    in_specs = (
        P(("groups", "dp"), "tensor"),
        P(("groups", "dp"), None),
        P("tensor", None),
        P(),
        P(("groups", "dp"), None),
    )
    out_specs = P(("groups", "dp", "tensor"), None)
    return jax.shard_map(local, mesh=mesh, in_specs=in_specs, out_specs=out_specs, check_vma=False)
```

```python
import math

import jax
import jax.numpy as jnp
from jax import lax
from jax.experimental import pallas as pl
from jax.experimental.pallas import tpu as pltpu
from jax.sharding import PartitionSpec as P

R = 64
LEN = 128
LANES = 128
MIB = 1024 * 1024


def fetched(block, offsets):
    axes = ("dp", "tensor")
    dp, cores = (lax.axis_size(a) for a in axes)
    route = [((p ^ offsets[c]) * cores + c, p * cores + c) for p in range(dp) for c in range(cores)]
    return lax.ppermute(block, axes, route)


def gathered_offsets(dp):
    far = list(range(dp - 2, 2, -2))
    far = [far[0::2], far[1::2]]
    return [far[0] + [2], far[1] + [3]], [[o ^ 1 for o in f] for f in far]


def swapped(block):
    return lax.ppermute(block, "tensor", [(0, 1), (1, 0)])


def times_transposed(a, b, **kwargs):
    return lax.dot_general(
        a, b, (((1,), (1,)), ((), ())), preferred_element_type=jnp.float32, **kwargs
    )


def ready_kernel(out_ref):
    out_ref[...] = jnp.zeros_like(out_ref)


def project_packed(start, x_ref, p_ref, out_ref):
    rows = out_ref.shape[0]
    for h in range(2):
        some = x_ref[pl.ds(pl.multiple_of(start + h * rows, rows), rows), :]
        out_ref[:, h * R : (h + 1) * R] = times_transposed(some, p_ref[...])


def sent_kernel(x_ref, p_ref, _, out_ref):
    start = (1 - lax.axis_index("tensor")) * 2 * out_ref.shape[0]
    project_packed(start, x_ref, p_ref, out_ref)


def kept_kernel(x_ref, p_ref, g_ref, q_ref, _, left_ref, right_ref):
    start = lax.axis_index("tensor") * 2 * left_ref.shape[0]
    project_packed(start, g_ref, q_ref, right_ref)
    project_packed(start, x_ref, p_ref, left_ref)


def order_kernel(*_):
    pass


def features_kernel(kept_ref, received_ref, right_ref, out_ref, square):
    packed = kept_ref.shape[0] // LEN
    for k in range(packed):
        rows = slice(k * LEN, (k + 1) * LEN)
        square[k] = lax.dot_general(
            kept_ref[rows, :] + received_ref[rows, :],
            right_ref[rows, :],
            (((0,), (0,)), ((), ())),
            precision=lax.Precision.HIGHEST,
            preferred_element_type=jnp.float32,
        )
        for h in range(2):
            e = h * packed + k
            even = square[k, pl.ds(h * R, R // 2, stride=2), :]
            odd = square[k, pl.ds(h * R + 1, R // 2, stride=2), :]
            lanes = slice(h * R, (h + 1) * R)
            out_ref[e * R // 2 : (e + 1) * R // 2, :] = jnp.concatenate(
                [even[:, lanes], odd[:, lanes]], 1
            )


def add_products(held, f_ref, sums):
    position = lax.axis_index("dp")
    block = sums.shape[1]
    examples = sums.shape[2] // LANES
    tiles = f_ref.shape[0] // examples
    sums[...] = jnp.zeros_like(sums)
    for group in range(0, len(held), 6):
        chosen = held[group : group + 6]
        totals = [[None] * examples for _ in chosen]
        for r in range(tiles):
            for i, (ref, row, offsets) in enumerate(chosen):
                q = ref[row : row + len(offsets) * block, r * LANES : (r + 1) * LANES]
                for e in range(examples):
                    term = q * f_ref[e * tiles + r : e * tiles + r + 1, :]
                    totals[i][e] = term if r == 0 else totals[i][e] + term
        for (ref, row, offsets), total in zip(chosen, totals):
            for j, offset in enumerate(offsets):
                for e in range(examples):
                    sums[position ^ offset, :, e * LANES : (e + 1) * LANES] = total[e][
                        j * block : (j + 1) * block, :
                    ]


def in_order(refs, core, shape):
    dp, block, _ = shape
    held = []
    for ref, offsets in zip(refs, gathered_offsets(dp)):
        offsets = [jnp.where(core == 0, a, b) for a, b in zip(*offsets)]
        held += [(ref, k * block, offsets[k : k + 2]) for k in range(0, len(offsets), 2)]
    return held


def near_kernel(f_ref, own_ref, beside_ref, *refs):
    sums = refs[-1]
    held = [(own_ref, 0, [0]), (beside_ref, 0, [1])]
    add_products(held + in_order(refs[:-1], lax.axis_index("tensor"), sums.shape), f_ref, sums)


def scores_kernel(f_ref, near_ref, *refs):
    out_ref, sums = refs[-2:]
    dp, block, width = sums.shape
    add_products(in_order(refs[:-2], 1 - lax.axis_index("tensor"), sums.shape), f_ref, sums)
    every = (sums[...] + near_ref[...]).reshape(dp * block, width)
    row = lax.broadcasted_iota(jnp.int32, (width // LANES, width), 0)
    lane = lax.broadcasted_iota(jnp.int32, (width // LANES, width), 1)
    own_lanes = jnp.where(lane // LANES == row, 1.0, 0.0).astype(jnp.float32)
    out_ref[...] = times_transposed(own_lanes, every, precision=lax.Precision.HIGHEST) / (
        R * math.sqrt(LEN)
    )


VMEM = pl.BlockSpec(memory_space=pltpu.VMEM)
ANY = pl.BlockSpec(memory_space=pl.ANY)


def call(kernel, shapes, operands, flops, scratch=(), in_specs=None, out_specs=None, limit=16, **kwargs):
    outs = [jax.ShapeDtypeStruct(s, jnp.float32) for s in shapes]
    moved = sum(math.prod(o.shape) * o.dtype.itemsize for o in list(operands) + outs)
    return pl.pallas_call(
        kernel,
        out_shape=outs,
        in_specs=in_specs or [VMEM] * len(operands),
        out_specs=out_specs or [VMEM] * len(outs),
        scratch_shapes=list(scratch),
        cost_estimate=pl.CostEstimate(flops=flops, bytes_accessed=moved, transcendentals=0),
        compiler_params=pltpu.CompilerParams(vmem_limit_bytes=limit * MIB),
        **kwargs,
    )(*operands)


def after(operands, arrays, flops):
    n = len(operands)
    return call(
        order_kernel,
        [a.shape for a in arrays],
        operands + arrays,
        flops,
        in_specs=[ANY] * (n + len(arrays)),
        out_specs=[ANY] * len(arrays),
        input_output_aliases={n + k: k for k in range(len(arrays))},
    )


def local(layer_input, out_grad, proj_in, proj_out, query_features):
    dp = lax.axis_size("dp")
    half = layer_input.shape[0] // lax.axis_size("tensor")
    examples = half // LEN
    packed = (half // 2, 2 * R)

    (ready,) = call(ready_kernel, [(8, LANES)], [], 5 * 10**9)

    direct = [fetched(query_features, o) for o in zip(*gathered_offsets(dp)[0])]
    beside = fetched(query_features, (1, 1))
    relayed = fetched(jnp.concatenate(direct[:-1], 0), (1, 1))

    p_in, p_out = proj_in.T, proj_out.T
    flops = 2 * half * R * layer_input.shape[1]
    (sent,) = call(
        sent_kernel, [packed], [layer_input, p_in, ready], flops, in_specs=[VMEM] * 2 + [ANY]
    )
    received = swapped(sent)
    kept, right = call(
        kept_kernel,
        [packed, packed],
        [layer_input, p_in, out_grad, p_out, sent],
        3 * flops,
        in_specs=[VMEM] * 4 + [ANY],
    )
    right, relayed = after([], [right, relayed], 1)
    (right,) = after([beside, received], [right], 10**9)
    first = [jnp.concatenate(direct, 0), relayed]
    (features,) = call(
        features_kernel,
        [(examples * R // 2, LANES)],
        [kept, received, right],
        12 * half * R * R,
        scratch=[pltpu.VMEM((half // 2 // LEN, LANES, LANES), jnp.float32)],
    )

    second = [swapped(b) for b in first]
    block = query_features.shape[0]
    sums = (dp, block, examples * LANES)
    flops = 2 * examples * dp * block * R * R
    (near,) = call(near_kernel, [sums], [features, query_features, beside] + first, flops)
    (scores,) = call(
        scores_kernel,
        [(examples, dp * block)],
        [features, near] + second,
        flops,
        scratch=[pltpu.VMEM(sums, jnp.float32)],
    )
    return scores


def solution(mesh):
    in_specs = (
        P(("groups", "dp"), "tensor"),
        P(("groups", "dp"), None),
        P("tensor", None),
        P(),
        P(("groups", "dp"), None),
    )
    out_specs = P(("groups", "dp", "tensor"), None)
    return jax.shard_map(local, mesh=mesh, in_specs=in_specs, out_specs=out_specs, check_vma=False)
```

```python
import math

import jax
import jax.numpy as jnp
from jax import lax
from jax.experimental import pallas as pl
from jax.experimental.pallas import tpu as pltpu
from jax.sharding import PartitionSpec as P

R = 64
LEN = 128
LANES = 128
MIB = 1024 * 1024


def fetched(block, offsets):
    axes = ("dp", "tensor")
    dp, cores = (lax.axis_size(a) for a in axes)
    route = [((p ^ offsets[c]) * cores + c, p * cores + c) for p in range(dp) for c in range(cores)]
    return lax.ppermute(block, axes, route)


def gathered_offsets(dp):
    far = list(range(dp - 2, 2, -2))
    far = [far[0::2], far[1::2]]
    return [far[0] + [2], far[1] + [3]], [[o ^ 1 for o in f] for f in far]


def swapped(block):
    return lax.ppermute(block, "tensor", [(0, 1), (1, 0)])


def times_transposed(a, b, **kwargs):
    return lax.dot_general(
        a, b, (((1,), (1,)), ((), ())), preferred_element_type=jnp.float32, **kwargs
    )


def ready_kernel(out_ref):
    out_ref[...] = jnp.zeros_like(out_ref)


def project_packed(start, x_ref, p_ref, out_ref):
    rows = out_ref.shape[0]
    for h in range(2):
        some = x_ref[pl.ds(pl.multiple_of(start + h * rows, rows), rows), :]
        out_ref[:, h * R : (h + 1) * R] = times_transposed(some, p_ref[...])


def left_kernel(x_ref, p_ref, block_ref, _, sent_ref, kept_ref, out_ref):
    core = lax.axis_index("tensor")
    rows = 2 * sent_ref.shape[0]
    project_packed((1 - core) * rows, x_ref, p_ref, sent_ref)
    project_packed(core * rows, x_ref, p_ref, kept_ref)
    out_ref[...] = block_ref[...]


def right_kernel(g_ref, q_ref, _, __, right_ref):
    project_packed(lax.axis_index("tensor") * 2 * right_ref.shape[0], g_ref, q_ref, right_ref)


def order_kernel(*_):
    pass


def features_kernel(kept_ref, received_ref, right_ref, out_ref, square):
    packed = kept_ref.shape[0] // LEN
    for k in range(packed):
        rows = slice(k * LEN, (k + 1) * LEN)
        square[k] = lax.dot_general(
            kept_ref[rows, :] + received_ref[rows, :],
            right_ref[rows, :],
            (((0,), (0,)), ((), ())),
            precision=lax.Precision.HIGHEST,
            preferred_element_type=jnp.float32,
        )
        for h in range(2):
            e = h * packed + k
            even = square[k, pl.ds(h * R, R // 2, stride=2), :]
            odd = square[k, pl.ds(h * R + 1, R // 2, stride=2), :]
            lanes = slice(h * R, (h + 1) * R)
            out_ref[e * R // 2 : (e + 1) * R // 2, :] = jnp.concatenate(
                [even[:, lanes], odd[:, lanes]], 1
            )


def add_products(held, f_ref, sums):
    position = lax.axis_index("dp")
    block = sums.shape[1]
    examples = sums.shape[2] // LANES
    tiles = f_ref.shape[0] // examples
    sums[...] = jnp.zeros_like(sums)
    for group in range(0, len(held), 6):
        chosen = held[group : group + 6]
        totals = [[None] * examples for _ in chosen]
        for r in range(tiles):
            for i, (ref, row, offsets) in enumerate(chosen):
                q = ref[row : row + len(offsets) * block, r * LANES : (r + 1) * LANES]
                for e in range(examples):
                    term = q * f_ref[e * tiles + r : e * tiles + r + 1, :]
                    totals[i][e] = term if r == 0 else totals[i][e] + term
        for (ref, row, offsets), total in zip(chosen, totals):
            for j, offset in enumerate(offsets):
                for e in range(examples):
                    sums[position ^ offset, :, e * LANES : (e + 1) * LANES] = total[e][
                        j * block : (j + 1) * block, :
                    ]


def in_order(refs, core, shape):
    dp, block, _ = shape
    held = []
    for ref, offsets in zip(refs, gathered_offsets(dp)):
        offsets = [jnp.where(core == 0, a, b) for a, b in zip(*offsets)]
        held += [(ref, k * block, offsets[k : k + 2]) for k in range(0, len(offsets), 2)]
    return held


def near_kernel(f_ref, own_ref, beside_ref, *refs):
    sums = refs[-1]
    held = [(own_ref, 0, [0]), (beside_ref, 0, [1])]
    add_products(held + in_order(refs[:-1], lax.axis_index("tensor"), sums.shape), f_ref, sums)


def scores_kernel(f_ref, near_ref, *refs):
    out_ref, sums = refs[-2:]
    dp, block, width = sums.shape
    add_products(in_order(refs[:-2], 1 - lax.axis_index("tensor"), sums.shape), f_ref, sums)
    every = (sums[...] + near_ref[...]).reshape(dp * block, width)
    row = lax.broadcasted_iota(jnp.int32, (width // LANES, width), 0)
    lane = lax.broadcasted_iota(jnp.int32, (width // LANES, width), 1)
    own_lanes = jnp.where(lane // LANES == row, 1.0, 0.0).astype(jnp.float32)
    out_ref[...] = times_transposed(own_lanes, every, precision=lax.Precision.HIGHEST) / (
        R * math.sqrt(LEN)
    )


VMEM = pl.BlockSpec(memory_space=pltpu.VMEM)
ANY = pl.BlockSpec(memory_space=pl.ANY)


def call(kernel, shapes, operands, flops, scratch=(), in_specs=None, out_specs=None, limit=16, **kwargs):
    outs = [jax.ShapeDtypeStruct(s, jnp.float32) for s in shapes]
    moved = sum(math.prod(o.shape) * o.dtype.itemsize for o in list(operands) + outs)
    return pl.pallas_call(
        kernel,
        out_shape=outs,
        in_specs=in_specs or [VMEM] * len(operands),
        out_specs=out_specs or [VMEM] * len(outs),
        scratch_shapes=list(scratch),
        cost_estimate=pl.CostEstimate(flops=flops, bytes_accessed=moved, transcendentals=0),
        compiler_params=pltpu.CompilerParams(vmem_limit_bytes=limit * MIB),
        **kwargs,
    )(*operands)


def after(operands, arrays, flops):
    n = len(operands)
    return call(
        order_kernel,
        [a.shape for a in arrays],
        operands + arrays,
        flops,
        in_specs=[ANY] * (n + len(arrays)),
        out_specs=[ANY] * len(arrays),
        input_output_aliases={n + k: k for k in range(len(arrays))},
    )


def local(layer_input, out_grad, proj_in, proj_out, query_features):
    dp = lax.axis_size("dp")
    half = layer_input.shape[0] // lax.axis_size("tensor")
    examples = half // LEN
    packed = (half // 2, 2 * R)

    (ready,) = call(ready_kernel, [(8, LANES)], [], 5 * 10**9)

    direct = [fetched(query_features, o) for o in zip(*gathered_offsets(dp)[0])]
    relayed = fetched(jnp.concatenate(direct[:-1], 0), (1, 1))

    p_in, p_out = proj_in.T, proj_out.T
    flops = 2 * half * R * layer_input.shape[1]
    sent, kept, queries = call(
        left_kernel,
        [packed, packed, query_features.shape],
        [layer_input, p_in, query_features, ready],
        2 * flops,
        in_specs=[VMEM] * 3 + [ANY],
    )
    beside = fetched(queries, (1, 1))
    received = swapped(sent)
    (right,) = call(
        right_kernel, [packed], [out_grad, p_out, sent, direct[0]], 2 * flops, in_specs=[VMEM] * 2 + [ANY] * 2
    )
    (direct[-1],) = after([right], [direct[-1]], 1)
    right, relayed = after([], [right, relayed], 1)
    (right,) = after([beside, received], [right], 10**9)
    first = [jnp.concatenate(direct, 0), relayed]
    (features,) = call(
        features_kernel,
        [(examples * R // 2, LANES)],
        [kept, received, right],
        12 * half * R * R,
        scratch=[pltpu.VMEM((half // 2 // LEN, LANES, LANES), jnp.float32)],
    )

    second = [swapped(b) for b in first]
    block = query_features.shape[0]
    sums = (dp, block, examples * LANES)
    flops = 2 * examples * dp * block * R * R
    (near,) = call(near_kernel, [sums], [features, queries, beside] + first, flops)
    (scores,) = call(
        scores_kernel,
        [(examples, dp * block)],
        [features, near] + second,
        flops,
        scratch=[pltpu.VMEM(sums, jnp.float32)],
    )
    return scores


def solution(mesh):
    in_specs = (
        P(("groups", "dp"), "tensor"),
        P(("groups", "dp"), None),
        P("tensor", None),
        P(),
        P(("groups", "dp"), None),
    )
    out_specs = P(("groups", "dp", "tensor"), None)
    return jax.shard_map(local, mesh=mesh, in_specs=in_specs, out_specs=out_specs, check_vma=False)
```

```python
import math

import jax
import jax.numpy as jnp
from jax import lax
from jax.experimental import pallas as pl
from jax.experimental.pallas import tpu as pltpu
from jax.sharding import PartitionSpec as P

R = 64
LEN = 128
LANES = 128
MIB = 1024 * 1024


def fetched(block, offsets):
    axes = ("dp", "tensor")
    dp, cores = (lax.axis_size(a) for a in axes)
    pairs = [(p, c) for p in range(dp) for c in range(cores) if offsets[c] is not None]
    route = [((p ^ offsets[c]) * cores + c, p * cores + c) for p, c in pairs]
    return lax.ppermute(block, axes, route)


def gathered_offsets(dp):
    far = list(range(dp - 2, 2, -2))
    near = [2, 1] + [None] * (len(far) - 2)
    relayed = [(o ^ 1, n ^ 1 if n == 2 else None) for o, n in zip(far, near)]
    return list(zip(far, near)), relayed


def swapped(block):
    return lax.ppermute(block, "tensor", [(0, 1), (1, 0)])


def times_transposed(a, b, **kwargs):
    return lax.dot_general(
        a, b, (((1,), (1,)), ((), ())), preferred_element_type=jnp.float32, **kwargs
    )


def ready_kernel(out_ref):
    out_ref[...] = jnp.zeros_like(out_ref)


def project_packed(start, x_ref, p_ref, out_ref):
    rows = out_ref.shape[0]
    for h in range(2):
        some = x_ref[pl.ds(pl.multiple_of(start + h * rows, rows), rows), :]
        out_ref[:, h * R : (h + 1) * R] = times_transposed(some, p_ref[...])


def left_kernel(x_ref, p_ref, _, sent_ref, kept_ref):
    core = lax.axis_index("tensor")
    rows = 2 * sent_ref.shape[0]
    project_packed((1 - core) * rows, x_ref, p_ref, sent_ref)
    project_packed(core * rows, x_ref, p_ref, kept_ref)


def right_kernel(g_ref, q_ref, *refs):
    right_ref = refs[-1]
    project_packed(lax.axis_index("tensor") * 2 * right_ref.shape[0], g_ref, q_ref, right_ref)


def order_kernel(*_):
    pass


def features_kernel(kept_ref, received_ref, right_ref, out_ref, square):
    packed = kept_ref.shape[0] // LEN
    for k in range(packed):
        rows = slice(k * LEN, (k + 1) * LEN)
        square[k] = lax.dot_general(
            kept_ref[rows, :] + received_ref[rows, :],
            right_ref[rows, :],
            (((0,), (0,)), ((), ())),
            precision=lax.Precision.HIGHEST,
            preferred_element_type=jnp.float32,
        )
        for h in range(2):
            e = h * packed + k
            even = square[k, pl.ds(h * R, R // 2, stride=2), :]
            odd = square[k, pl.ds(h * R + 1, R // 2, stride=2), :]
            lanes = slice(h * R, (h + 1) * R)
            out_ref[e * R // 2 : (e + 1) * R // 2, :] = jnp.concatenate(
                [even[:, lanes], odd[:, lanes]], 1
            )


def add_products(held, f_ref, sums):
    position = lax.axis_index("dp")
    block = sums.shape[1]
    examples = sums.shape[2] // LANES
    tiles = f_ref.shape[0] // examples
    sums[...] = jnp.zeros_like(sums)
    for group in range(0, len(held), 6):
        chosen = held[group : group + 6]
        totals = [[None] * examples for _ in chosen]
        for r in range(tiles):
            for i, (ref, row, offsets) in enumerate(chosen):
                q = ref[row : row + len(offsets) * block, r * LANES : (r + 1) * LANES]
                for e in range(examples):
                    term = q * f_ref[e * tiles + r : e * tiles + r + 1, :]
                    totals[i][e] = term if r == 0 else totals[i][e] + term
        for (ref, row, offsets), total in zip(chosen, totals):
            for j, offset in enumerate(offsets):
                for e in range(examples):
                    sums[position ^ offset, :, e * LANES : (e + 1) * LANES] = total[e][
                        j * block : (j + 1) * block, :
                    ]


def in_order(refs, core, shape):
    dp, block, _ = shape
    held = []
    for ref, offsets in zip(refs, gathered_offsets(dp)):
        offsets = [jnp.where(core == 0, a, a if b is None else b) for a, b in offsets]
        held += [(ref, k * block, offsets[k : k + 2]) for k in range(0, len(offsets), 2)]
    return held


def near_kernel(f_ref, own_ref, *refs):
    sums = refs[-1]
    held = [(own_ref, 0, [0])]
    add_products(held + in_order(refs[:-1], lax.axis_index("tensor"), sums.shape), f_ref, sums)


def scores_kernel(f_ref, near_ref, *refs):
    out_ref, sums = refs[-2:]
    dp, block, width = sums.shape
    add_products(in_order(refs[:-2], 1 - lax.axis_index("tensor"), sums.shape), f_ref, sums)
    every = (sums[...] + near_ref[...]).reshape(dp * block, width)
    row = lax.broadcasted_iota(jnp.int32, (width // LANES, width), 0)
    lane = lax.broadcasted_iota(jnp.int32, (width // LANES, width), 1)
    own_lanes = jnp.where(lane // LANES == row, 1.0, 0.0).astype(jnp.float32)
    out_ref[...] = times_transposed(own_lanes, every, precision=lax.Precision.HIGHEST) / (
        R * math.sqrt(LEN)
    )


VMEM = pl.BlockSpec(memory_space=pltpu.VMEM)
ANY = pl.BlockSpec(memory_space=pl.ANY)


def call(kernel, shapes, operands, flops, scratch=(), in_specs=None, out_specs=None, limit=16, **kwargs):
    outs = [jax.ShapeDtypeStruct(s, jnp.float32) for s in shapes]
    moved = sum(math.prod(o.shape) * o.dtype.itemsize for o in list(operands) + outs)
    return pl.pallas_call(
        kernel,
        out_shape=outs,
        in_specs=in_specs or [VMEM] * len(operands),
        out_specs=out_specs or [VMEM] * len(outs),
        scratch_shapes=list(scratch),
        cost_estimate=pl.CostEstimate(flops=flops, bytes_accessed=moved, transcendentals=0),
        compiler_params=pltpu.CompilerParams(vmem_limit_bytes=limit * MIB),
        **kwargs,
    )(*operands)


def after(operands, arrays, flops):
    n = len(operands)
    return call(
        order_kernel,
        [a.shape for a in arrays],
        operands + arrays,
        flops,
        in_specs=[ANY] * (n + len(arrays)),
        out_specs=[ANY] * len(arrays),
        input_output_aliases={n + k: k for k in range(len(arrays))},
    )


def local(layer_input, out_grad, proj_in, proj_out, query_features):
    dp = lax.axis_size("dp")
    half = layer_input.shape[0] // lax.axis_size("tensor")
    examples = half // LEN
    packed = (half // 2, 2 * R)

    (ready,) = call(ready_kernel, [(8, LANES)], [], 5 * 10**9)

    from_owner, from_partner = gathered_offsets(dp)
    direct = [fetched(query_features, o) for o in from_owner]
    relayed = [
        fetched(block, tuple(None if o is None else 1 for o in offsets))
        for block, offsets in zip(direct, from_partner)
    ]

    p_in, p_out = proj_in.T, proj_out.T
    flops = 2 * half * R * layer_input.shape[1]
    sent, kept = call(
        left_kernel, [packed] * 2, [layer_input, p_in, ready], 2 * flops, in_specs=[VMEM] * 2 + [ANY]
    )
    received = swapped(sent)
    (right,) = call(
        right_kernel,
        [packed],
        [out_grad, p_out, sent, direct[0]],
        2 * flops,
        in_specs=[VMEM] * 2 + [ANY] * 2,
    )
    right, relayed[0] = after([], [right, relayed[0]], 1)
    (right,) = after([received], [right], 10**9)
    first = [jnp.concatenate(direct, 0), jnp.concatenate(relayed, 0)]
    (features,) = call(
        features_kernel,
        [(examples * R // 2, LANES)],
        [kept, received, right],
        12 * half * R * R,
        scratch=[pltpu.VMEM((half // 2 // LEN, LANES, LANES), jnp.float32)],
    )

    second = [swapped(b) for b in first]
    block = query_features.shape[0]
    sums = (dp, block, examples * LANES)
    flops = 2 * examples * dp * block * R * R
    (near,) = call(near_kernel, [sums], [features, query_features] + first, flops)
    (scores,) = call(
        scores_kernel,
        [(examples, dp * block)],
        [features, near] + second,
        flops,
        scratch=[pltpu.VMEM(sums, jnp.float32)],
    )
    return scores


def solution(mesh):
    in_specs = (
        P(("groups", "dp"), "tensor"),
        P(("groups", "dp"), None),
        P("tensor", None),
        P(),
        P(("groups", "dp"), None),
    )
    out_specs = P(("groups", "dp", "tensor"), None)
    return jax.shard_map(local, mesh=mesh, in_specs=in_specs, out_specs=out_specs, check_vma=False)
```

```python
import math

import jax
import jax.numpy as jnp
from jax import lax
from jax.experimental import pallas as pl
from jax.experimental.pallas import tpu as pltpu
from jax.sharding import PartitionSpec as P

R = 64
LEN = 128
LANES = 128
MIB = 1024 * 1024


def owner(position, offset, side, dp):
    return (position + dp - offset) % dp ^ side


def fetched(block, sources):
    axes = ("dp", "tensor")
    dp, cores = (lax.axis_size(a) for a in axes)
    route = [
        (owner(p, *sources[c], dp) * cores + c, p * cores + c) for p in range(dp) for c in range(cores)
    ]
    return lax.ppermute(block, axes, route)


def even_offsets(dp):
    evens = list(range(2, dp, 2))
    return evens[-1:] + evens[:-1]


def swapped(block):
    return lax.ppermute(block, "tensor", [(0, 1), (1, 0)])


def times_transposed(a, b, **kwargs):
    return lax.dot_general(
        a, b, (((1,), (1,)), ((), ())), preferred_element_type=jnp.float32, **kwargs
    )


def ready_kernel(out_ref):
    out_ref[...] = jnp.zeros_like(out_ref)


def project_packed(start, x_ref, p_ref, out_ref):
    rows = out_ref.shape[0]
    for h in range(2):
        some = x_ref[pl.ds(pl.multiple_of(start + h * rows, rows), rows), :]
        out_ref[:, h * R : (h + 1) * R] = times_transposed(some, p_ref[...])


def sent_kernel(x_ref, p_ref, _, out_ref):
    start = (1 - lax.axis_index("tensor")) * 2 * out_ref.shape[0]
    project_packed(start, x_ref, p_ref, out_ref)


def kept_kernel(x_ref, p_ref, g_ref, q_ref, _, left_ref, right_ref):
    start = lax.axis_index("tensor") * 2 * left_ref.shape[0]
    project_packed(start, g_ref, q_ref, right_ref)
    project_packed(start, x_ref, p_ref, left_ref)


def order_kernel(*_):
    pass


def features_kernel(kept_ref, received_ref, right_ref, out_ref, square):
    packed = kept_ref.shape[0] // LEN
    for k in range(packed):
        rows = slice(k * LEN, (k + 1) * LEN)
        square[k] = lax.dot_general(
            kept_ref[rows, :] + received_ref[rows, :],
            right_ref[rows, :],
            (((0,), (0,)), ((), ())),
            precision=lax.Precision.HIGHEST,
            preferred_element_type=jnp.float32,
        )
        for h in range(2):
            e = h * packed + k
            even = square[k, pl.ds(h * R, R // 2, stride=2), :]
            odd = square[k, pl.ds(h * R + 1, R // 2, stride=2), :]
            lanes = slice(h * R, (h + 1) * R)
            out_ref[e * R // 2 : (e + 1) * R // 2, :] = jnp.concatenate(
                [even[:, lanes], odd[:, lanes]], 1
            )


def add_products(held, f_ref, sums):
    position = lax.axis_index("dp")
    block = sums.shape[1]
    examples = sums.shape[2] // LANES
    tiles = f_ref.shape[0] // examples
    sums[...] = jnp.zeros_like(sums)
    for group in range(0, len(held), 6):
        chosen = held[group : group + 6]
        totals = [[None] * examples for _ in chosen]
        for r in range(tiles):
            for i, (ref, row, offsets) in enumerate(chosen):
                q = ref[row : row + len(offsets) * block, r * LANES : (r + 1) * LANES]
                for e in range(examples):
                    term = q * f_ref[e * tiles + r : e * tiles + r + 1, :]
                    totals[i][e] = term if r == 0 else totals[i][e] + term
        for (ref, row, offsets), total in zip(chosen, totals):
            for j, source in enumerate(offsets):
                anchor = owner(position, *source, sums.shape[0])
                for e in range(examples):
                    sums[anchor, :, e * LANES : (e + 1) * LANES] = total[e][
                        j * block : (j + 1) * block, :
                    ]


def paired(refs, side, dp, block):
    pairs, held = even_offsets(dp), []
    for ref in refs:
        for k in range(0, ref.shape[0] // block, 2):
            count = min(2, ref.shape[0] // block - k)
            here, pairs = pairs[:count], pairs[count:]
            held.append((ref, k * block, [(m, side) for m in here]))
    return held


def near_kernel(f_ref, own_ref, beside_ref, *refs):
    sums = refs[-1]
    dp, block, _ = sums.shape
    held = [(own_ref, 0, [(0, 0)]), (beside_ref, 0, [(0, 1)])]
    add_products(held + paired(refs[:-1], lax.axis_index("tensor"), dp, block), f_ref, sums)


def scores_kernel(f_ref, near_ref, *refs):
    out_ref, sums = refs[-2:]
    dp, block, width = sums.shape
    add_products(paired(refs[:-2], 1 - lax.axis_index("tensor"), dp, block), f_ref, sums)
    every = (sums[...] + near_ref[...]).reshape(dp * block, width)
    row = lax.broadcasted_iota(jnp.int32, (width // LANES, width), 0)
    lane = lax.broadcasted_iota(jnp.int32, (width // LANES, width), 1)
    own_lanes = jnp.where(lane // LANES == row, 1.0, 0.0).astype(jnp.float32)
    out_ref[...] = times_transposed(own_lanes, every, precision=lax.Precision.HIGHEST) / (
        R * math.sqrt(LEN)
    )


VMEM = pl.BlockSpec(memory_space=pltpu.VMEM)
ANY = pl.BlockSpec(memory_space=pl.ANY)


def call(kernel, shapes, operands, flops, scratch=(), in_specs=None, out_specs=None, limit=16, **kwargs):
    outs = [jax.ShapeDtypeStruct(s, jnp.float32) for s in shapes]
    moved = sum(math.prod(o.shape) * o.dtype.itemsize for o in list(operands) + outs)
    return pl.pallas_call(
        kernel,
        out_shape=outs,
        in_specs=in_specs or [VMEM] * len(operands),
        out_specs=out_specs or [VMEM] * len(outs),
        scratch_shapes=list(scratch),
        cost_estimate=pl.CostEstimate(flops=flops, bytes_accessed=moved, transcendentals=0),
        compiler_params=pltpu.CompilerParams(vmem_limit_bytes=limit * MIB),
        **kwargs,
    )(*operands)


def after(operands, arrays, flops):
    n = len(operands)
    return call(
        order_kernel,
        [a.shape for a in arrays],
        operands + arrays,
        flops,
        in_specs=[ANY] * (n + len(arrays)),
        out_specs=[ANY] * len(arrays),
        input_output_aliases={n + k: k for k in range(len(arrays))},
    )


def local(layer_input, out_grad, proj_in, proj_out, query_features):
    dp = lax.axis_size("dp")
    half = layer_input.shape[0] // lax.axis_size("tensor")
    examples = half // LEN
    packed = (half // 2, 2 * R)
    pairs = even_offsets(dp)

    (ready,) = call(ready_kernel, [(8, LANES)], [], 5 * 10**9)

    beside = fetched(query_features, ((0, 1), (0, 1)))
    first = [fetched(query_features, ((m, 0), (m, 1))) for m in pairs]

    p_in, p_out = proj_in.T, proj_out.T
    flops = 2 * half * R * layer_input.shape[1]
    (sent,) = call(
        sent_kernel, [packed], [layer_input, p_in, ready], flops, in_specs=[VMEM] * 2 + [ANY]
    )
    received = swapped(sent)
    kept, right = call(
        kept_kernel,
        [packed, packed],
        [layer_input, p_in, out_grad, p_out, sent],
        3 * flops,
        in_specs=[VMEM] * 4 + [ANY],
    )
    early, late = first[:-1], first[-1]
    right, early[0] = after(early[1:], [right, early[0]], 1)
    right, late = after([early[0]], [right, late], 1)
    (right,) = after([beside, received], [right], 10**9)
    first = [jnp.concatenate(early, 0), late]
    (features,) = call(
        features_kernel,
        [(examples * R // 2, LANES)],
        [kept, received, right],
        12 * half * R * R,
        scratch=[pltpu.VMEM((half // 2 // LEN, LANES, LANES), jnp.float32)],
    )

    second = [swapped(b) for b in first]
    block = query_features.shape[0]
    sums = (dp, block, examples * LANES)
    flops = 2 * examples * dp * block * R * R
    (near,) = call(near_kernel, [sums], [features, query_features, beside] + first, flops)
    (scores,) = call(
        scores_kernel,
        [(examples, dp * block)],
        [features, near] + second,
        flops,
        scratch=[pltpu.VMEM(sums, jnp.float32)],
    )
    return scores


def solution(mesh):
    in_specs = (
        P(("groups", "dp"), "tensor"),
        P(("groups", "dp"), None),
        P("tensor", None),
        P(),
        P(("groups", "dp"), None),
    )
    out_specs = P(("groups", "dp", "tensor"), None)
    return jax.shard_map(local, mesh=mesh, in_specs=in_specs, out_specs=out_specs, check_vma=False)
```

```python
import math

import jax
import jax.numpy as jnp
from jax import lax
from jax.experimental import pallas as pl
from jax.experimental.pallas import tpu as pltpu
from jax.sharding import PartitionSpec as P

R = 64
LEN = 128
LANES = 128
MIB = 1024 * 1024


def owner(position, offset, side, dp):
    return (position + dp - offset) % dp ^ side


def fetched(block, sources):
    axes = ("dp", "tensor")
    dp, cores = (lax.axis_size(a) for a in axes)
    route = [
        (owner(p, *sources[c], dp) * cores + c, p * cores + c) for p in range(dp) for c in range(cores)
    ]
    return lax.ppermute(block, axes, route)


def even_offsets(dp):
    evens = list(range(2, dp, 2))
    return evens


def swapped(block):
    return lax.ppermute(block, "tensor", [(0, 1), (1, 0)])


def times_transposed(a, b, **kwargs):
    return lax.dot_general(
        a, b, (((1,), (1,)), ((), ())), preferred_element_type=jnp.float32, **kwargs
    )


def ready_kernel(out_ref):
    out_ref[...] = jnp.zeros_like(out_ref)


def project_packed(start, x_ref, p_ref, out_ref):
    rows = out_ref.shape[0]
    for h in range(2):
        some = x_ref[pl.ds(pl.multiple_of(start + h * rows, rows), rows), :]
        out_ref[:, h * R : (h + 1) * R] = times_transposed(some, p_ref[...])


def sent_kernel(x_ref, p_ref, _, out_ref):
    start = (1 - lax.axis_index("tensor")) * 2 * out_ref.shape[0]
    project_packed(start, x_ref, p_ref, out_ref)


def kept_kernel(x_ref, p_ref, g_ref, q_ref, _, left_ref, right_ref):
    start = lax.axis_index("tensor") * 2 * left_ref.shape[0]
    project_packed(start, g_ref, q_ref, right_ref)
    project_packed(start, x_ref, p_ref, left_ref)


def order_kernel(*_):
    pass


def features_kernel(kept_ref, received_ref, right_ref, out_ref, square):
    packed = kept_ref.shape[0] // LEN
    for k in range(packed):
        rows = slice(k * LEN, (k + 1) * LEN)
        square[k] = lax.dot_general(
            kept_ref[rows, :] + received_ref[rows, :],
            right_ref[rows, :],
            (((0,), (0,)), ((), ())),
            precision=lax.Precision.HIGHEST,
            preferred_element_type=jnp.float32,
        )
        for h in range(2):
            e = h * packed + k
            even = square[k, pl.ds(h * R, R // 2, stride=2), :]
            odd = square[k, pl.ds(h * R + 1, R // 2, stride=2), :]
            lanes = slice(h * R, (h + 1) * R)
            out_ref[e * R // 2 : (e + 1) * R // 2, :] = jnp.concatenate(
                [even[:, lanes], odd[:, lanes]], 1
            )


def add_products(held, f_ref, sums):
    position = lax.axis_index("dp")
    block = sums.shape[1]
    examples = sums.shape[2] // LANES
    tiles = f_ref.shape[0] // examples
    sums[...] = jnp.zeros_like(sums)
    for group in range(0, len(held), 6):
        chosen = held[group : group + 6]
        totals = [[None] * examples for _ in chosen]
        for r in range(tiles):
            for i, (ref, row, offsets) in enumerate(chosen):
                q = ref[row : row + len(offsets) * block, r * LANES : (r + 1) * LANES]
                for e in range(examples):
                    term = q * f_ref[e * tiles + r : e * tiles + r + 1, :]
                    totals[i][e] = term if r == 0 else totals[i][e] + term
        for (ref, row, offsets), total in zip(chosen, totals):
            for j, source in enumerate(offsets):
                anchor = owner(position, *source, sums.shape[0])
                for e in range(examples):
                    sums[anchor, :, e * LANES : (e + 1) * LANES] = total[e][
                        j * block : (j + 1) * block, :
                    ]


def paired(refs, side, dp, block):
    pairs, held = even_offsets(dp), []
    for ref in refs:
        for k in range(0, ref.shape[0] // block, 2):
            count = min(2, ref.shape[0] // block - k)
            here, pairs = pairs[:count], pairs[count:]
            held.append((ref, k * block, [(m, side) for m in here]))
    return held


def near_kernel(f_ref, own_ref, beside_ref, *refs):
    sums = refs[-1]
    dp, block, _ = sums.shape
    held = [(own_ref, 0, [(0, 0)]), (beside_ref, 0, [(0, 1)])]
    add_products(held + paired(refs[:-1], lax.axis_index("tensor"), dp, block), f_ref, sums)


def scores_kernel(f_ref, near_ref, *refs):
    out_ref, sums = refs[-2:]
    dp, block, width = sums.shape
    add_products(paired(refs[:-2], 1 - lax.axis_index("tensor"), dp, block), f_ref, sums)
    every = (sums[...] + near_ref[...]).reshape(dp * block, width)
    row = lax.broadcasted_iota(jnp.int32, (width // LANES, width), 0)
    lane = lax.broadcasted_iota(jnp.int32, (width // LANES, width), 1)
    own_lanes = jnp.where(lane // LANES == row, 1.0, 0.0).astype(jnp.float32)
    out_ref[...] = times_transposed(own_lanes, every, precision=lax.Precision.HIGHEST) / (
        R * math.sqrt(LEN)
    )


VMEM = pl.BlockSpec(memory_space=pltpu.VMEM)
ANY = pl.BlockSpec(memory_space=pl.ANY)


def call(kernel, shapes, operands, flops, scratch=(), in_specs=None, out_specs=None, limit=16, **kwargs):
    outs = [jax.ShapeDtypeStruct(s, jnp.float32) for s in shapes]
    moved = sum(math.prod(o.shape) * o.dtype.itemsize for o in list(operands) + outs)
    return pl.pallas_call(
        kernel,
        out_shape=outs,
        in_specs=in_specs or [VMEM] * len(operands),
        out_specs=out_specs or [VMEM] * len(outs),
        scratch_shapes=list(scratch),
        cost_estimate=pl.CostEstimate(flops=flops, bytes_accessed=moved, transcendentals=0),
        compiler_params=pltpu.CompilerParams(vmem_limit_bytes=limit * MIB),
        **kwargs,
    )(*operands)


def after(operands, arrays, flops):
    n = len(operands)
    return call(
        order_kernel,
        [a.shape for a in arrays],
        operands + arrays,
        flops,
        in_specs=[ANY] * (n + len(arrays)),
        out_specs=[ANY] * len(arrays),
        input_output_aliases={n + k: k for k in range(len(arrays))},
    )


def local(layer_input, out_grad, proj_in, proj_out, query_features):
    dp = lax.axis_size("dp")
    half = layer_input.shape[0] // lax.axis_size("tensor")
    examples = half // LEN
    packed = (half // 2, 2 * R)
    pairs = even_offsets(dp)

    (ready,) = call(ready_kernel, [(8, LANES)], [], 5 * 10**9)

    beside = fetched(query_features, ((0, 1), (0, 1)))
    first = [fetched(query_features, ((m, 0), (m, 1))) for m in pairs]

    p_in, p_out = proj_in.T, proj_out.T
    flops = 2 * half * R * layer_input.shape[1]
    (sent,) = call(
        sent_kernel, [packed], [layer_input, p_in, ready], flops, in_specs=[VMEM] * 2 + [ANY]
    )
    received = swapped(sent)
    kept, right = call(
        kept_kernel,
        [packed, packed],
        [layer_input, p_in, out_grad, p_out, sent],
        3 * flops,
        in_specs=[VMEM] * 4 + [ANY],
    )
    early, late = first[:-1], first[-1]
    right, early[0] = after(early[1:], [right, early[0]], 1)
    right, late = after([early[0]], [right, late], 1)
    (right,) = after([beside, received], [right], 10**9)
    first = [jnp.concatenate(early, 0), late]
    (features,) = call(
        features_kernel,
        [(examples * R // 2, LANES)],
        [kept, received, right],
        12 * half * R * R,
        scratch=[pltpu.VMEM((half // 2 // LEN, LANES, LANES), jnp.float32)],
    )

    second = [swapped(b) for b in first]
    block = query_features.shape[0]
    sums = (dp, block, examples * LANES)
    flops = 2 * examples * dp * block * R * R
    (near,) = call(near_kernel, [sums], [features, query_features, beside] + first, flops)
    (scores,) = call(
        scores_kernel,
        [(examples, dp * block)],
        [features, near] + second,
        flops,
        scratch=[pltpu.VMEM(sums, jnp.float32)],
    )
    return scores


def solution(mesh):
    in_specs = (
        P(("groups", "dp"), "tensor"),
        P(("groups", "dp"), None),
        P("tensor", None),
        P(),
        P(("groups", "dp"), None),
    )
    out_specs = P(("groups", "dp", "tensor"), None)
    return jax.shard_map(local, mesh=mesh, in_specs=in_specs, out_specs=out_specs, check_vma=False)
```

```python
import math

import jax
import jax.numpy as jnp
from jax import lax
from jax.experimental import pallas as pl
from jax.experimental.pallas import tpu as pltpu
from jax.sharding import PartitionSpec as P

R = 64
LEN = 128
LANES = 128
MIB = 1024 * 1024


def fetched(block, offsets):
    axes = ("dp", "tensor")
    dp, cores = (lax.axis_size(a) for a in axes)
    route = [((p ^ offsets[c]) * cores + c, p * cores + c) for p in range(dp) for c in range(cores)]
    return lax.ppermute(block, axes, route)


def gathered_offsets(dp):
    even = list(range(dp - 2, 1, -2))
    even = even[-1:] + even[:-1]
    odd = even[-1:] + even[1:-1] + even[:1]
    return [(e, o + 1) for e, o in zip(even, odd)]


def swapped(block):
    return lax.ppermute(block, "tensor", [(0, 1), (1, 0)])


def times_transposed(a, b, **kwargs):
    return lax.dot_general(
        a, b, (((1,), (1,)), ((), ())), preferred_element_type=jnp.float32, **kwargs
    )


def ready_kernel(out_ref):
    out_ref[...] = jnp.zeros_like(out_ref)


def project_packed(start, x_ref, p_ref, out_ref):
    rows = out_ref.shape[0]
    for h in range(2):
        some = x_ref[pl.ds(pl.multiple_of(start + h * rows, rows), rows), :]
        out_ref[:, h * R : (h + 1) * R] = times_transposed(some, p_ref[...])


def sent_kernel(x_ref, p_ref, _, out_ref):
    start = (1 - lax.axis_index("tensor")) * 2 * out_ref.shape[0]
    project_packed(start, x_ref, p_ref, out_ref)


def kept_kernel(x_ref, p_ref, g_ref, q_ref, _, left_ref, right_ref):
    start = lax.axis_index("tensor") * 2 * left_ref.shape[0]
    project_packed(start, g_ref, q_ref, right_ref)
    project_packed(start, x_ref, p_ref, left_ref)


def order_kernel(*_):
    pass


def features_kernel(kept_ref, received_ref, right_ref, out_ref, square):
    packed = kept_ref.shape[0] // LEN
    for k in range(packed):
        rows = slice(k * LEN, (k + 1) * LEN)
        square[k] = lax.dot_general(
            kept_ref[rows, :] + received_ref[rows, :],
            right_ref[rows, :],
            (((0,), (0,)), ((), ())),
            precision=lax.Precision.HIGHEST,
            preferred_element_type=jnp.float32,
        )
        for h in range(2):
            e = h * packed + k
            even = square[k, pl.ds(h * R, R // 2, stride=2), :]
            odd = square[k, pl.ds(h * R + 1, R // 2, stride=2), :]
            lanes = slice(h * R, (h + 1) * R)
            out_ref[e * R // 2 : (e + 1) * R // 2, :] = jnp.concatenate(
                [even[:, lanes], odd[:, lanes]], 1
            )


def add_products(held, f_ref, sums):
    position = lax.axis_index("dp")
    block = sums.shape[1]
    examples = sums.shape[2] // LANES
    tiles = f_ref.shape[0] // examples
    sums[...] = jnp.zeros_like(sums)
    for group in range(0, len(held), 6):
        chosen = held[group : group + 6]
        totals = [[None] * examples for _ in chosen]
        for r in range(tiles):
            for i, (ref, row, offsets) in enumerate(chosen):
                q = ref[row : row + len(offsets) * block, r * LANES : (r + 1) * LANES]
                for e in range(examples):
                    term = q * f_ref[e * tiles + r : e * tiles + r + 1, :]
                    totals[i][e] = term if r == 0 else totals[i][e] + term
        for (ref, row, offsets), total in zip(chosen, totals):
            for j, offset in enumerate(offsets):
                for e in range(examples):
                    sums[position ^ offset, :, e * LANES : (e + 1) * LANES] = total[e][
                        j * block : (j + 1) * block, :
                    ]


def in_order(refs, core, shape):
    dp, block, _ = shape
    offsets = [jnp.where(core == 0, a, b) for a, b in gathered_offsets(dp)]
    held = []
    for ref in refs:
        for row in range(0, ref.shape[0], 2 * block):
            count = min(2, (ref.shape[0] - row) // block)
            held.append((ref, row, offsets[:count]))
            offsets = offsets[count:]
    return held


def near_kernel(f_ref, own_ref, beside_ref, *refs):
    sums = refs[-1]
    held = [(own_ref, 0, [0]), (beside_ref, 0, [1])]
    add_products(held + in_order(refs[:-1], lax.axis_index("tensor"), sums.shape), f_ref, sums)


def scores_kernel(f_ref, near_ref, *refs):
    out_ref, sums = refs[-2:]
    dp, block, width = sums.shape
    add_products(in_order(refs[:-2], 1 - lax.axis_index("tensor"), sums.shape), f_ref, sums)
    every = (sums[...] + near_ref[...]).reshape(dp * block, width)
    row = lax.broadcasted_iota(jnp.int32, (width // LANES, width), 0)
    lane = lax.broadcasted_iota(jnp.int32, (width // LANES, width), 1)
    own_lanes = jnp.where(lane // LANES == row, 1.0, 0.0).astype(jnp.float32)
    out_ref[...] = times_transposed(own_lanes, every, precision=lax.Precision.HIGHEST) / (
        R * math.sqrt(LEN)
    )


VMEM = pl.BlockSpec(memory_space=pltpu.VMEM)
ANY = pl.BlockSpec(memory_space=pl.ANY)


def call(kernel, shapes, operands, flops, scratch=(), in_specs=None, out_specs=None, limit=16, **kwargs):
    outs = [jax.ShapeDtypeStruct(s, jnp.float32) for s in shapes]
    moved = sum(math.prod(o.shape) * o.dtype.itemsize for o in list(operands) + outs)
    return pl.pallas_call(
        kernel,
        out_shape=outs,
        in_specs=in_specs or [VMEM] * len(operands),
        out_specs=out_specs or [VMEM] * len(outs),
        scratch_shapes=list(scratch),
        cost_estimate=pl.CostEstimate(flops=flops, bytes_accessed=moved, transcendentals=0),
        compiler_params=pltpu.CompilerParams(vmem_limit_bytes=limit * MIB),
        **kwargs,
    )(*operands)


def after(operands, arrays, flops):
    n = len(operands)
    return call(
        order_kernel,
        [a.shape for a in arrays],
        operands + arrays,
        flops,
        in_specs=[ANY] * (n + len(arrays)),
        out_specs=[ANY] * len(arrays),
        input_output_aliases={n + k: k for k in range(len(arrays))},
    )


def local(layer_input, out_grad, proj_in, proj_out, query_features):
    dp = lax.axis_size("dp")
    half = layer_input.shape[0] // lax.axis_size("tensor")
    examples = half // LEN
    packed = (half // 2, 2 * R)

    (ready,) = call(ready_kernel, [(8, LANES)], [], 5 * 10**9)

    beside = fetched(query_features, (1, 1))
    first = [fetched(query_features, offsets) for offsets in gathered_offsets(dp)]

    p_in, p_out = proj_in.T, proj_out.T
    flops = 2 * half * R * layer_input.shape[1]
    (sent,) = call(
        sent_kernel, [packed], [layer_input, p_in, ready], flops, in_specs=[VMEM] * 2 + [ANY]
    )
    received = swapped(sent)
    kept, right = call(
        kept_kernel,
        [packed, packed],
        [layer_input, p_in, out_grad, p_out, sent],
        3 * flops,
        in_specs=[VMEM] * 4 + [ANY],
    )
    early, late = first[:-1], first[-1]
    right, early[0] = after(early[1:], [right, early[0]], 1)
    right, late = after([early[0]], [right, late], 1)
    (right,) = after([beside, received], [right], 10**9)
    first = [jnp.concatenate(early, 0), late]
    (features,) = call(
        features_kernel,
        [(examples * R // 2, LANES)],
        [kept, received, right],
        12 * half * R * R,
        scratch=[pltpu.VMEM((half // 2 // LEN, LANES, LANES), jnp.float32)],
    )

    second = [swapped(b) for b in first]
    block = query_features.shape[0]
    sums = (dp, block, examples * LANES)
    flops = 2 * examples * dp * block * R * R
    (near,) = call(near_kernel, [sums], [features, query_features, beside] + first, flops)
    (scores,) = call(
        scores_kernel,
        [(examples, dp * block)],
        [features, near] + second,
        flops,
        scratch=[pltpu.VMEM(sums, jnp.float32)],
    )
    return scores


def solution(mesh):
    in_specs = (
        P(("groups", "dp"), "tensor"),
        P(("groups", "dp"), None),
        P("tensor", None),
        P(),
        P(("groups", "dp"), None),
    )
    out_specs = P(("groups", "dp", "tensor"), None)
    return jax.shard_map(local, mesh=mesh, in_specs=in_specs, out_specs=out_specs, check_vma=False)
```

```python
import math

import jax
import jax.numpy as jnp
from jax import lax
from jax.experimental import pallas as pl
from jax.experimental.pallas import tpu as pltpu
from jax.sharding import PartitionSpec as P

R = 64
LEN = 128
LANES = 128
MIB = 1024 * 1024


def fetched(block, offsets):
    axes = ("dp", "tensor")
    dp, cores = (lax.axis_size(a) for a in axes)
    route = [((p ^ offsets[c]) * cores + c, p * cores + c) for p in range(dp) for c in range(cores)]
    return lax.ppermute(block, axes, route)


def even_offsets(dp):
    evens = list(range(dp - 2, 1, -2))
    return evens[1:-1] + evens[:1] + evens[-1:]


def swapped(block):
    return lax.ppermute(block, "tensor", [(0, 1), (1, 0)])


def times_transposed(a, b, **kwargs):
    return lax.dot_general(
        a, b, (((1,), (1,)), ((), ())), preferred_element_type=jnp.float32, **kwargs
    )


def ready_kernel(out_ref):
    out_ref[...] = jnp.zeros_like(out_ref)


def project_packed(start, x_ref, p_ref, out_ref):
    rows = out_ref.shape[0]
    for h in range(2):
        some = x_ref[pl.ds(pl.multiple_of(start + h * rows, rows), rows), :]
        out_ref[:, h * R : (h + 1) * R] = times_transposed(some, p_ref[...])


def sent_kernel(x_ref, p_ref, _, out_ref):
    start = (1 - lax.axis_index("tensor")) * 2 * out_ref.shape[0]
    project_packed(start, x_ref, p_ref, out_ref)


def kept_kernel(x_ref, p_ref, g_ref, q_ref, _, left_ref, right_ref):
    start = lax.axis_index("tensor") * 2 * left_ref.shape[0]
    project_packed(start, g_ref, q_ref, right_ref)
    project_packed(start, x_ref, p_ref, left_ref)


def order_kernel(*_):
    pass


def features_kernel(kept_ref, received_ref, right_ref, out_ref, square):
    packed = kept_ref.shape[0] // LEN
    for k in range(packed):
        rows = slice(k * LEN, (k + 1) * LEN)
        square[k] = lax.dot_general(
            kept_ref[rows, :] + received_ref[rows, :],
            right_ref[rows, :],
            (((0,), (0,)), ((), ())),
            precision=lax.Precision.HIGHEST,
            preferred_element_type=jnp.float32,
        )
        for h in range(2):
            e = h * packed + k
            even = square[k, pl.ds(h * R, R // 2, stride=2), :]
            odd = square[k, pl.ds(h * R + 1, R // 2, stride=2), :]
            lanes = slice(h * R, (h + 1) * R)
            out_ref[e * R // 2 : (e + 1) * R // 2, :] = jnp.concatenate(
                [even[:, lanes], odd[:, lanes]], 1
            )


def add_products(held, f_ref, sums):
    position = lax.axis_index("dp")
    block = sums.shape[1]
    examples = sums.shape[2] // LANES
    tiles = f_ref.shape[0] // examples
    sums[...] = jnp.zeros_like(sums)
    for group in range(0, len(held), 6):
        chosen = held[group : group + 6]
        totals = [[None] * examples for _ in chosen]
        for r in range(tiles):
            for i, (ref, row, offsets) in enumerate(chosen):
                q = ref[row : row + len(offsets) * block, r * LANES : (r + 1) * LANES]
                for e in range(examples):
                    term = q * f_ref[e * tiles + r : e * tiles + r + 1, :]
                    totals[i][e] = term if r == 0 else totals[i][e] + term
        for (ref, row, offsets), total in zip(chosen, totals):
            for j, offset in enumerate(offsets):
                for e in range(examples):
                    sums[position ^ offset, :, e * LANES : (e + 1) * LANES] = total[e][
                        j * block : (j + 1) * block, :
                    ]


def paired(refs, side, dp, block):
    pairs, held = even_offsets(dp), []
    for ref in refs:
        for k in range(0, ref.shape[0] // block, 2):
            count = min(2, ref.shape[0] // block - k)
            here, pairs = pairs[:count], pairs[count:]
            held.append((ref, k * block, [m + side for m in here]))
    return held


def near_kernel(f_ref, own_ref, beside_ref, *refs):
    sums = refs[-1]
    dp, block, _ = sums.shape
    held = [(own_ref, 0, [0]), (beside_ref, 0, [1])]
    add_products(held + paired(refs[:-1], lax.axis_index("tensor"), dp, block), f_ref, sums)


def scores_kernel(f_ref, near_ref, *refs):
    out_ref, sums = refs[-2:]
    dp, block, width = sums.shape
    add_products(paired(refs[:-2], 1 - lax.axis_index("tensor"), dp, block), f_ref, sums)
    every = (sums[...] + near_ref[...]).reshape(dp * block, width)
    row = lax.broadcasted_iota(jnp.int32, (width // LANES, width), 0)
    lane = lax.broadcasted_iota(jnp.int32, (width // LANES, width), 1)
    own_lanes = jnp.where(lane // LANES == row, 1.0, 0.0).astype(jnp.float32)
    out_ref[...] = times_transposed(own_lanes, every, precision=lax.Precision.HIGHEST) / (
        R * math.sqrt(LEN)
    )


VMEM = pl.BlockSpec(memory_space=pltpu.VMEM)
ANY = pl.BlockSpec(memory_space=pl.ANY)


def call(kernel, shapes, operands, flops, scratch=(), in_specs=None, out_specs=None, limit=16, **kwargs):
    outs = [jax.ShapeDtypeStruct(s, jnp.float32) for s in shapes]
    moved = sum(math.prod(o.shape) * o.dtype.itemsize for o in list(operands) + outs)
    return pl.pallas_call(
        kernel,
        out_shape=outs,
        in_specs=in_specs or [VMEM] * len(operands),
        out_specs=out_specs or [VMEM] * len(outs),
        scratch_shapes=list(scratch),
        cost_estimate=pl.CostEstimate(flops=flops, bytes_accessed=moved, transcendentals=0),
        compiler_params=pltpu.CompilerParams(vmem_limit_bytes=limit * MIB),
        **kwargs,
    )(*operands)


def after(operands, arrays, flops):
    n = len(operands)
    return call(
        order_kernel,
        [a.shape for a in arrays],
        operands + arrays,
        flops,
        in_specs=[ANY] * (n + len(arrays)),
        out_specs=[ANY] * len(arrays),
        input_output_aliases={n + k: k for k in range(len(arrays))},
    )


def local(layer_input, out_grad, proj_in, proj_out, query_features):
    dp = lax.axis_size("dp")
    half = layer_input.shape[0] // lax.axis_size("tensor")
    examples = half // LEN
    packed = (half // 2, 2 * R)
    pairs = even_offsets(dp)

    (ready,) = call(ready_kernel, [(8, LANES)], [], 5 * 10**9)

    beside = fetched(query_features, (1, 1))
    first = [fetched(query_features, (m, m + 1)) for m in pairs]

    p_in, p_out = proj_in.T, proj_out.T
    flops = 2 * half * R * layer_input.shape[1]
    (sent,) = call(
        sent_kernel, [packed], [layer_input, p_in, ready], flops, in_specs=[VMEM] * 2 + [ANY]
    )
    received = swapped(sent)
    kept, right = call(
        kept_kernel,
        [packed, packed],
        [layer_input, p_in, out_grad, p_out, sent],
        3 * flops,
        in_specs=[VMEM] * 4 + [ANY],
    )
    early, late = first[:-1], first[-1]
    right, early[0] = after(early[1:], [right, early[0]], 1)
    right, late = after([early[0]], [right, late], 1)
    (right,) = after([beside, received], [right], 10**9)
    first = [jnp.concatenate(early, 0), late]
    (features,) = call(
        features_kernel,
        [(examples * R // 2, LANES)],
        [kept, received, right],
        12 * half * R * R,
        scratch=[pltpu.VMEM((half // 2 // LEN, LANES, LANES), jnp.float32)],
    )

    second = [swapped(b) for b in first]
    block = query_features.shape[0]
    sums = (dp, block, examples * LANES)
    flops = 2 * examples * dp * block * R * R
    (near,) = call(near_kernel, [sums], [features, query_features, beside] + first, flops)
    (scores,) = call(
        scores_kernel,
        [(examples, dp * block)],
        [features, near] + second,
        flops,
        scratch=[pltpu.VMEM(sums, jnp.float32)],
    )
    return scores


def solution(mesh):
    in_specs = (
        P(("groups", "dp"), "tensor"),
        P(("groups", "dp"), None),
        P("tensor", None),
        P(),
        P(("groups", "dp"), None),
    )
    out_specs = P(("groups", "dp", "tensor"), None)
    return jax.shard_map(local, mesh=mesh, in_specs=in_specs, out_specs=out_specs, check_vma=False)
```

```python
import math

import jax
import jax.numpy as jnp
from jax import lax
from jax.experimental import pallas as pl
from jax.experimental.pallas import tpu as pltpu
from jax.sharding import PartitionSpec as P

R = 64
LEN = 128
LANES = 128
MIB = 1024 * 1024


def fetched(block, offsets):
    axes = ("dp", "tensor")
    dp, cores = (lax.axis_size(a) for a in axes)
    route = [((p ^ offsets[c]) * cores + c, p * cores + c) for p in range(dp) for c in range(cores)]
    return lax.ppermute(block, axes, route)


def even_offsets(dp):
    evens = list(range(dp - 2, 1, -2))
    return evens[-1:] + evens[:-1]


def swapped(block):
    return lax.ppermute(block, "tensor", [(0, 1), (1, 0)])


def times_transposed(a, b, **kwargs):
    return lax.dot_general(
        a, b, (((1,), (1,)), ((), ())), preferred_element_type=jnp.float32, **kwargs
    )


def ready_kernel(out_ref):
    out_ref[...] = jnp.zeros_like(out_ref)


def project_packed(start, x_ref, p_ref, out_ref):
    rows = out_ref.shape[0]
    for h in range(2):
        some = x_ref[pl.ds(pl.multiple_of(start + h * rows, rows), rows), :]
        out_ref[:, h * R : (h + 1) * R] = times_transposed(some, p_ref[...])


def sent_kernel(x_ref, p_ref, _, out_ref):
    start = (1 - lax.axis_index("tensor")) * 2 * out_ref.shape[0]
    project_packed(start, x_ref, p_ref, out_ref)


def kept_kernel(x_ref, p_ref, g_ref, q_ref, _, left_ref, right_ref):
    start = lax.axis_index("tensor") * 2 * left_ref.shape[0]
    project_packed(start, g_ref, q_ref, right_ref)
    project_packed(start, x_ref, p_ref, left_ref)


def order_kernel(*_):
    pass


def features_kernel(kept_ref, received_ref, right_ref, out_ref, square):
    packed = kept_ref.shape[0] // LEN
    for k in range(packed):
        rows = slice(k * LEN, (k + 1) * LEN)
        square[k] = lax.dot_general(
            kept_ref[rows, :] + received_ref[rows, :],
            right_ref[rows, :],
            (((0,), (0,)), ((), ())),
            precision=lax.Precision.HIGHEST,
            preferred_element_type=jnp.float32,
        )
        for h in range(2):
            e = h * packed + k
            even = square[k, pl.ds(h * R, R // 2, stride=2), :]
            odd = square[k, pl.ds(h * R + 1, R // 2, stride=2), :]
            lanes = slice(h * R, (h + 1) * R)
            out_ref[e * R // 2 : (e + 1) * R // 2, :] = jnp.concatenate(
                [even[:, lanes], odd[:, lanes]], 1
            )


def add_products(held, f_ref, sums):
    position = lax.axis_index("dp")
    block = sums.shape[1]
    examples = sums.shape[2] // LANES
    tiles = f_ref.shape[0] // examples
    sums[...] = jnp.zeros_like(sums)
    for group in range(0, len(held), 6):
        chosen = held[group : group + 6]
        totals = [[None] * examples for _ in chosen]
        for r in range(tiles):
            for i, (ref, row, offsets) in enumerate(chosen):
                q = ref[row : row + len(offsets) * block, r * LANES : (r + 1) * LANES]
                for e in range(examples):
                    term = q * f_ref[e * tiles + r : e * tiles + r + 1, :]
                    totals[i][e] = term if r == 0 else totals[i][e] + term
        for (ref, row, offsets), total in zip(chosen, totals):
            for j, offset in enumerate(offsets):
                for e in range(examples):
                    sums[position ^ offset, :, e * LANES : (e + 1) * LANES] = total[e][
                        j * block : (j + 1) * block, :
                    ]


def paired(refs, side, dp, block):
    pairs, held = even_offsets(dp), []
    for ref in refs:
        for k in range(0, ref.shape[0] // block, 2):
            count = min(2, ref.shape[0] // block - k)
            here, pairs = pairs[:count], pairs[count:]
            held.append((ref, k * block, [m + side for m in here]))
    return held


def near_kernel(f_ref, own_ref, beside_ref, *refs):
    sums = refs[-1]
    dp, block, _ = sums.shape
    held = [(own_ref, 0, [0]), (beside_ref, 0, [1])]
    add_products(held + paired(refs[:-1], lax.axis_index("tensor"), dp, block), f_ref, sums)


def scores_kernel(f_ref, near_ref, *refs):
    out_ref, sums = refs[-2:]
    dp, block, width = sums.shape
    add_products(paired(refs[:-2], 1 - lax.axis_index("tensor"), dp, block), f_ref, sums)
    every = (sums[...] + near_ref[...]).reshape(dp * block, width)
    row = lax.broadcasted_iota(jnp.int32, (width // LANES, width), 0)
    lane = lax.broadcasted_iota(jnp.int32, (width // LANES, width), 1)
    own_lanes = jnp.where(lane // LANES == row, 1.0, 0.0).astype(jnp.bfloat16)
    total = None
    for _ in range(3):
        part = every.astype(jnp.bfloat16)
        every = every - part.astype(jnp.float32)
        term = times_transposed(own_lanes, part)
        total = term if total is None else total + term
    out_ref[...] = total / (R * math.sqrt(LEN))


VMEM = pl.BlockSpec(memory_space=pltpu.VMEM)
ANY = pl.BlockSpec(memory_space=pl.ANY)


def call(kernel, shapes, operands, flops, scratch=(), in_specs=None, out_specs=None, limit=16, **kwargs):
    outs = [jax.ShapeDtypeStruct(s, jnp.float32) for s in shapes]
    moved = sum(math.prod(o.shape) * o.dtype.itemsize for o in list(operands) + outs)
    return pl.pallas_call(
        kernel,
        out_shape=outs,
        in_specs=in_specs or [VMEM] * len(operands),
        out_specs=out_specs or [VMEM] * len(outs),
        scratch_shapes=list(scratch),
        cost_estimate=pl.CostEstimate(flops=flops, bytes_accessed=moved, transcendentals=0),
        compiler_params=pltpu.CompilerParams(vmem_limit_bytes=limit * MIB),
        **kwargs,
    )(*operands)


def after(operands, arrays, flops):
    n = len(operands)
    return call(
        order_kernel,
        [a.shape for a in arrays],
        operands + arrays,
        flops,
        in_specs=[ANY] * (n + len(arrays)),
        out_specs=[ANY] * len(arrays),
        input_output_aliases={n + k: k for k in range(len(arrays))},
    )


def local(layer_input, out_grad, proj_in, proj_out, query_features):
    dp = lax.axis_size("dp")
    half = layer_input.shape[0] // lax.axis_size("tensor")
    examples = half // LEN
    packed = (half // 2, 2 * R)
    pairs = even_offsets(dp)

    (ready,) = call(ready_kernel, [(8, LANES)], [], 5 * 10**9)

    beside = fetched(query_features, (1, 1))
    first = [fetched(query_features, (m, m + 1)) for m in pairs]

    p_in, p_out = proj_in.T, proj_out.T
    flops = 2 * half * R * layer_input.shape[1]
    (sent,) = call(
        sent_kernel, [packed], [layer_input, p_in, ready], flops, in_specs=[VMEM] * 2 + [ANY]
    )
    received = swapped(sent)
    kept, right = call(
        kept_kernel,
        [packed, packed],
        [layer_input, p_in, out_grad, p_out, sent],
        3 * flops,
        in_specs=[VMEM] * 4 + [ANY],
    )
    early, late = first[:-1], first[-1]
    right, early[0] = after(early[1:], [right, early[0]], 1)
    right, late = after([early[0]], [right, late], 1)
    (right,) = after([beside, received], [right], 10**9)
    first = [jnp.concatenate(early, 0), late]
    (features,) = call(
        features_kernel,
        [(examples * R // 2, LANES)],
        [kept, received, right],
        12 * half * R * R,
        scratch=[pltpu.VMEM((half // 2 // LEN, LANES, LANES), jnp.float32)],
    )

    second = [swapped(b) for b in first]
    block = query_features.shape[0]
    sums = (dp, block, examples * LANES)
    flops = 2 * examples * dp * block * R * R
    (near,) = call(near_kernel, [sums], [features, query_features, beside] + first, flops)
    (scores,) = call(
        scores_kernel,
        [(examples, dp * block)],
        [features, near] + second,
        flops,
        scratch=[pltpu.VMEM(sums, jnp.float32)],
    )
    return scores


def solution(mesh):
    in_specs = (
        P(("groups", "dp"), "tensor"),
        P(("groups", "dp"), None),
        P("tensor", None),
        P(),
        P(("groups", "dp"), None),
    )
    out_specs = P(("groups", "dp", "tensor"), None)
    return jax.shard_map(local, mesh=mesh, in_specs=in_specs, out_specs=out_specs, check_vma=False)
```

```python
import math

import jax
import jax.numpy as jnp
from jax import lax
from jax.experimental import pallas as pl
from jax.experimental.pallas import tpu as pltpu
from jax.sharding import PartitionSpec as P

R = 64
LEN = 128
LANES = 128
MIB = 1024 * 1024


def fetched(block, sources):
    axes = ("dp", "tensor")
    dp, cores = (lax.axis_size(a) for a in axes)
    pairs = [(p, c, sources[c]) for p in range(dp) for c in range(cores) if sources[c]]
    return lax.ppermute(block, axes, [((p ^ s[0]) * cores + s[1], p * cores + c) for p, c, s in pairs])


def gathered_offsets(dp):
    even = list(range(dp - 2, 1, -2))
    return list(zip(even, [3] + [o + 1 for o in even[1:-1]] + [even[0] + 1]))


def swapped(block):
    return lax.ppermute(block, "tensor", [(0, 1), (1, 0)])


def times_transposed(a, b, **kwargs):
    return lax.dot_general(
        a, b, (((1,), (1,)), ((), ())), preferred_element_type=jnp.float32, **kwargs
    )


def ready_kernel(out_ref):
    out_ref[...] = jnp.zeros_like(out_ref)


def project_packed(start, x_ref, p_ref, out_ref):
    rows = out_ref.shape[0]
    for h in range(2):
        some = x_ref[pl.ds(pl.multiple_of(start + h * rows, rows), rows), :]
        out_ref[:, h * R : (h + 1) * R] = times_transposed(some, p_ref[...])


def sent_kernel(x_ref, p_ref, block_ref, _, out_ref, same_ref):
    start = (1 - lax.axis_index("tensor")) * 2 * out_ref.shape[0]
    project_packed(start, x_ref, p_ref, out_ref)
    same_ref[...] = block_ref[...]


def kept_kernel(x_ref, p_ref, g_ref, q_ref, _, __, left_ref, right_ref):
    start = lax.axis_index("tensor") * 2 * left_ref.shape[0]
    project_packed(start, g_ref, q_ref, right_ref)
    project_packed(start, x_ref, p_ref, left_ref)


def order_kernel(*_):
    pass


def features_kernel(kept_ref, received_ref, right_ref, out_ref, square):
    packed = kept_ref.shape[0] // LEN
    for k in range(packed):
        rows = slice(k * LEN, (k + 1) * LEN)
        square[k] = lax.dot_general(
            kept_ref[rows, :] + received_ref[rows, :],
            right_ref[rows, :],
            (((0,), (0,)), ((), ())),
            precision=lax.Precision.HIGHEST,
            preferred_element_type=jnp.float32,
        )
        for h in range(2):
            e = h * packed + k
            even = square[k, pl.ds(h * R, R // 2, stride=2), :]
            odd = square[k, pl.ds(h * R + 1, R // 2, stride=2), :]
            lanes = slice(h * R, (h + 1) * R)
            out_ref[e * R // 2 : (e + 1) * R // 2, :] = jnp.concatenate(
                [even[:, lanes], odd[:, lanes]], 1
            )


def add_products(held, f_ref, sums):
    position = lax.axis_index("dp")
    block = sums.shape[1]
    examples = sums.shape[2] // LANES
    tiles = f_ref.shape[0] // examples
    sums[...] = jnp.zeros_like(sums)
    for group in range(0, len(held), 6):
        chosen = held[group : group + 6]
        totals = [[None] * examples for _ in chosen]
        for r in range(tiles):
            for i, (ref, row, offsets) in enumerate(chosen):
                q = ref[row : row + len(offsets) * block, r * LANES : (r + 1) * LANES]
                for e in range(examples):
                    term = q * f_ref[e * tiles + r : e * tiles + r + 1, :]
                    totals[i][e] = term if r == 0 else totals[i][e] + term
        for (ref, row, offsets), total in zip(chosen, totals):
            for j, offset in enumerate(offsets):
                for e in range(examples):
                    sums[position ^ offset, :, e * LANES : (e + 1) * LANES] = total[e][
                        j * block : (j + 1) * block, :
                    ]


def in_order(refs, core, shape):
    dp, block, _ = shape
    offsets = [jnp.where(core == 0, a, b) for a, b in gathered_offsets(dp)]
    held = []
    for ref in refs:
        for row in range(0, ref.shape[0], 2 * block):
            count = min(2, (ref.shape[0] - row) // block)
            held.append((ref, row, offsets[:count]))
            offsets = offsets[count:]
    return held


def near_kernel(f_ref, own_ref, beside_ref, *refs):
    sums = refs[-1]
    held = [(own_ref, 0, [0]), (beside_ref, 0, [1])]
    add_products(held + in_order(refs[:-1], lax.axis_index("tensor"), sums.shape), f_ref, sums)


def scores_kernel(f_ref, near_ref, *refs):
    out_ref, sums = refs[-2:]
    dp, block, width = sums.shape
    add_products(in_order(refs[:-2], 1 - lax.axis_index("tensor"), sums.shape), f_ref, sums)
    every = (sums[...] + near_ref[...]).reshape(dp * block, width)
    row = lax.broadcasted_iota(jnp.int32, (width // LANES, width), 0)
    lane = lax.broadcasted_iota(jnp.int32, (width // LANES, width), 1)
    own_lanes = jnp.where(lane // LANES == row, 1.0, 0.0).astype(jnp.float32)
    out_ref[...] = times_transposed(own_lanes, every, precision=lax.Precision.HIGHEST) / (
        R * math.sqrt(LEN)
    )


VMEM = pl.BlockSpec(memory_space=pltpu.VMEM)
ANY = pl.BlockSpec(memory_space=pl.ANY)


def call(kernel, shapes, operands, flops, scratch=(), in_specs=None, out_specs=None, limit=16, **kwargs):
    outs = [jax.ShapeDtypeStruct(s, jnp.float32) for s in shapes]
    moved = sum(math.prod(o.shape) * o.dtype.itemsize for o in list(operands) + outs)
    return pl.pallas_call(
        kernel,
        out_shape=outs,
        in_specs=in_specs or [VMEM] * len(operands),
        out_specs=out_specs or [VMEM] * len(outs),
        scratch_shapes=list(scratch),
        cost_estimate=pl.CostEstimate(flops=flops, bytes_accessed=moved, transcendentals=0),
        compiler_params=pltpu.CompilerParams(vmem_limit_bytes=limit * MIB),
        **kwargs,
    )(*operands)


def after(operands, arrays, flops):
    n = len(operands)
    return call(
        order_kernel,
        [a.shape for a in arrays],
        operands + arrays,
        flops,
        in_specs=[ANY] * (n + len(arrays)),
        out_specs=[ANY] * len(arrays),
        input_output_aliases={n + k: k for k in range(len(arrays))},
    )


def local(layer_input, out_grad, proj_in, proj_out, query_features):
    dp = lax.axis_size("dp")
    half = layer_input.shape[0] // lax.axis_size("tensor")
    examples = half // LEN
    packed = (half // 2, 2 * R)

    (ready,) = call(ready_kernel, [(8, LANES)], [], 5 * 10**9)

    *direct, last = gathered_offsets(dp)
    direct = [fetched(query_features, ((a, 0), (b, 1))) for a, b in direct]
    near_one = fetched(query_features, ((last[0], 0), None))

    p_in, p_out = proj_in.T, proj_out.T
    flops = 2 * half * R * layer_input.shape[1]
    sent, queries = call(
        sent_kernel,
        [packed, query_features.shape],
        [layer_input, p_in, query_features, ready],
        flops,
        in_specs=[VMEM] * 3 + [ANY],
    )
    received = swapped(sent)
    (direct[0],) = after([sent], [direct[0]], 1)
    far_one = fetched(direct[0], (None, (1, 0)))
    beside = fetched(queries, ((1, 0), (1, 1)))
    kept, right = call(
        kept_kernel,
        [packed, packed],
        [layer_input, p_in, out_grad, p_out, sent, direct[0]],
        3 * flops,
        in_specs=[VMEM] * 4 + [ANY] * 2,
    )
    right, direct[1] = after([], [right, direct[1]], 1)
    (right,) = after([beside, received], [right], 10**9)
    first = [direct[0], jnp.concatenate(direct[1:] + [near_one + far_one], 0)]
    (features,) = call(
        features_kernel,
        [(examples * R // 2, LANES)],
        [kept, received, right],
        12 * half * R * R,
        scratch=[pltpu.VMEM((half // 2 // LEN, LANES, LANES), jnp.float32)],
    )

    second = [swapped(b) for b in first]
    block = query_features.shape[0]
    sums = (dp, block, examples * LANES)
    flops = 2 * examples * dp * block * R * R
    (near,) = call(near_kernel, [sums], [features, queries, beside] + first, flops)
    (scores,) = call(
        scores_kernel,
        [(examples, dp * block)],
        [features, near] + second,
        flops,
        scratch=[pltpu.VMEM(sums, jnp.float32)],
    )
    return scores


def solution(mesh):
    in_specs = (
        P(("groups", "dp"), "tensor"),
        P(("groups", "dp"), None),
        P("tensor", None),
        P(),
        P(("groups", "dp"), None),
    )
    out_specs = P(("groups", "dp", "tensor"), None)
    return jax.shard_map(local, mesh=mesh, in_specs=in_specs, out_specs=out_specs, check_vma=False)
```

```python
import math

import jax
import jax.numpy as jnp
from jax import lax
from jax.experimental import pallas as pl
from jax.experimental.pallas import tpu as pltpu
from jax.sharding import PartitionSpec as P

R = 64
LEN = 128
LANES = 128
MIB = 1024 * 1024


def owner(position, offset, side, dp):
    return (position + dp - offset) % dp ^ side


def fetched(block, sources):
    axes = ("dp", "tensor")
    dp, cores = (lax.axis_size(a) for a in axes)
    route = [
        (owner(p, *sources[c], dp) * cores + c, p * cores + c) for p in range(dp) for c in range(cores)
    ]
    return lax.ppermute(block, axes, route)


def even_offsets(dp):
    evens = list(range(2, dp, 2))
    return evens[1:2] + evens[:1] + evens[2:]


def swapped(block):
    return lax.ppermute(block, "tensor", [(0, 1), (1, 0)])


def times_transposed(a, b, **kwargs):
    return lax.dot_general(
        a, b, (((1,), (1,)), ((), ())), preferred_element_type=jnp.float32, **kwargs
    )


def ready_kernel(out_ref):
    out_ref[...] = jnp.zeros_like(out_ref)


def project_packed(start, x_ref, p_ref, out_ref):
    rows = out_ref.shape[0]
    for h in range(2):
        some = x_ref[pl.ds(pl.multiple_of(start + h * rows, rows), rows), :]
        out_ref[:, h * R : (h + 1) * R] = times_transposed(some, p_ref[...])


def sent_kernel(x_ref, p_ref, _, out_ref):
    start = (1 - lax.axis_index("tensor")) * 2 * out_ref.shape[0]
    project_packed(start, x_ref, p_ref, out_ref)


def kept_kernel(x_ref, p_ref, g_ref, q_ref, _, left_ref, right_ref):
    start = lax.axis_index("tensor") * 2 * left_ref.shape[0]
    project_packed(start, g_ref, q_ref, right_ref)
    project_packed(start, x_ref, p_ref, left_ref)


def order_kernel(*_):
    pass


def features_kernel(kept_ref, received_ref, right_ref, out_ref, square):
    packed = kept_ref.shape[0] // LEN
    for k in range(packed):
        rows = slice(k * LEN, (k + 1) * LEN)
        square[k] = lax.dot_general(
            kept_ref[rows, :] + received_ref[rows, :],
            right_ref[rows, :],
            (((0,), (0,)), ((), ())),
            precision=lax.Precision.HIGHEST,
            preferred_element_type=jnp.float32,
        )
        for h in range(2):
            e = h * packed + k
            even = square[k, pl.ds(h * R, R // 2, stride=2), :]
            odd = square[k, pl.ds(h * R + 1, R // 2, stride=2), :]
            lanes = slice(h * R, (h + 1) * R)
            out_ref[e * R // 2 : (e + 1) * R // 2, :] = jnp.concatenate(
                [even[:, lanes], odd[:, lanes]], 1
            )


def add_products(held, f_ref, sums):
    position = lax.axis_index("dp")
    block = sums.shape[1]
    examples = sums.shape[2] // LANES
    tiles = f_ref.shape[0] // examples
    sums[...] = jnp.zeros_like(sums)
    for group in range(0, len(held), 6):
        chosen = held[group : group + 6]
        totals = [[None] * examples for _ in chosen]
        for r in range(tiles):
            for i, (ref, row, offsets) in enumerate(chosen):
                q = ref[row : row + len(offsets) * block, r * LANES : (r + 1) * LANES]
                for e in range(examples):
                    term = q * f_ref[e * tiles + r : e * tiles + r + 1, :]
                    totals[i][e] = term if r == 0 else totals[i][e] + term
        for (ref, row, offsets), total in zip(chosen, totals):
            for j, source in enumerate(offsets):
                anchor = owner(position, *source, sums.shape[0])
                for e in range(examples):
                    sums[anchor, :, e * LANES : (e + 1) * LANES] = total[e][
                        j * block : (j + 1) * block, :
                    ]


def paired(refs, side, dp, block):
    pairs, held = even_offsets(dp), []
    for ref in refs:
        for k in range(0, ref.shape[0] // block, 2):
            count = min(2, ref.shape[0] // block - k)
            here, pairs = pairs[:count], pairs[count:]
            held.append((ref, k * block, [(m, side) for m in here]))
    return held


def near_kernel(f_ref, own_ref, beside_ref, *refs):
    sums = refs[-1]
    dp, block, _ = sums.shape
    held = [(own_ref, 0, [(0, 0)]), (beside_ref, 0, [(0, 1)])]
    add_products(held + paired(refs[:-1], lax.axis_index("tensor"), dp, block), f_ref, sums)


def scores_kernel(f_ref, near_ref, *refs):
    out_ref, sums = refs[-2:]
    dp, block, width = sums.shape
    add_products(paired(refs[:-2], 1 - lax.axis_index("tensor"), dp, block), f_ref, sums)
    every = (sums[...] + near_ref[...]).reshape(dp * block, width)
    row = lax.broadcasted_iota(jnp.int32, (width // LANES, width), 0)
    lane = lax.broadcasted_iota(jnp.int32, (width // LANES, width), 1)
    own_lanes = jnp.where(lane // LANES == row, 1.0, 0.0).astype(jnp.float32)
    out_ref[...] = times_transposed(own_lanes, every, precision=lax.Precision.HIGHEST) / (
        R * math.sqrt(LEN)
    )


VMEM = pl.BlockSpec(memory_space=pltpu.VMEM)
ANY = pl.BlockSpec(memory_space=pl.ANY)


def call(kernel, shapes, operands, flops, scratch=(), in_specs=None, out_specs=None, limit=16, **kwargs):
    outs = [jax.ShapeDtypeStruct(s, jnp.float32) for s in shapes]
    moved = sum(math.prod(o.shape) * o.dtype.itemsize for o in list(operands) + outs)
    return pl.pallas_call(
        kernel,
        out_shape=outs,
        in_specs=in_specs or [VMEM] * len(operands),
        out_specs=out_specs or [VMEM] * len(outs),
        scratch_shapes=list(scratch),
        cost_estimate=pl.CostEstimate(flops=flops, bytes_accessed=moved, transcendentals=0),
        compiler_params=pltpu.CompilerParams(vmem_limit_bytes=limit * MIB),
        **kwargs,
    )(*operands)


def after(operands, arrays, flops):
    n = len(operands)
    return call(
        order_kernel,
        [a.shape for a in arrays],
        operands + arrays,
        flops,
        in_specs=[ANY] * (n + len(arrays)),
        out_specs=[ANY] * len(arrays),
        input_output_aliases={n + k: k for k in range(len(arrays))},
    )


def local(layer_input, out_grad, proj_in, proj_out, query_features):
    dp = lax.axis_size("dp")
    half = layer_input.shape[0] // lax.axis_size("tensor")
    examples = half // LEN
    packed = (half // 2, 2 * R)
    pairs = even_offsets(dp)

    (ready,) = call(ready_kernel, [(8, LANES)], [], 5 * 10**9)

    beside = fetched(query_features, ((0, 1), (0, 1)))
    first = [fetched(query_features, ((m, 0), (m, 1))) for m in pairs]

    p_in, p_out = proj_in.T, proj_out.T
    flops = 2 * half * R * layer_input.shape[1]
    (sent,) = call(
        sent_kernel, [packed], [layer_input, p_in, ready], flops, in_specs=[VMEM] * 2 + [ANY]
    )
    received = swapped(sent)
    kept, right = call(
        kept_kernel,
        [packed, packed],
        [layer_input, p_in, out_grad, p_out, sent],
        3 * flops,
        in_specs=[VMEM] * 4 + [ANY],
    )
    early, late = first[:-1], first[-1]
    right, early[0] = after(early[1:], [right, early[0]], 1)
    right, late = after([early[0]], [right, late], 1)
    (right,) = after([beside, received], [right], 10**9)
    first = [jnp.concatenate(early, 0), late]
    (features,) = call(
        features_kernel,
        [(examples * R // 2, LANES)],
        [kept, received, right],
        12 * half * R * R,
        scratch=[pltpu.VMEM((half // 2 // LEN, LANES, LANES), jnp.float32)],
    )

    second = [swapped(b) for b in first]
    block = query_features.shape[0]
    sums = (dp, block, examples * LANES)
    flops = 2 * examples * dp * block * R * R
    (near,) = call(near_kernel, [sums], [features, query_features, beside] + first, flops)
    (scores,) = call(
        scores_kernel,
        [(examples, dp * block)],
        [features, near] + second,
        flops,
        scratch=[pltpu.VMEM(sums, jnp.float32)],
    )
    return scores


def solution(mesh):
    in_specs = (
        P(("groups", "dp"), "tensor"),
        P(("groups", "dp"), None),
        P("tensor", None),
        P(),
        P(("groups", "dp"), None),
    )
    out_specs = P(("groups", "dp", "tensor"), None)
    return jax.shard_map(local, mesh=mesh, in_specs=in_specs, out_specs=out_specs, check_vma=False)
```

```python
import math

import jax
import jax.numpy as jnp
from jax import lax
from jax.experimental import pallas as pl
from jax.experimental.pallas import tpu as pltpu
from jax.sharding import PartitionSpec as P

R = 64
LEN = 128
LANES = 128
MIB = 1024 * 1024


def fetched(block, offsets):
    axes = ("dp", "tensor")
    dp, cores = (lax.axis_size(a) for a in axes)
    route = [((p ^ offsets[c]) * cores + c, p * cores + c) for p in range(dp) for c in range(cores)]
    return lax.ppermute(block, axes, route)


def even_offsets(dp):
    evens = list(range(dp - 2, 1, -2))
    return evens[-1:] + evens[:-1]


def swapped(block):
    return lax.ppermute(block, "tensor", [(0, 1), (1, 0)])


def times_transposed(a, b, **kwargs):
    return lax.dot_general(
        a, b, (((1,), (1,)), ((), ())), preferred_element_type=jnp.float32, **kwargs
    )


def ready_kernel(out_ref):
    out_ref[...] = jnp.zeros_like(out_ref)


def project_packed(start, x_ref, p_ref, out_ref):
    rows = out_ref.shape[0]
    for h in range(2):
        some = x_ref[pl.ds(pl.multiple_of(start + h * rows, rows), rows), :]
        out_ref[:, h * R : (h + 1) * R] = times_transposed(some, p_ref[...])


def sent_kernel(x_ref, p_ref, _, out_ref):
    start = (1 - lax.axis_index("tensor")) * 2 * out_ref.shape[0]
    project_packed(start, x_ref, p_ref, out_ref)


def kept_kernel(x_ref, p_ref, g_ref, q_ref, _, left_ref, right_ref):
    start = lax.axis_index("tensor") * 2 * left_ref.shape[0]
    project_packed(start, g_ref, q_ref, right_ref)
    project_packed(start, x_ref, p_ref, left_ref)


def order_kernel(*_):
    pass


def features_kernel(kept_ref, received_ref, right_ref, out_ref, square):
    packed = kept_ref.shape[0] // LEN
    for k in range(packed):
        rows = slice(k * LEN, (k + 1) * LEN)
        square[k] = lax.dot_general(
            kept_ref[rows, :] + received_ref[rows, :],
            right_ref[rows, :],
            (((0,), (0,)), ((), ())),
            precision=lax.Precision.HIGHEST,
            preferred_element_type=jnp.float32,
        )
        for h in range(2):
            e = h * packed + k
            even = square[k, pl.ds(h * R, R // 2, stride=2), :]
            odd = square[k, pl.ds(h * R + 1, R // 2, stride=2), :]
            lanes = slice(h * R, (h + 1) * R)
            out_ref[e * R // 2 : (e + 1) * R // 2, :] = jnp.concatenate(
                [even[:, lanes], odd[:, lanes]], 1
            )


def add_products(held, f_ref, sums):
    position = lax.axis_index("dp")
    block = sums.shape[1]
    examples = sums.shape[2] // LANES
    tiles = f_ref.shape[0] // examples
    sums[...] = jnp.zeros_like(sums)
    for group in range(0, len(held), 6):
        chosen = held[group : group + 6]
        totals = [[None] * examples for _ in chosen]
        for r in range(tiles):
            for i, (ref, row, offsets) in enumerate(chosen):
                q = ref[row : row + len(offsets) * block, r * LANES : (r + 1) * LANES]
                for e in range(examples):
                    term = q * f_ref[e * tiles + r : e * tiles + r + 1, :]
                    totals[i][e] = term if r == 0 else totals[i][e] + term
        for (ref, row, offsets), total in zip(chosen, totals):
            for j, offset in enumerate(offsets):
                for e in range(examples):
                    sums[position ^ offset, :, e * LANES : (e + 1) * LANES] = total[e][
                        j * block : (j + 1) * block, :
                    ]


def paired(refs, side, dp, block):
    pairs, held = even_offsets(dp), []
    for ref in refs:
        for k in range(0, ref.shape[0] // block, 2):
            count = min(2, ref.shape[0] // block - k)
            here, pairs = pairs[:count], pairs[count:]
            held.append((ref, k * block, [m + side for m in here]))
    return held


def near_kernel(f_ref, own_ref, beside_ref, *refs):
    sums = refs[-1]
    dp, block, _ = sums.shape
    held = [(own_ref, 0, [0]), (beside_ref, 0, [1])]
    add_products(held + paired(refs[:-1], 1 - lax.axis_index("tensor"), dp, block), f_ref, sums)


def scores_kernel(f_ref, near_ref, *refs):
    out_ref, sums = refs[-2:]
    dp, block, width = sums.shape
    add_products(paired(refs[:-2], lax.axis_index("tensor"), dp, block), f_ref, sums)
    every = (sums[...] + near_ref[...]).reshape(dp * block, width)
    row = lax.broadcasted_iota(jnp.int32, (width // LANES, width), 0)
    lane = lax.broadcasted_iota(jnp.int32, (width // LANES, width), 1)
    own_lanes = jnp.where(lane // LANES == row, 1.0, 0.0).astype(jnp.float32)
    out_ref[...] = times_transposed(own_lanes, every, precision=lax.Precision.HIGHEST) / (
        R * math.sqrt(LEN)
    )


VMEM = pl.BlockSpec(memory_space=pltpu.VMEM)
ANY = pl.BlockSpec(memory_space=pl.ANY)


def call(kernel, shapes, operands, flops, scratch=(), in_specs=None, out_specs=None, limit=16, **kwargs):
    outs = [jax.ShapeDtypeStruct(s, jnp.float32) for s in shapes]
    moved = sum(math.prod(o.shape) * o.dtype.itemsize for o in list(operands) + outs)
    return pl.pallas_call(
        kernel,
        out_shape=outs,
        in_specs=in_specs or [VMEM] * len(operands),
        out_specs=out_specs or [VMEM] * len(outs),
        scratch_shapes=list(scratch),
        cost_estimate=pl.CostEstimate(flops=flops, bytes_accessed=moved, transcendentals=0),
        compiler_params=pltpu.CompilerParams(vmem_limit_bytes=limit * MIB),
        **kwargs,
    )(*operands)


def after(operands, arrays, flops):
    n = len(operands)
    return call(
        order_kernel,
        [a.shape for a in arrays],
        operands + arrays,
        flops,
        in_specs=[ANY] * (n + len(arrays)),
        out_specs=[ANY] * len(arrays),
        input_output_aliases={n + k: k for k in range(len(arrays))},
    )


def local(layer_input, out_grad, proj_in, proj_out, query_features):
    dp = lax.axis_size("dp")
    half = layer_input.shape[0] // lax.axis_size("tensor")
    examples = half // LEN
    packed = (half // 2, 2 * R)
    pairs = even_offsets(dp)

    (ready,) = call(ready_kernel, [(8, LANES)], [], 5 * 10**9)

    beside = fetched(query_features, (1, 1))
    first = [fetched(query_features, (m + 1, m)) for m in pairs]

    p_in, p_out = proj_in.T, proj_out.T
    flops = 2 * half * R * layer_input.shape[1]
    (sent,) = call(
        sent_kernel, [packed], [layer_input, p_in, ready], flops, in_specs=[VMEM] * 2 + [ANY]
    )
    received = swapped(sent)
    kept, right = call(
        kept_kernel,
        [packed, packed],
        [layer_input, p_in, out_grad, p_out, sent],
        3 * flops,
        in_specs=[VMEM] * 4 + [ANY],
    )
    early, late = first[:-1], first[-1]
    right, early[0] = after(early[1:], [right, early[0]], 1)
    right, late = after([early[0]], [right, late], 1)
    (right,) = after([beside, received], [right], 10**9)
    first = [jnp.concatenate(early, 0), late]
    (features,) = call(
        features_kernel,
        [(examples * R // 2, LANES)],
        [kept, received, right],
        12 * half * R * R,
        scratch=[pltpu.VMEM((half // 2 // LEN, LANES, LANES), jnp.float32)],
    )

    second = [swapped(b) for b in first]
    block = query_features.shape[0]
    sums = (dp, block, examples * LANES)
    flops = 2 * examples * dp * block * R * R
    (near,) = call(near_kernel, [sums], [features, query_features, beside] + first, flops)
    (scores,) = call(
        scores_kernel,
        [(examples, dp * block)],
        [features, near] + second,
        flops,
        scratch=[pltpu.VMEM(sums, jnp.float32)],
    )
    return scores


def solution(mesh):
    in_specs = (
        P(("groups", "dp"), "tensor"),
        P(("groups", "dp"), None),
        P("tensor", None),
        P(),
        P(("groups", "dp"), None),
    )
    out_specs = P(("groups", "dp", "tensor"), None)
    return jax.shard_map(local, mesh=mesh, in_specs=in_specs, out_specs=out_specs, check_vma=False)
```

```python
import math

import jax
import jax.numpy as jnp
from jax import lax
from jax.experimental import pallas as pl
from jax.experimental.pallas import tpu as pltpu
from jax.sharding import PartitionSpec as P

R = 64
LEN = 128
LANES = 128
MIB = 1024 * 1024


def fetched(block, offsets):
    axes = ("dp", "tensor")
    dp, cores = (lax.axis_size(a) for a in axes)
    route = [((p ^ offsets[c]) * cores + c, p * cores + c) for p in range(dp) for c in range(cores)]
    return lax.ppermute(block, axes, route)


def even_offsets(dp):
    evens = list(range(dp - 2, 1, -2))
    return evens[::-1]


def swapped(block):
    return lax.ppermute(block, "tensor", [(0, 1), (1, 0)])


def times_transposed(a, b, **kwargs):
    return lax.dot_general(
        a, b, (((1,), (1,)), ((), ())), preferred_element_type=jnp.float32, **kwargs
    )


def ready_kernel(out_ref):
    out_ref[...] = jnp.zeros_like(out_ref)


def project_packed(start, x_ref, p_ref, out_ref):
    rows = out_ref.shape[0]
    for h in range(2):
        some = x_ref[pl.ds(pl.multiple_of(start + h * rows, rows), rows), :]
        out_ref[:, h * R : (h + 1) * R] = times_transposed(some, p_ref[...])


def sent_kernel(x_ref, p_ref, _, out_ref):
    start = (1 - lax.axis_index("tensor")) * 2 * out_ref.shape[0]
    project_packed(start, x_ref, p_ref, out_ref)


def kept_kernel(x_ref, p_ref, g_ref, q_ref, _, left_ref, right_ref):
    start = lax.axis_index("tensor") * 2 * left_ref.shape[0]
    project_packed(start, g_ref, q_ref, right_ref)
    project_packed(start, x_ref, p_ref, left_ref)


def order_kernel(*_):
    pass


def features_kernel(kept_ref, received_ref, right_ref, out_ref, square):
    packed = kept_ref.shape[0] // LEN
    for k in range(packed):
        rows = slice(k * LEN, (k + 1) * LEN)
        square[k] = lax.dot_general(
            kept_ref[rows, :] + received_ref[rows, :],
            right_ref[rows, :],
            (((0,), (0,)), ((), ())),
            precision=lax.Precision.HIGHEST,
            preferred_element_type=jnp.float32,
        )
        for h in range(2):
            e = h * packed + k
            even = square[k, pl.ds(h * R, R // 2, stride=2), :]
            odd = square[k, pl.ds(h * R + 1, R // 2, stride=2), :]
            lanes = slice(h * R, (h + 1) * R)
            out_ref[e * R // 2 : (e + 1) * R // 2, :] = jnp.concatenate(
                [even[:, lanes], odd[:, lanes]], 1
            )


def add_products(held, f_ref, sums):
    position = lax.axis_index("dp")
    block = sums.shape[1]
    examples = sums.shape[2] // LANES
    tiles = f_ref.shape[0] // examples
    sums[...] = jnp.zeros_like(sums)
    for group in range(0, len(held), 6):
        chosen = held[group : group + 6]
        totals = [[None] * examples for _ in chosen]
        for r in range(tiles):
            for i, (ref, row, offsets) in enumerate(chosen):
                q = ref[row : row + len(offsets) * block, r * LANES : (r + 1) * LANES]
                for e in range(examples):
                    term = q * f_ref[e * tiles + r : e * tiles + r + 1, :]
                    totals[i][e] = term if r == 0 else totals[i][e] + term
        for (ref, row, offsets), total in zip(chosen, totals):
            for j, offset in enumerate(offsets):
                for e in range(examples):
                    sums[position ^ offset, :, e * LANES : (e + 1) * LANES] = total[e][
                        j * block : (j + 1) * block, :
                    ]


def paired(refs, side, dp, block):
    pairs, held = even_offsets(dp), []
    for ref in refs:
        for k in range(0, ref.shape[0] // block, 2):
            count = min(2, ref.shape[0] // block - k)
            here, pairs = pairs[:count], pairs[count:]
            held.append((ref, k * block, [m + side for m in here]))
    return held


def near_kernel(f_ref, own_ref, beside_ref, *refs):
    sums = refs[-1]
    dp, block, _ = sums.shape
    held = [(own_ref, 0, [0]), (beside_ref, 0, [1])]
    add_products(held + paired(refs[:-1], lax.axis_index("tensor"), dp, block), f_ref, sums)


def scores_kernel(f_ref, near_ref, *refs):
    out_ref, sums = refs[-2:]
    dp, block, width = sums.shape
    add_products(paired(refs[:-2], 1 - lax.axis_index("tensor"), dp, block), f_ref, sums)
    every = (sums[...] + near_ref[...]).reshape(dp * block, width)
    row = lax.broadcasted_iota(jnp.int32, (width // LANES, width), 0)
    lane = lax.broadcasted_iota(jnp.int32, (width // LANES, width), 1)
    own_lanes = jnp.where(lane // LANES == row, 1.0, 0.0).astype(jnp.float32)
    out_ref[...] = times_transposed(own_lanes, every, precision=lax.Precision.HIGHEST) / (
        R * math.sqrt(LEN)
    )


VMEM = pl.BlockSpec(memory_space=pltpu.VMEM)
ANY = pl.BlockSpec(memory_space=pl.ANY)


def call(kernel, shapes, operands, flops, scratch=(), in_specs=None, out_specs=None, limit=16, **kwargs):
    outs = [jax.ShapeDtypeStruct(s, jnp.float32) for s in shapes]
    moved = sum(math.prod(o.shape) * o.dtype.itemsize for o in list(operands) + outs)
    return pl.pallas_call(
        kernel,
        out_shape=outs,
        in_specs=in_specs or [VMEM] * len(operands),
        out_specs=out_specs or [VMEM] * len(outs),
        scratch_shapes=list(scratch),
        cost_estimate=pl.CostEstimate(flops=flops, bytes_accessed=moved, transcendentals=0),
        compiler_params=pltpu.CompilerParams(vmem_limit_bytes=limit * MIB),
        **kwargs,
    )(*operands)


def after(operands, arrays, flops):
    n = len(operands)
    return call(
        order_kernel,
        [a.shape for a in arrays],
        operands + arrays,
        flops,
        in_specs=[ANY] * (n + len(arrays)),
        out_specs=[ANY] * len(arrays),
        input_output_aliases={n + k: k for k in range(len(arrays))},
    )


def local(layer_input, out_grad, proj_in, proj_out, query_features):
    dp = lax.axis_size("dp")
    half = layer_input.shape[0] // lax.axis_size("tensor")
    examples = half // LEN
    packed = (half // 2, 2 * R)
    pairs = even_offsets(dp)

    (ready,) = call(ready_kernel, [(8, LANES)], [], 5 * 10**9)

    beside = fetched(query_features, (1, 1))
    first = [fetched(query_features, (m, m + 1)) for m in pairs]

    p_in, p_out = proj_in.T, proj_out.T
    flops = 2 * half * R * layer_input.shape[1]
    (sent,) = call(
        sent_kernel, [packed], [layer_input, p_in, ready], flops, in_specs=[VMEM] * 2 + [ANY]
    )
    received = swapped(sent)
    kept, right = call(
        kept_kernel,
        [packed, packed],
        [layer_input, p_in, out_grad, p_out, sent],
        3 * flops,
        in_specs=[VMEM] * 4 + [ANY],
    )
    early, late = first[:-1], first[-1]
    right, early[0] = after(early[1:], [right, early[0]], 1)
    right, late = after([early[0]], [right, late], 1)
    (right,) = after([beside, received], [right], 10**9)
    first = [jnp.concatenate(early, 0), late]
    (features,) = call(
        features_kernel,
        [(examples * R // 2, LANES)],
        [kept, received, right],
        12 * half * R * R,
        scratch=[pltpu.VMEM((half // 2 // LEN, LANES, LANES), jnp.float32)],
    )

    second = [swapped(b) for b in first]
    block = query_features.shape[0]
    sums = (dp, block, examples * LANES)
    flops = 2 * examples * dp * block * R * R
    (near,) = call(near_kernel, [sums], [features, query_features, beside] + first, flops)
    (scores,) = call(
        scores_kernel,
        [(examples, dp * block)],
        [features, near] + second,
        flops,
        scratch=[pltpu.VMEM(sums, jnp.float32)],
    )
    return scores


def solution(mesh):
    in_specs = (
        P(("groups", "dp"), "tensor"),
        P(("groups", "dp"), None),
        P("tensor", None),
        P(),
        P(("groups", "dp"), None),
    )
    out_specs = P(("groups", "dp", "tensor"), None)
    return jax.shard_map(local, mesh=mesh, in_specs=in_specs, out_specs=out_specs, check_vma=False)
```

```python
import math

import jax
import jax.numpy as jnp
from jax import lax
from jax.experimental import pallas as pl
from jax.experimental.pallas import tpu as pltpu
from jax.sharding import PartitionSpec as P

R = 64
LEN = 128
LANES = 128
MIB = 1024 * 1024


def fetched(block, offsets):
    axes = ("dp", "tensor")
    dp, cores = (lax.axis_size(a) for a in axes)
    route = [((p ^ offsets[c]) * cores + c, p * cores + c) for p in range(dp) for c in range(cores)]
    return lax.ppermute(block, axes, route)


def even_offsets(dp):
    evens = list(range(dp - 2, 1, -2))
    return evens[-1:] + evens[:-1]


def swapped(block):
    return lax.ppermute(block, "tensor", [(0, 1), (1, 0)])


def times_transposed(a, b, **kwargs):
    return lax.dot_general(
        a, b, (((1,), (1,)), ((), ())), preferred_element_type=jnp.float32, **kwargs
    )


def ready_kernel(out_ref):
    out_ref[...] = jnp.zeros_like(out_ref)


def project_packed(start, x_ref, p_ref, out_ref):
    rows = out_ref.shape[0]
    for h in range(2):
        some = x_ref[pl.ds(pl.multiple_of(start + h * rows, rows), rows), :]
        out_ref[:, h * R : (h + 1) * R] = times_transposed(some, p_ref[...])


def sent_kernel(x_ref, p_ref, block_ref, _, out_ref, same_ref):
    start = (1 - lax.axis_index("tensor")) * 2 * out_ref.shape[0]
    project_packed(start, x_ref, p_ref, out_ref)
    same_ref[...] = block_ref[...]


def kept_kernel(x_ref, p_ref, g_ref, q_ref, _, left_ref, right_ref):
    start = lax.axis_index("tensor") * 2 * left_ref.shape[0]
    project_packed(start, g_ref, q_ref, right_ref)
    project_packed(start, x_ref, p_ref, left_ref)


def order_kernel(*_):
    pass


def features_kernel(kept_ref, received_ref, right_ref, out_ref, square):
    packed = kept_ref.shape[0] // LEN
    for k in range(packed):
        rows = slice(k * LEN, (k + 1) * LEN)
        square[k] = lax.dot_general(
            kept_ref[rows, :] + received_ref[rows, :],
            right_ref[rows, :],
            (((0,), (0,)), ((), ())),
            precision=lax.Precision.HIGHEST,
            preferred_element_type=jnp.float32,
        )
        for h in range(2):
            e = h * packed + k
            even = square[k, pl.ds(h * R, R // 2, stride=2), :]
            odd = square[k, pl.ds(h * R + 1, R // 2, stride=2), :]
            lanes = slice(h * R, (h + 1) * R)
            out_ref[e * R // 2 : (e + 1) * R // 2, :] = jnp.concatenate(
                [even[:, lanes], odd[:, lanes]], 1
            )


def add_products(held, f_ref, sums):
    position = lax.axis_index("dp")
    block = sums.shape[1]
    examples = sums.shape[2] // LANES
    tiles = f_ref.shape[0] // examples
    sums[...] = jnp.zeros_like(sums)
    for group in range(0, len(held), 6):
        chosen = held[group : group + 6]
        totals = [[None] * examples for _ in chosen]
        for r in range(tiles):
            for i, (ref, row, offsets) in enumerate(chosen):
                q = ref[row : row + len(offsets) * block, r * LANES : (r + 1) * LANES]
                for e in range(examples):
                    term = q * f_ref[e * tiles + r : e * tiles + r + 1, :]
                    totals[i][e] = term if r == 0 else totals[i][e] + term
        for (ref, row, offsets), total in zip(chosen, totals):
            for j, offset in enumerate(offsets):
                for e in range(examples):
                    sums[position ^ offset, :, e * LANES : (e + 1) * LANES] = total[e][
                        j * block : (j + 1) * block, :
                    ]


def paired(refs, side, dp, block):
    pairs, held = even_offsets(dp), []
    for ref in refs:
        for k in range(0, ref.shape[0] // block, 2):
            count = min(2, ref.shape[0] // block - k)
            here, pairs = pairs[:count], pairs[count:]
            held.append((ref, k * block, [m + side for m in here]))
    return held


def near_kernel(f_ref, own_ref, beside_ref, *refs):
    sums = refs[-1]
    dp, block, _ = sums.shape
    held = [(own_ref, 0, [0]), (beside_ref, 0, [1])]
    add_products(held + paired(refs[:-1], lax.axis_index("tensor"), dp, block), f_ref, sums)


def scores_kernel(f_ref, near_ref, *refs):
    out_ref, sums = refs[-2:]
    dp, block, width = sums.shape
    add_products(paired(refs[:-2], 1 - lax.axis_index("tensor"), dp, block), f_ref, sums)
    every = (sums[...] + near_ref[...]).reshape(dp * block, width)
    row = lax.broadcasted_iota(jnp.int32, (width // LANES, width), 0)
    lane = lax.broadcasted_iota(jnp.int32, (width // LANES, width), 1)
    own_lanes = jnp.where(lane // LANES == row, 1.0, 0.0).astype(jnp.float32)
    out_ref[...] = times_transposed(own_lanes, every, precision=lax.Precision.HIGHEST) / (
        R * math.sqrt(LEN)
    )


VMEM = pl.BlockSpec(memory_space=pltpu.VMEM)
ANY = pl.BlockSpec(memory_space=pl.ANY)


def call(kernel, shapes, operands, flops, scratch=(), in_specs=None, out_specs=None, limit=16, **kwargs):
    outs = [jax.ShapeDtypeStruct(s, jnp.float32) for s in shapes]
    moved = sum(math.prod(o.shape) * o.dtype.itemsize for o in list(operands) + outs)
    return pl.pallas_call(
        kernel,
        out_shape=outs,
        in_specs=in_specs or [VMEM] * len(operands),
        out_specs=out_specs or [VMEM] * len(outs),
        scratch_shapes=list(scratch),
        cost_estimate=pl.CostEstimate(flops=flops, bytes_accessed=moved, transcendentals=0),
        compiler_params=pltpu.CompilerParams(vmem_limit_bytes=limit * MIB),
        **kwargs,
    )(*operands)


def after(operands, arrays, flops):
    n = len(operands)
    return call(
        order_kernel,
        [a.shape for a in arrays],
        operands + arrays,
        flops,
        in_specs=[ANY] * (n + len(arrays)),
        out_specs=[ANY] * len(arrays),
        input_output_aliases={n + k: k for k in range(len(arrays))},
    )


def local(layer_input, out_grad, proj_in, proj_out, query_features):
    dp = lax.axis_size("dp")
    half = layer_input.shape[0] // lax.axis_size("tensor")
    examples = half // LEN
    packed = (half // 2, 2 * R)
    pairs = even_offsets(dp)

    (ready,) = call(ready_kernel, [(8, LANES)], [], 5 * 10**9)

    first = [fetched(query_features, (m, m + 1)) for m in pairs]

    p_in, p_out = proj_in.T, proj_out.T
    flops = 2 * half * R * layer_input.shape[1]
    sent, queries = call(
        sent_kernel,
        [packed, query_features.shape],
        [layer_input, p_in, query_features, ready],
        flops,
        in_specs=[VMEM] * 3 + [ANY],
    )
    beside = fetched(queries, (1, 1))
    received = swapped(sent)
    kept, right = call(
        kept_kernel,
        [packed, packed],
        [layer_input, p_in, out_grad, p_out, sent],
        3 * flops,
        in_specs=[VMEM] * 4 + [ANY],
    )
    early, late = first[:-1], first[-1]
    right, early[0] = after(early[1:], [right, early[0]], 1)
    right, late = after([early[0]], [right, late], 1)
    (right,) = after([beside, received], [right], 10**9)
    first = [jnp.concatenate(early, 0), late]
    (features,) = call(
        features_kernel,
        [(examples * R // 2, LANES)],
        [kept, received, right],
        12 * half * R * R,
        scratch=[pltpu.VMEM((half // 2 // LEN, LANES, LANES), jnp.float32)],
    )

    second = [swapped(b) for b in first]
    block = query_features.shape[0]
    sums = (dp, block, examples * LANES)
    flops = 2 * examples * dp * block * R * R
    (near,) = call(near_kernel, [sums], [features, queries, beside] + first, flops)
    (scores,) = call(
        scores_kernel,
        [(examples, dp * block)],
        [features, near] + second,
        flops,
        scratch=[pltpu.VMEM(sums, jnp.float32)],
    )
    return scores


def solution(mesh):
    in_specs = (
        P(("groups", "dp"), "tensor"),
        P(("groups", "dp"), None),
        P("tensor", None),
        P(),
        P(("groups", "dp"), None),
    )
    out_specs = P(("groups", "dp", "tensor"), None)
    return jax.shard_map(local, mesh=mesh, in_specs=in_specs, out_specs=out_specs, check_vma=False)
```

```python
import math

import jax
import jax.numpy as jnp
from jax import lax
from jax.experimental import pallas as pl
from jax.experimental.pallas import tpu as pltpu
from jax.sharding import PartitionSpec as P

R = 64
LEN = 128
LANES = 128
MIB = 1024 * 1024


def fetched(block, offsets):
    axes = ("dp", "tensor")
    dp, cores = (lax.axis_size(a) for a in axes)
    route = [((p ^ offsets[c]) * cores + c, p * cores + c) for p in range(dp) for c in range(cores)]
    return lax.ppermute(block, axes, route)


def even_offsets(dp):
    evens = list(range(dp - 2, 1, -2))
    return evens[:1] + evens[:0:-1]


def swapped(block):
    return lax.ppermute(block, "tensor", [(0, 1), (1, 0)])


def times_transposed(a, b, **kwargs):
    return lax.dot_general(
        a, b, (((1,), (1,)), ((), ())), preferred_element_type=jnp.float32, **kwargs
    )


def ready_kernel(out_ref):
    out_ref[...] = jnp.zeros_like(out_ref)


def project_packed(start, x_ref, p_ref, out_ref):
    rows = out_ref.shape[0]
    for h in range(2):
        some = x_ref[pl.ds(pl.multiple_of(start + h * rows, rows), rows), :]
        out_ref[:, h * R : (h + 1) * R] = times_transposed(some, p_ref[...])


def sent_kernel(x_ref, p_ref, _, out_ref):
    start = (1 - lax.axis_index("tensor")) * 2 * out_ref.shape[0]
    project_packed(start, x_ref, p_ref, out_ref)


def kept_kernel(x_ref, p_ref, g_ref, q_ref, _, left_ref, right_ref):
    start = lax.axis_index("tensor") * 2 * left_ref.shape[0]
    project_packed(start, g_ref, q_ref, right_ref)
    project_packed(start, x_ref, p_ref, left_ref)


def order_kernel(*_):
    pass


def features_kernel(kept_ref, received_ref, right_ref, out_ref, square):
    packed = kept_ref.shape[0] // LEN
    for k in range(packed):
        rows = slice(k * LEN, (k + 1) * LEN)
        square[k] = lax.dot_general(
            kept_ref[rows, :] + received_ref[rows, :],
            right_ref[rows, :],
            (((0,), (0,)), ((), ())),
            precision=lax.Precision.HIGHEST,
            preferred_element_type=jnp.float32,
        )
        for h in range(2):
            e = h * packed + k
            even = square[k, pl.ds(h * R, R // 2, stride=2), :]
            odd = square[k, pl.ds(h * R + 1, R // 2, stride=2), :]
            lanes = slice(h * R, (h + 1) * R)
            out_ref[e * R // 2 : (e + 1) * R // 2, :] = jnp.concatenate(
                [even[:, lanes], odd[:, lanes]], 1
            )


def add_products(held, f_ref, sums):
    position = lax.axis_index("dp")
    block = sums.shape[1]
    examples = sums.shape[2] // LANES
    tiles = f_ref.shape[0] // examples
    sums[...] = jnp.zeros_like(sums)
    for group in range(0, len(held), 6):
        chosen = held[group : group + 6]
        totals = [[None] * examples for _ in chosen]
        for r in range(tiles):
            for i, (ref, row, offsets) in enumerate(chosen):
                q = ref[row : row + len(offsets) * block, r * LANES : (r + 1) * LANES]
                for e in range(examples):
                    term = q * f_ref[e * tiles + r : e * tiles + r + 1, :]
                    totals[i][e] = term if r == 0 else totals[i][e] + term
        for (ref, row, offsets), total in zip(chosen, totals):
            for j, offset in enumerate(offsets):
                for e in range(examples):
                    sums[position ^ offset, :, e * LANES : (e + 1) * LANES] = total[e][
                        j * block : (j + 1) * block, :
                    ]


def paired(refs, side, dp, block):
    pairs, held = even_offsets(dp), []
    for ref in refs:
        for k in range(0, ref.shape[0] // block, 2):
            count = min(2, ref.shape[0] // block - k)
            here, pairs = pairs[:count], pairs[count:]
            held.append((ref, k * block, [m + side for m in here]))
    return held


def near_kernel(f_ref, own_ref, beside_ref, *refs):
    sums = refs[-1]
    dp, block, _ = sums.shape
    held = [(own_ref, 0, [0]), (beside_ref, 0, [1])]
    add_products(held + paired(refs[:-1], lax.axis_index("tensor"), dp, block), f_ref, sums)


def scores_kernel(f_ref, near_ref, *refs):
    out_ref, sums = refs[-2:]
    dp, block, width = sums.shape
    add_products(paired(refs[:-2], 1 - lax.axis_index("tensor"), dp, block), f_ref, sums)
    every = (sums[...] + near_ref[...]).reshape(dp * block, width)
    row = lax.broadcasted_iota(jnp.int32, (width // LANES, width), 0)
    lane = lax.broadcasted_iota(jnp.int32, (width // LANES, width), 1)
    own_lanes = jnp.where(lane // LANES == row, 1.0, 0.0).astype(jnp.float32)
    out_ref[...] = times_transposed(own_lanes, every, precision=lax.Precision.HIGHEST) / (
        R * math.sqrt(LEN)
    )


VMEM = pl.BlockSpec(memory_space=pltpu.VMEM)
ANY = pl.BlockSpec(memory_space=pl.ANY)


def call(kernel, shapes, operands, flops, scratch=(), in_specs=None, out_specs=None, limit=16, **kwargs):
    outs = [jax.ShapeDtypeStruct(s, jnp.float32) for s in shapes]
    moved = sum(math.prod(o.shape) * o.dtype.itemsize for o in list(operands) + outs)
    return pl.pallas_call(
        kernel,
        out_shape=outs,
        in_specs=in_specs or [VMEM] * len(operands),
        out_specs=out_specs or [VMEM] * len(outs),
        scratch_shapes=list(scratch),
        cost_estimate=pl.CostEstimate(flops=flops, bytes_accessed=moved, transcendentals=0),
        compiler_params=pltpu.CompilerParams(vmem_limit_bytes=limit * MIB),
        **kwargs,
    )(*operands)


def after(operands, arrays, flops):
    n = len(operands)
    return call(
        order_kernel,
        [a.shape for a in arrays],
        operands + arrays,
        flops,
        in_specs=[ANY] * (n + len(arrays)),
        out_specs=[ANY] * len(arrays),
        input_output_aliases={n + k: k for k in range(len(arrays))},
    )


def local(layer_input, out_grad, proj_in, proj_out, query_features):
    dp = lax.axis_size("dp")
    half = layer_input.shape[0] // lax.axis_size("tensor")
    examples = half // LEN
    packed = (half // 2, 2 * R)
    pairs = even_offsets(dp)

    (ready,) = call(ready_kernel, [(8, LANES)], [], 5 * 10**9)

    beside = fetched(query_features, (1, 1))
    first = [fetched(query_features, (m, m + 1)) for m in pairs]

    p_in, p_out = proj_in.T, proj_out.T
    flops = 2 * half * R * layer_input.shape[1]
    (sent,) = call(
        sent_kernel, [packed], [layer_input, p_in, ready], flops, in_specs=[VMEM] * 2 + [ANY]
    )
    received = swapped(sent)
    kept, right = call(
        kept_kernel,
        [packed, packed],
        [layer_input, p_in, out_grad, p_out, sent],
        3 * flops,
        in_specs=[VMEM] * 4 + [ANY],
    )
    early, late = first[0], first[1:]
    right, early = after([], [right, early], 1)
    second = swapped(early)
    right, late[-1] = after([second] + late[:-1], [right, late[-1]], 1)
    (right,) = after([beside, received], [right], 10**9)
    first = [early, jnp.concatenate(late, 0)]
    (features,) = call(
        features_kernel,
        [(examples * R // 2, LANES)],
        [kept, received, right],
        12 * half * R * R,
        scratch=[pltpu.VMEM((half // 2 // LEN, LANES, LANES), jnp.float32)],
    )

    second = [second, swapped(first[1])]
    block = query_features.shape[0]
    sums = (dp, block, examples * LANES)
    flops = 2 * examples * dp * block * R * R
    (near,) = call(near_kernel, [sums], [features, query_features, beside] + first, flops)
    (scores,) = call(
        scores_kernel,
        [(examples, dp * block)],
        [features, near] + second,
        flops,
        scratch=[pltpu.VMEM(sums, jnp.float32)],
    )
    return scores


def solution(mesh):
    in_specs = (
        P(("groups", "dp"), "tensor"),
        P(("groups", "dp"), None),
        P("tensor", None),
        P(),
        P(("groups", "dp"), None),
    )
    out_specs = P(("groups", "dp", "tensor"), None)
    return jax.shard_map(local, mesh=mesh, in_specs=in_specs, out_specs=out_specs, check_vma=False)
```

```python
import math

import jax
import jax.numpy as jnp
from jax import lax
from jax.experimental import pallas as pl
from jax.experimental.pallas import tpu as pltpu
from jax.sharding import PartitionSpec as P

R = 64
LEN = 128
LANES = 128
MIB = 1024 * 1024


def fetched(block, offsets):
    axes = ("dp", "tensor")
    dp, cores = (lax.axis_size(a) for a in axes)
    route = [((p ^ offsets[c]) * cores + c, p * cores + c) for p in range(dp) for c in range(cores)]
    return lax.ppermute(block, axes, route)


def gathered_offsets(dp):
    even = list(range(dp - 2, 1, -2))
    even = even[1:-1] + even[:1] + even[-1:]
    odd = even[-1:] + even[1:-1] + even[:1]
    return [(e, o + 1) for e, o in zip(even, odd)]


def swapped(block):
    return lax.ppermute(block, "tensor", [(0, 1), (1, 0)])


def times_transposed(a, b, **kwargs):
    return lax.dot_general(
        a, b, (((1,), (1,)), ((), ())), preferred_element_type=jnp.float32, **kwargs
    )


def ready_kernel(out_ref):
    out_ref[...] = jnp.zeros_like(out_ref)


def project_packed(start, x_ref, p_ref, out_ref):
    rows = out_ref.shape[0]
    for h in range(2):
        some = x_ref[pl.ds(pl.multiple_of(start + h * rows, rows), rows), :]
        out_ref[:, h * R : (h + 1) * R] = times_transposed(some, p_ref[...])


def sent_kernel(x_ref, p_ref, _, out_ref):
    start = (1 - lax.axis_index("tensor")) * 2 * out_ref.shape[0]
    project_packed(start, x_ref, p_ref, out_ref)


def kept_kernel(x_ref, p_ref, g_ref, q_ref, _, left_ref, right_ref):
    start = lax.axis_index("tensor") * 2 * left_ref.shape[0]
    project_packed(start, g_ref, q_ref, right_ref)
    project_packed(start, x_ref, p_ref, left_ref)


def order_kernel(*_):
    pass


def features_kernel(kept_ref, received_ref, right_ref, out_ref, square):
    packed = kept_ref.shape[0] // LEN
    for k in range(packed):
        rows = slice(k * LEN, (k + 1) * LEN)
        square[k] = lax.dot_general(
            kept_ref[rows, :] + received_ref[rows, :],
            right_ref[rows, :],
            (((0,), (0,)), ((), ())),
            precision=lax.Precision.HIGHEST,
            preferred_element_type=jnp.float32,
        )
        for h in range(2):
            e = h * packed + k
            even = square[k, pl.ds(h * R, R // 2, stride=2), :]
            odd = square[k, pl.ds(h * R + 1, R // 2, stride=2), :]
            lanes = slice(h * R, (h + 1) * R)
            out_ref[e * R // 2 : (e + 1) * R // 2, :] = jnp.concatenate(
                [even[:, lanes], odd[:, lanes]], 1
            )


def add_products(held, f_ref, sums):
    position = lax.axis_index("dp")
    block = sums.shape[1]
    examples = sums.shape[2] // LANES
    tiles = f_ref.shape[0] // examples
    sums[...] = jnp.zeros_like(sums)
    for group in range(0, len(held), 6):
        chosen = held[group : group + 6]
        totals = [[None] * examples for _ in chosen]
        for r in range(tiles):
            for i, (ref, row, offsets) in enumerate(chosen):
                q = ref[row : row + len(offsets) * block, r * LANES : (r + 1) * LANES]
                for e in range(examples):
                    term = q * f_ref[e * tiles + r : e * tiles + r + 1, :]
                    totals[i][e] = term if r == 0 else totals[i][e] + term
        for (ref, row, offsets), total in zip(chosen, totals):
            for j, offset in enumerate(offsets):
                for e in range(examples):
                    sums[position ^ offset, :, e * LANES : (e + 1) * LANES] = total[e][
                        j * block : (j + 1) * block, :
                    ]


def in_order(refs, core, shape):
    dp, block, _ = shape
    offsets = [jnp.where(core == 0, a, b) for a, b in gathered_offsets(dp)]
    held = []
    for ref in refs:
        for row in range(0, ref.shape[0], 2 * block):
            count = min(2, (ref.shape[0] - row) // block)
            held.append((ref, row, offsets[:count]))
            offsets = offsets[count:]
    return held


def near_kernel(f_ref, own_ref, beside_ref, *refs):
    sums = refs[-1]
    held = [(own_ref, 0, [0]), (beside_ref, 0, [1])]
    add_products(held + in_order(refs[:-1], lax.axis_index("tensor"), sums.shape), f_ref, sums)


def scores_kernel(f_ref, near_ref, *refs):
    out_ref, sums = refs[-2:]
    dp, block, width = sums.shape
    add_products(in_order(refs[:-2], 1 - lax.axis_index("tensor"), sums.shape), f_ref, sums)
    every = (sums[...] + near_ref[...]).reshape(dp * block, width)
    row = lax.broadcasted_iota(jnp.int32, (width // LANES, width), 0)
    lane = lax.broadcasted_iota(jnp.int32, (width // LANES, width), 1)
    own_lanes = jnp.where(lane // LANES == row, 1.0, 0.0).astype(jnp.float32)
    out_ref[...] = times_transposed(own_lanes, every, precision=lax.Precision.HIGHEST) / (
        R * math.sqrt(LEN)
    )


VMEM = pl.BlockSpec(memory_space=pltpu.VMEM)
ANY = pl.BlockSpec(memory_space=pl.ANY)


def call(kernel, shapes, operands, flops, scratch=(), in_specs=None, out_specs=None, limit=16, **kwargs):
    outs = [jax.ShapeDtypeStruct(s, jnp.float32) for s in shapes]
    moved = sum(math.prod(o.shape) * o.dtype.itemsize for o in list(operands) + outs)
    return pl.pallas_call(
        kernel,
        out_shape=outs,
        in_specs=in_specs or [VMEM] * len(operands),
        out_specs=out_specs or [VMEM] * len(outs),
        scratch_shapes=list(scratch),
        cost_estimate=pl.CostEstimate(flops=flops, bytes_accessed=moved, transcendentals=0),
        compiler_params=pltpu.CompilerParams(vmem_limit_bytes=limit * MIB),
        **kwargs,
    )(*operands)


def after(operands, arrays, flops):
    n = len(operands)
    return call(
        order_kernel,
        [a.shape for a in arrays],
        operands + arrays,
        flops,
        in_specs=[ANY] * (n + len(arrays)),
        out_specs=[ANY] * len(arrays),
        input_output_aliases={n + k: k for k in range(len(arrays))},
    )


def local(layer_input, out_grad, proj_in, proj_out, query_features):
    dp = lax.axis_size("dp")
    half = layer_input.shape[0] // lax.axis_size("tensor")
    examples = half // LEN
    packed = (half // 2, 2 * R)

    (ready,) = call(ready_kernel, [(8, LANES)], [], 5 * 10**9)

    beside = fetched(query_features, (1, 1))
    first = [fetched(query_features, offsets) for offsets in gathered_offsets(dp)]

    p_in, p_out = proj_in.T, proj_out.T
    flops = 2 * half * R * layer_input.shape[1]
    (sent,) = call(
        sent_kernel, [packed], [layer_input, p_in, ready], flops, in_specs=[VMEM] * 2 + [ANY]
    )
    received = swapped(sent)
    kept, right = call(
        kept_kernel,
        [packed, packed],
        [layer_input, p_in, out_grad, p_out, sent],
        3 * flops,
        in_specs=[VMEM] * 4 + [ANY],
    )
    early, late = first[:-1], first[-1]
    right, early[0] = after(early[1:], [right, early[0]], 1)
    right, late = after([early[0]], [right, late], 1)
    (right,) = after([beside, received], [right], 10**9)
    first = [jnp.concatenate(early, 0), late]
    (features,) = call(
        features_kernel,
        [(examples * R // 2, LANES)],
        [kept, received, right],
        12 * half * R * R,
        scratch=[pltpu.VMEM((half // 2 // LEN, LANES, LANES), jnp.float32)],
    )

    second = [swapped(b) for b in first]
    block = query_features.shape[0]
    sums = (dp, block, examples * LANES)
    flops = 2 * examples * dp * block * R * R
    (near,) = call(near_kernel, [sums], [features, query_features, beside] + first, flops)
    (scores,) = call(
        scores_kernel,
        [(examples, dp * block)],
        [features, near] + second,
        flops,
        scratch=[pltpu.VMEM(sums, jnp.float32)],
    )
    return scores


def solution(mesh):
    in_specs = (
        P(("groups", "dp"), "tensor"),
        P(("groups", "dp"), None),
        P("tensor", None),
        P(),
        P(("groups", "dp"), None),
    )
    out_specs = P(("groups", "dp", "tensor"), None)
    return jax.shard_map(local, mesh=mesh, in_specs=in_specs, out_specs=out_specs, check_vma=False)
```

```python
import math

import jax
import jax.numpy as jnp
from jax import lax
from jax.experimental import pallas as pl
from jax.experimental.pallas import tpu as pltpu
from jax.sharding import PartitionSpec as P

R = 64
LEN = 128
LANES = 128
MIB = 1024 * 1024


def fetched(block, offsets):
    axes = ("dp", "tensor")
    dp, cores = (lax.axis_size(a) for a in axes)
    route = [((p ^ offsets[c]) * cores + c, p * cores + c) for p in range(dp) for c in range(cores)]
    return lax.ppermute(block, axes, route)


def gathered_offsets(dp):
    even = list(range(dp - 2, 1, -2))
    even = even[-1:] + even[:-1]
    odd = even[1:2] + even[:1] + even[2:]
    return [(e, o + 1) for e, o in zip(even, odd)]


def swapped(block):
    return lax.ppermute(block, "tensor", [(0, 1), (1, 0)])


def times_transposed(a, b, **kwargs):
    return lax.dot_general(
        a, b, (((1,), (1,)), ((), ())), preferred_element_type=jnp.float32, **kwargs
    )


def ready_kernel(out_ref):
    out_ref[...] = jnp.zeros_like(out_ref)


def project_packed(start, x_ref, p_ref, out_ref):
    rows = out_ref.shape[0]
    for h in range(2):
        some = x_ref[pl.ds(pl.multiple_of(start + h * rows, rows), rows), :]
        out_ref[:, h * R : (h + 1) * R] = times_transposed(some, p_ref[...])


def sent_kernel(x_ref, p_ref, _, out_ref):
    start = (1 - lax.axis_index("tensor")) * 2 * out_ref.shape[0]
    project_packed(start, x_ref, p_ref, out_ref)


def kept_kernel(x_ref, p_ref, g_ref, q_ref, _, left_ref, right_ref):
    start = lax.axis_index("tensor") * 2 * left_ref.shape[0]
    project_packed(start, g_ref, q_ref, right_ref)
    project_packed(start, x_ref, p_ref, left_ref)


def order_kernel(*_):
    pass


def features_kernel(kept_ref, received_ref, right_ref, out_ref, square):
    packed = kept_ref.shape[0] // LEN
    for k in range(packed):
        rows = slice(k * LEN, (k + 1) * LEN)
        square[k] = lax.dot_general(
            kept_ref[rows, :] + received_ref[rows, :],
            right_ref[rows, :],
            (((0,), (0,)), ((), ())),
            precision=lax.Precision.HIGHEST,
            preferred_element_type=jnp.float32,
        )
        for h in range(2):
            e = h * packed + k
            even = square[k, pl.ds(h * R, R // 2, stride=2), :]
            odd = square[k, pl.ds(h * R + 1, R // 2, stride=2), :]
            lanes = slice(h * R, (h + 1) * R)
            out_ref[e * R // 2 : (e + 1) * R // 2, :] = jnp.concatenate(
                [even[:, lanes], odd[:, lanes]], 1
            )


def add_products(held, f_ref, sums):
    position = lax.axis_index("dp")
    block = sums.shape[1]
    examples = sums.shape[2] // LANES
    tiles = f_ref.shape[0] // examples
    sums[...] = jnp.zeros_like(sums)
    for group in range(0, len(held), 6):
        chosen = held[group : group + 6]
        totals = [[None] * examples for _ in chosen]
        for r in range(tiles):
            for i, (ref, row, offsets) in enumerate(chosen):
                q = ref[row : row + len(offsets) * block, r * LANES : (r + 1) * LANES]
                for e in range(examples):
                    term = q * f_ref[e * tiles + r : e * tiles + r + 1, :]
                    totals[i][e] = term if r == 0 else totals[i][e] + term
        for (ref, row, offsets), total in zip(chosen, totals):
            for j, offset in enumerate(offsets):
                for e in range(examples):
                    sums[position ^ offset, :, e * LANES : (e + 1) * LANES] = total[e][
                        j * block : (j + 1) * block, :
                    ]


def in_order(refs, core, shape):
    dp, block, _ = shape
    offsets = [jnp.where(core == 0, a, b) for a, b in gathered_offsets(dp)]
    held = []
    for ref in refs:
        for row in range(0, ref.shape[0], 2 * block):
            count = min(2, (ref.shape[0] - row) // block)
            held.append((ref, row, offsets[:count]))
            offsets = offsets[count:]
    return held


def near_kernel(f_ref, own_ref, beside_ref, *refs):
    sums = refs[-1]
    held = [(own_ref, 0, [0]), (beside_ref, 0, [1])]
    add_products(held + in_order(refs[:-1], lax.axis_index("tensor"), sums.shape), f_ref, sums)


def scores_kernel(f_ref, near_ref, *refs):
    out_ref, sums = refs[-2:]
    dp, block, width = sums.shape
    add_products(in_order(refs[:-2], 1 - lax.axis_index("tensor"), sums.shape), f_ref, sums)
    every = (sums[...] + near_ref[...]).reshape(dp * block, width)
    row = lax.broadcasted_iota(jnp.int32, (width // LANES, width), 0)
    lane = lax.broadcasted_iota(jnp.int32, (width // LANES, width), 1)
    own_lanes = jnp.where(lane // LANES == row, 1.0, 0.0).astype(jnp.float32)
    out_ref[...] = times_transposed(own_lanes, every, precision=lax.Precision.HIGHEST) / (
        R * math.sqrt(LEN)
    )


VMEM = pl.BlockSpec(memory_space=pltpu.VMEM)
ANY = pl.BlockSpec(memory_space=pl.ANY)


def call(kernel, shapes, operands, flops, scratch=(), in_specs=None, out_specs=None, limit=16, **kwargs):
    outs = [jax.ShapeDtypeStruct(s, jnp.float32) for s in shapes]
    moved = sum(math.prod(o.shape) * o.dtype.itemsize for o in list(operands) + outs)
    return pl.pallas_call(
        kernel,
        out_shape=outs,
        in_specs=in_specs or [VMEM] * len(operands),
        out_specs=out_specs or [VMEM] * len(outs),
        scratch_shapes=list(scratch),
        cost_estimate=pl.CostEstimate(flops=flops, bytes_accessed=moved, transcendentals=0),
        compiler_params=pltpu.CompilerParams(vmem_limit_bytes=limit * MIB),
        **kwargs,
    )(*operands)


def after(operands, arrays, flops):
    n = len(operands)
    return call(
        order_kernel,
        [a.shape for a in arrays],
        operands + arrays,
        flops,
        in_specs=[ANY] * (n + len(arrays)),
        out_specs=[ANY] * len(arrays),
        input_output_aliases={n + k: k for k in range(len(arrays))},
    )


def local(layer_input, out_grad, proj_in, proj_out, query_features):
    dp = lax.axis_size("dp")
    half = layer_input.shape[0] // lax.axis_size("tensor")
    examples = half // LEN
    packed = (half // 2, 2 * R)

    (ready,) = call(ready_kernel, [(8, LANES)], [], 5 * 10**9)

    beside = fetched(query_features, (1, 1))
    first = [fetched(query_features, offsets) for offsets in gathered_offsets(dp)]

    p_in, p_out = proj_in.T, proj_out.T
    flops = 2 * half * R * layer_input.shape[1]
    (sent,) = call(
        sent_kernel, [packed], [layer_input, p_in, ready], flops, in_specs=[VMEM] * 2 + [ANY]
    )
    received = swapped(sent)
    kept, right = call(
        kept_kernel,
        [packed, packed],
        [layer_input, p_in, out_grad, p_out, sent],
        3 * flops,
        in_specs=[VMEM] * 4 + [ANY],
    )
    early, late = first[:-1], first[-1]
    right, early[0] = after(early[1:], [right, early[0]], 1)
    right, late = after([early[0]], [right, late], 1)
    (right,) = after([beside, received], [right], 10**9)
    first = [jnp.concatenate(early, 0), late]
    (features,) = call(
        features_kernel,
        [(examples * R // 2, LANES)],
        [kept, received, right],
        12 * half * R * R,
        scratch=[pltpu.VMEM((half // 2 // LEN, LANES, LANES), jnp.float32)],
    )

    second = [swapped(b) for b in first]
    block = query_features.shape[0]
    sums = (dp, block, examples * LANES)
    flops = 2 * examples * dp * block * R * R
    (near,) = call(near_kernel, [sums], [features, query_features, beside] + first, flops)
    (scores,) = call(
        scores_kernel,
        [(examples, dp * block)],
        [features, near] + second,
        flops,
        scratch=[pltpu.VMEM(sums, jnp.float32)],
    )
    return scores


def solution(mesh):
    in_specs = (
        P(("groups", "dp"), "tensor"),
        P(("groups", "dp"), None),
        P("tensor", None),
        P(),
        P(("groups", "dp"), None),
    )
    out_specs = P(("groups", "dp", "tensor"), None)
    return jax.shard_map(local, mesh=mesh, in_specs=in_specs, out_specs=out_specs, check_vma=False)
```
